32 devices in a mesh: dp: 8 (over z, core), tensor: 4 (over y, x).
Axes of the slice: x: 2, y: 2, z: 4, core: 2. Of those that a mesh axis runs over, the one named last changes fastest.
Arguments:
- tokens: bfloat16 [16, 1024, 2048], P(None, ('tensor', 'dp')), may hold values from -6 to 6
- cotangent: bfloat16 [16, 1024, 2048], P('dp', 'tensor'), may hold values from -6 to 6
- lengths: int32 [16], replicated, may hold values from 256 to 1024, as said below
- dealing: int32 [16], replicated, may hold values from 0 to 15, as said below
- query_weight: float32 [2048, 2048], P('dp', 'tensor'), may hold values from -0.125 to 0.125
- key_weight: float32 [2048, 2048], P('dp', 'tensor'), may hold values from -0.125 to 0.125
- value_weight: float32 [2048, 2048], P('dp', 'tensor'), may hold values from -0.125 to 0.125
- output_weight: float32 [2048, 2048], P('tensor', 'dp'), may hold values from -3 to 3
- up_weight: float32 [2048, 8192], P('dp', 'tensor'), may hold values from -0.125 to 0.125
- down_weight: float32 [8192, 2048], P('tensor', 'dp'), may hold values from -0.0625 to 0.0625
- query_bias: float32 [2048], P(('tensor', 'dp')), may hold values from -3 to 3
- value_bias: float32 [2048], P(('tensor', 'dp')), may hold values from -3 to 3
- output_bias: float32 [2048], P(('tensor', 'dp')), may hold values from -3 to 3
- attention_gain: float32 [2048], P(('tensor', 'dp')), may hold values from 0.25 to 1.75
- attention_shift: float32 [2048], P(('tensor', 'dp')), may hold values from -3 to 3
- up_bias: float32 [8192], P(('tensor', 'dp')), may hold values from -3 to 3
- down_bias: float32 [2048], P(('tensor', 'dp')), may hold values from -3 to 3
- feedforward_gain: float32 [2048], P(('tensor', 'dp')), may hold values from 0.25 to 1.75
- feedforward_shift: float32 [2048], P(('tensor', 'dp')), may hold values from -3 to 3
Outputs:
- result: bfloat16 [16, 1024, 2048], P(None, ('tensor', 'dp'))
- token_gradient: bfloat16 [16, 1024, 2048], P(None, ('tensor', 'dp'))
- query_weight_gradient: float32 [2048, 2048], P('dp', 'tensor')
- key_weight_gradient: float32 [2048, 2048], P('dp', 'tensor')
- value_weight_gradient: float32 [2048, 2048], P('dp', 'tensor')
- output_weight_gradient: float32 [2048, 2048], P('tensor', 'dp')
- up_weight_gradient: float32 [2048, 8192], P('dp', 'tensor')
- down_weight_gradient: float32 [8192, 2048], P('tensor', 'dp')
- query_bias_gradient: float32 [2048], P(('tensor', 'dp'))
- value_bias_gradient: float32 [2048], P(('tensor', 'dp'))
- output_bias_gradient: float32 [2048], P(('tensor', 'dp'))
- attention_gain_gradient: float32 [2048], P(('tensor', 'dp'))
- attention_shift_gradient: float32 [2048], P(('tensor', 'dp'))
- up_bias_gradient: float32 [8192], P(('tensor', 'dp'))
- down_bias_gradient: float32 [2048], P(('tensor', 'dp'))
- feedforward_gain_gradient: float32 [2048], P(('tensor', 'dp'))
- feedforward_shift_gradient: float32 [2048], P(('tensor', 'dp'))
The draws below stay inside these ranges and needn't reach their ends.
Inputs may be any that keep to these rules, and one draw needn't show every extreme that they name: `lengths`: at least 8 sequences are longer than 960 tokens, and at least one has exactly 1024. `dealing`: each sequence stands in exactly one dealt slot.
All inputs are finite; a program needn't handle non-finite values.
Results may differ from the reference program's by a relative error of at most 0.019.
Values may be sent and summed in bfloat16 or wider, within the bound.
No kernel may reach another device: no remote copies, remote signals or barrier semaphores. Data moves between devices by JAX's collectives and lax.ppermute only.
A program may use at most 256 MiB of HBM per device.

```python
import math
import jax
import jax.numpy as jnp
from jax import lax

D = 2048
HEADS = 16
HEAD = 128
FF = 8192
LEN = 1024
SPG = 2
NSEQ = 16


def shared_lengths(key):
    short_key, long_key, mask_key, longest_key = jax.random.split(jax.random.fold_in(key, 101), 4)
    shorter = jax.random.randint(short_key, (NSEQ,), LEN // 4, LEN + 1)
    longer = jax.random.randint(long_key, (NSEQ,), LEN - LEN // 16 + 1, LEN + 1)
    chosen = jax.random.permutation(mask_key, NSEQ) < NSEQ // 2
    mixed_lengths = jnp.where(chosen, longer, shorter)
    longest = jax.random.randint(longest_key, (), 0, NSEQ)
    return mixed_lengths.at[longest].set(LEN).astype(jnp.int32)


def draw_lengths(key, part):
    return shared_lengths(key)


def draw_dealing(key, part):
    lengths = shared_lengths(key)
    groups = NSEQ // SPG
    ordering = jnp.argsort(-lengths, stable=True).astype(jnp.int32)
    ranking = jnp.arange(NSEQ, dtype=jnp.int32)
    rounds = ranking // groups
    position = ranking % groups
    target = jnp.where(rounds % 2 == 0, position, groups - 1 - position)
    destination = target * SPG + rounds
    return jnp.zeros((NSEQ,), jnp.int32).at[destination].set(ordering)


def block_levels(stream_key, shape, pieces, smallest, largest):
    def one(axis_at, blocks):
        steps = jax.random.uniform(jax.random.fold_in(jax.random.fold_in(stream_key, 6), axis_at), (blocks,), jnp.float32, smallest / len(pieces), largest / len(pieces))
        return jnp.repeat(jnp.exp(steps), shape[axis_at] // blocks).reshape((-1,) + (1,) * (len(shape) - axis_at - 1))

    level = one(*pieces[0])
    for cut in pieces[1:]:
        level = level * one(*cut)
    return level


def gaussian(rng, dims, scale, limit, shards=(), kind=jnp.bfloat16):
    values = scale * jax.random.normal(rng, dims, jnp.float32)
    if shards:
        values = values * block_levels(rng, dims, shards, -0.22, 0.18)
    return jnp.clip(values, -limit, limit).astype(kind)


def setup_inputs(seed: int = 0) -> dict:
    seeds = jax.random.split(jax.random.key(seed), 20)
    return {
        "tokens": gaussian(seeds[0], (NSEQ, LEN, D), 1.0, 6.0, ((1, 32),)),
        "cotangent": gaussian(seeds[1], (NSEQ, LEN, D), 1.0, 6.0, ((0, 8), (1, 4))),
        "lengths": draw_lengths(jax.random.fold_in(seeds[19], 71), 0),
        "dealing": draw_dealing(jax.random.fold_in(seeds[19], 71), 0),
        "query_weight": gaussian(seeds[4], (D, D), D ** -0.5, 0.125, ((0, 8), (1, 4)), jnp.float32),
        "key_weight": gaussian(seeds[5], (D, D), D ** -0.5, 0.125, ((0, 8), (1, 4)), jnp.float32),
        "value_weight": gaussian(seeds[6], (D, D), D ** -0.5, 0.125, ((0, 8), (1, 4)), jnp.float32),
        "output_weight": gaussian(seeds[7], (D, D), (max(D // 512, 1)) ** -0.5, 3.0, ((0, 4), (1, 8)), jnp.float32),
        "up_weight": gaussian(seeds[8], (D, FF), D ** -0.5, 0.125, ((0, 8), (1, 4)), jnp.float32),
        "down_weight": gaussian(seeds[9], (FF, D), FF ** -0.5, 0.0625, ((0, 4), (1, 8)), jnp.float32),
        "query_bias": gaussian(seeds[10], (D,), 0.5, 3.0, ((0, 32),), jnp.float32),
        "value_bias": gaussian(seeds[11], (D,), 0.5, 3.0, ((0, 32),), jnp.float32),
        "output_bias": gaussian(seeds[12], (D,), 0.5, 3.0, ((0, 32),), jnp.float32),
        "attention_gain": jnp.clip(1.0 + 0.15 * jax.random.normal(seeds[13], (D,), jnp.float32), 0.25, 1.75),
        "attention_shift": gaussian(seeds[14], (D,), 0.5, 3.0, ((0, 32),), jnp.float32),
        "up_bias": gaussian(seeds[15], (FF,), 0.5, 3.0, ((0, 32),), jnp.float32),
        "down_bias": gaussian(seeds[16], (D,), 0.5, 3.0, ((0, 32),), jnp.float32),
        "feedforward_gain": jnp.clip(1.0 + 0.15 * jax.random.normal(seeds[17], (D,), jnp.float32), 0.25, 1.75),
        "feedforward_shift": gaussian(seeds[18], (D,), 0.5, 3.0, ((0, 32),), jnp.float32),
    }


@jax.custom_vjp
def low(v):
    return lax.optimization_barrier(v.astype(jnp.bfloat16)).astype(jnp.float32)

@jax.custom_vjp
def low_back(v):
    return v

def low_keep(v):
    return (low(v), None)

def low_pass(kept, grad):
    return (grad,)

def back_keep(v):
    return (v, None)

def back_low(kept, grad):
    return (low(grad),)
low.defvjp(low_keep, low_pass)
low_back.defvjp(back_keep, back_low)
norm_epsilon = 1e-05
masked_score = -1e+30

def product(left, right):
    return jnp.dot(left, right, precision=lax.Precision.HIGHEST, preferred_element_type=jnp.float32)

def both_ways(value):
    return low_back(low(value))

def layer_norm(inputs, gain, shift):
    centered = inputs - lax.optimization_barrier(jnp.mean(inputs, axis=-1, keepdims=True))
    variance = lax.optimization_barrier(jnp.mean(centered * centered, axis=-1, keepdims=True))
    return centered * lax.rsqrt(variance + norm_epsilon) * gain + shift

def one_sequence(weights, sequence, length):
    query_weight, key_weight, value_weight, output_weight, up_weight, down_weight, query_bias, value_bias, output_bias, attention_gain, attention_shift, up_bias, down_bias, feedforward_gain, feedforward_shift = weights
    queries = both_ways(product(sequence, query_weight) + query_bias).reshape(LEN, HEADS, HEAD)
    key_rows = both_ways(product(sequence, key_weight)).reshape(LEN, HEADS, HEAD)
    values = both_ways(product(sequence, value_weight) + value_bias).reshape(LEN, HEADS, HEAD)
    scores = low_back(jnp.einsum('qhd,khd->hqk', queries, key_rows, precision=lax.Precision.HIGHEST) / math.sqrt(HEAD))
    key_valid = jnp.arange(LEN) < length
    scores = jnp.where(key_valid[None, None, :], scores, masked_score)
    exponent = jnp.exp(scores - lax.optimization_barrier(jnp.max(scores, axis=-1, keepdims=True)))
    attention = low(exponent / lax.optimization_barrier(jnp.sum(exponent, axis=-1, keepdims=True)))
    mixture = both_ways(jnp.einsum('hqk,khd->qhd', attention, values, precision=lax.Precision.HIGHEST)).reshape(LEN, D)
    attended = low_back(product(mixture, output_weight)) + output_bias
    first_norm = layer_norm(sequence + attended, attention_gain, attention_shift)
    hidden = low_back(product(low(first_norm), up_weight) + up_bias)
    active = low(jax.nn.gelu(hidden, approximate=True))
    feedforward = low_back(product(active, down_weight)) + down_bias
    return layer_norm(first_norm + feedforward, feedforward_gain, feedforward_shift)

def reference(tokens, cotangent, lengths, dealing, query_weight, key_weight, value_weight, output_weight, up_weight, down_weight, query_bias, value_bias, output_bias, attention_gain, attention_shift, up_bias, down_bias, feedforward_gain, feedforward_shift):
    masters = (query_weight, key_weight, value_weight, output_weight, up_weight, down_weight, query_bias, value_bias, output_bias, attention_gain, attention_shift, up_bias, down_bias, feedforward_gain, feedforward_shift)

    def forward(inputs, weights):
        rounded = tuple((low(weight) for weight in weights))
        dealt_tokens = jnp.take(inputs, dealing, axis=0)
        dealt_lengths = jnp.take(lengths, dealing, axis=0)

        def apply_pair(paired):
            return one_sequence(rounded, paired[0], paired[1])
        return lax.map(jax.checkpoint(apply_pair), (dealt_tokens, dealt_lengths))
    outputs, pullback = jax.vjp(forward, tokens.astype(jnp.float32), masters)
    token_grad, weight_grads = pullback(cotangent.astype(jnp.float32))
    query_weight_gradient, key_weight_gradient, value_weight_gradient, output_weight_gradient, up_weight_gradient, down_weight_gradient, query_bias_gradient, value_bias_gradient, output_bias_gradient, attention_gain_gradient, attention_shift_gradient, up_bias_gradient, down_bias_gradient, feedforward_gain_gradient, feedforward_shift_gradient = weight_grads
    inverse = jnp.zeros((NSEQ,), jnp.int32).at[dealing].set(jnp.arange(NSEQ, dtype=jnp.int32))
    result = jnp.take(outputs, inverse, axis=0).astype(jnp.bfloat16)
    return (result, token_grad.astype(jnp.bfloat16), query_weight_gradient, key_weight_gradient, value_weight_gradient, output_weight_gradient, up_weight_gradient, down_weight_gradient, query_bias_gradient, value_bias_gradient, output_bias_gradient, attention_gain_gradient, attention_shift_gradient, up_bias_gradient, down_bias_gradient, feedforward_gain_gradient, feedforward_shift_gradient)
```

```python
import functools
import math

import jax
import jax.numpy as jnp
from jax import lax
from jax.experimental import pallas as pl
from jax.experimental.pallas import tpu as pltpu
from jax.sharding import PartitionSpec as P

HEAD = 128
norm_epsilon = 1e-05
masked_score = -1e30
log2_e = math.log2(math.e)
head_scale = 1.0 / math.sqrt(HEAD)
gelu_root = math.sqrt(2.0 / math.pi)
bf16 = jnp.bfloat16
f32 = jnp.float32


def dot(left, right, contract, out=f32):
    return lax.dot_general(left, right, (contract, ((), ())), preferred_element_type=f32).astype(out)


def forward_kernel(bias_ref, qkv_ref, mixed_ref, log_ref, *, heads, query_block):
    rows = qkv_ref.shape[0]
    width = heads * HEAD
    bias = bias_ref[...]
    for head in range(heads):
        low = head * HEAD
        keys = qkv_ref[:, width + low : width + low + HEAD]
        values = qkv_ref[:, 2 * width + low : 2 * width + low + HEAD]
        for first in range(0, rows, query_block):
            part = slice(first, first + query_block)
            queries = qkv_ref[part, low : low + HEAD]
            scores = dot(keys, queries, ((1,), (1,))) * (head_scale * log2_e) + bias
            peak = jnp.max(scores, axis=0, keepdims=True)
            weight = jnp.exp2(scores - peak)
            total = jnp.sum(weight, axis=0, keepdims=True)
            mixed = dot(values, weight.astype(bf16), ((0,), (0,))) * (1.0 / total)
            mixed_ref[part, low : low + HEAD] = mixed.T.astype(bf16)
            log_ref[0, head : head + 1, part] = peak + jnp.log2(total)


def backward_kernel(bias_ref, qkv_ref, mixed_ref, grad_ref, log_ref, out_ref, sum_ref, *, heads, query_block):
    rows = qkv_ref.shape[0]
    width = heads * HEAD
    bias = bias_ref[...]
    for head in range(heads):
        low = head * HEAD
        keys = qkv_ref[:, width + low : width + low + HEAD]
        values = qkv_ref[:, 2 * width + low : 2 * width + low + HEAD]
        key_total = jnp.zeros((rows, HEAD), f32)
        value_total = jnp.zeros((rows, HEAD), f32)
        query_sum = jnp.zeros((1, HEAD), f32)
        for first in range(0, rows, query_block):
            part = slice(first, first + query_block)
            queries = qkv_ref[part, low : low + HEAD]
            grads = grad_ref[part, low : low + HEAD]
            mixed = mixed_ref[part, low : low + HEAD]
            centre = jnp.sum((grads.astype(f32) * mixed.astype(f32)).T, axis=0, keepdims=True)
            scores = dot(keys, queries, ((1,), (1,))) * (head_scale * log2_e) + bias
            weight = jnp.exp2(scores - log_ref[0, head : head + 1, part])
            weight_grad = dot(values, grads, ((1,), (1,)))
            score_grad = (weight * (weight_grad - centre)).astype(bf16)
            value_total = value_total + dot(weight.astype(bf16), grads, ((1,), (0,)))
            key_total = key_total + dot(score_grad, queries, ((1,), (0,)))
            query_grad = dot(keys, score_grad, ((0,), (0,))) * head_scale
            query_grad = query_grad.T.astype(bf16)
            out_ref[part, low : low + HEAD] = query_grad
            query_sum = query_sum + jnp.sum(query_grad.astype(f32), axis=0, keepdims=True)
        out_ref[:, width + low : width + low + HEAD] = (key_total * head_scale).astype(bf16)
        value_total = value_total.astype(bf16)
        out_ref[:, 2 * width + low : 2 * width + low + HEAD] = value_total
        sum_ref[0, :, low : low + HEAD] = query_sum
        sum_ref[0, :, width + low : width + low + HEAD] = jnp.sum(
            value_total.astype(f32), axis=0, keepdims=True
        )


def attend(qkv, bias, halves):
    rows, columns = qkv.shape
    group = columns // halves
    heads = group // (3 * HEAD)
    width = heads * HEAD
    return pl.pallas_call(
        functools.partial(forward_kernel, heads=heads, query_block=min(256, rows)),
        grid=(halves,),
        in_specs=[
            pl.BlockSpec((rows, 1), lambda i: (0, 0)),
            pl.BlockSpec((rows, group), lambda i: (0, i)),
        ],
        out_specs=[
            pl.BlockSpec((rows, width), lambda i: (0, i)),
            pl.BlockSpec((1, heads, rows), lambda i: (i, 0, 0)),
        ],
        out_shape=[
            jax.ShapeDtypeStruct((rows, halves * width), bf16),
            jax.ShapeDtypeStruct((halves, heads, rows), f32),
        ],
        compiler_params=pltpu.CompilerParams(vmem_limit_bytes=40 * 1024 * 1024),
        cost_estimate=pl.CostEstimate(
            flops=4 * halves * heads * rows * rows * HEAD * 4,
            bytes_accessed=rows * columns * 3,
            transcendentals=halves * heads * rows * rows,
        ),
    )(bias, qkv)


def attend_back(qkv, bias, mixed, grads, logs, halves):
    rows, columns = qkv.shape
    group = columns // halves
    heads = group // (3 * HEAD)
    width = heads * HEAD
    return pl.pallas_call(
        functools.partial(backward_kernel, heads=heads, query_block=min(256, rows)),
        grid=(halves,),
        in_specs=[
            pl.BlockSpec((rows, 1), lambda i: (0, 0)),
            pl.BlockSpec((rows, group), lambda i: (0, i)),
            pl.BlockSpec((rows, width), lambda i: (0, i)),
            pl.BlockSpec((rows, width), lambda i: (0, i)),
            pl.BlockSpec((1, heads, rows), lambda i: (i, 0, 0)),
        ],
        out_specs=[
            pl.BlockSpec((rows, group), lambda i: (0, i)),
            pl.BlockSpec((1, 1, 2 * width), lambda i: (i, 0, 0)),
        ],
        out_shape=[
            jax.ShapeDtypeStruct((rows, columns), bf16),
            jax.ShapeDtypeStruct((halves, 1, 2 * width), f32),
        ],
        compiler_params=pltpu.CompilerParams(vmem_limit_bytes=40 * 1024 * 1024),
        cost_estimate=pl.CostEstimate(
            flops=10 * halves * heads * rows * rows * HEAD * 4,
            bytes_accessed=rows * columns * 6,
            transcendentals=halves * heads * rows * rows,
        ),
    )(bias, qkv, mixed, grads, logs)


class TensorAxis:
    def __init__(self):
        self.size = lax.axis_size("tensor")
        self.me = lax.axis_index("tensor")
        self.square = self.size == 4
        if self.square:
            self.origins = self.me ^ jnp.array([0, 1, 3, 2], jnp.int32)
        else:
            self.origins = jnp.arange(self.size, dtype=jnp.int32)

    def swap(self, array, bit):
        return lax.ppermute(array, "tensor", [(i, i ^ bit) for i in range(self.size)])

    def gather(self, block):
        if not self.square:
            return lax.all_gather(block, "tensor", axis=0, tiled=True)
        half = block.shape[0] // 2
        along_x = self.swap(block, 1)
        along_y = self.swap(block, 2)
        top = self.swap(along_y[:half], 1)
        bottom = self.swap(along_x[half:], 2)
        return jnp.concatenate([block, along_x, top, bottom, along_y], axis=0)

    def scatter(self, terms):
        if not self.square:
            return lax.psum_scatter(terms, "tensor", scatter_dimension=0, tiled=True).astype(f32)
        rows, columns = terms.shape[0] // 4, terms.shape[1] // 2
        left, right = terms[:, :columns], terms[:, columns:]
        from_x = self.swap(left[rows : 3 * rows], 1).astype(f32)
        from_y = self.swap(right[2 * rows :], 2).astype(f32)
        onward_y = (left[3 * rows :].astype(f32) + from_x[rows:]).astype(bf16)
        onward_x = (right[rows : 2 * rows].astype(f32) + from_y[:rows]).astype(bf16)
        left = left[:rows].astype(f32) + from_x[:rows] + self.swap(onward_y, 2).astype(f32)
        right = right[:rows].astype(f32) + from_y[rows:] + self.swap(onward_x, 1).astype(f32)
        return jnp.concatenate([left, right], axis=1)


class GroupAxis:
    def __init__(self):
        self.size = lax.axis_size("dp")
        self.me = lax.axis_index("dp")
        self.line = self.size == 8
        self.core = self.me % 2 if self.line else jnp.int32(0)
        self.z = self.me // 2
        n = self.size
        self.next = [(i, (i + 2) % n) for i in range(n)]
        self.last = [(i, (i - 2) % n) for i in range(n)]

    def send(self, array, pairs):
        return lax.ppermute(array, "dp", pairs)

    def other(self, array):
        return self.send(array, [(i, i ^ 1) for i in range(self.size)])

    def order(self, array, axis):
        half = array.shape[axis] // 2
        low = lax.slice_in_dim(array, 0, half, axis=axis)
        high = lax.slice_in_dim(array, half, 2 * half, axis=axis)
        first = self.core == 0
        return jnp.concatenate(
            [jnp.where(first, low, high), jnp.where(first, high, low)], axis=axis
        )

    def gather(self, mine, theirs):
        if not self.line:
            return lax.all_gather(
                jnp.concatenate([mine, theirs], axis=1), "dp", axis=0, tiled=True
            )
        got = self.other(theirs)
        first = self.core == 0
        pair = jnp.concatenate([jnp.where(first, mine, got), jnp.where(first, got, mine)], axis=0)
        behind = self.send(pair, self.next)
        ahead = self.send(pair, self.last)
        far_up = self.send(behind, [(2, 4), (3, 5), (4, 6), (5, 7)])
        far_down = self.send(ahead, [(2, 0), (3, 1), (4, 2), (5, 3)])
        far = jnp.where(self.z >= 2, far_up, far_down)
        full = jnp.zeros((4,) + pair.shape, pair.dtype)
        for step, piece in enumerate((pair, behind, far, ahead)):
            full = lax.dynamic_update_slice(full, piece[None], ((self.z - step) % 4, 0, 0))
        full = full.reshape(-1, pair.shape[1])
        return jnp.concatenate([full, self.other(full)], axis=1)

    def scatter(self, terms):
        if not self.line:
            return lax.psum_scatter(terms, "dp", scatter_dimension=0, tiled=True).astype(f32)
        half = terms.shape[1] // 2
        rows = terms.shape[0] // 4
        chip = (terms[:, :half].astype(f32) + self.other(terms[:, half:]).astype(f32)).astype(bf16)
        chip = chip.reshape(4, rows, half)

        def toward(step):
            return lax.dynamic_index_in_dim(chip, (self.z + step) % 4, 0, False)

        up = self.send(toward(2), [(0, 2), (1, 3), (2, 4), (3, 5)])
        down = self.send(toward(2), [(6, 4), (7, 5), (4, 2), (5, 3)])
        ahead = (toward(1).astype(f32) + up.astype(f32)).astype(bf16)
        behind = (toward(3).astype(f32) + down.astype(f32)).astype(bf16)
        total = (
            toward(0).astype(f32)
            + self.send(ahead, self.next).astype(f32)
            + self.send(behind, self.last).astype(f32)
        ).reshape(2, rows // 2, half)
        mine = lax.dynamic_index_in_dim(total, self.core, 0, False)
        theirs = self.other(lax.dynamic_index_in_dim(total, 1 - self.core, 0, False))
        first = self.core == 0
        return jnp.concatenate([jnp.where(first, mine, theirs), jnp.where(first, theirs, mine)], axis=1)


def split_columns(core, block):
    half = block.shape[1] // 2
    low, high = block[:, :half], block[:, half:]
    return jnp.where(core == 0, low, high), jnp.where(core == 0, high, low)


def after(array, *earlier):
    return lax.optimization_barrier((array,) + earlier)[0]


def norm(rows, gain, shift):
    centred = rows - jnp.mean(rows, axis=-1, keepdims=True)
    inverse = lax.rsqrt(jnp.mean(centred * centred, axis=-1, keepdims=True) + norm_epsilon)
    unit = centred * inverse
    return unit * gain + shift, unit, inverse


def norm_back(grads, unit, inverse, gain):
    scaled = grads * gain
    return inverse * (
        scaled
        - jnp.mean(scaled, axis=-1, keepdims=True)
        - unit * jnp.mean(scaled * unit, axis=-1, keepdims=True)
    )


def gelu(hidden):
    return 0.5 * hidden * (1.0 + jnp.tanh(gelu_root * (hidden + 0.044715 * hidden * hidden * hidden)))


def gelu_slope(hidden):
    square = hidden * hidden
    bend = jnp.tanh(gelu_root * (hidden + 0.044715 * hidden * square))
    return 0.5 * (1.0 + bend) + 0.5 * hidden * (1.0 - bend * bend) * gelu_root * (
        1.0 + 3 * 0.044715 * square
    )


def local(
    tokens,
    cotangent,
    lengths,
    dealing,
    query_weight,
    key_weight,
    value_weight,
    output_weight,
    up_weight,
    down_weight,
    query_bias,
    value_bias,
    output_bias,
    attention_gain,
    attention_shift,
    up_bias,
    down_bias,
    feedforward_gain,
    feedforward_shift,
):
    tensor, group = TensorAxis(), GroupAxis()
    groups, splits = group.size, tensor.size
    core = group.core
    slots, own_rows, model_width = cotangent.shape
    slot_rows = own_rows * splits
    arrival_rows = tokens.shape[1]
    head_width = query_weight.shape[1]
    hidden_width = up_weight.shape[1]
    half = head_width // 2
    piece = query_bias.shape[0]

    head_piece = jnp.concatenate([query_bias, value_bias, up_bias]).astype(bf16)
    row_piece = jnp.concatenate(
        [output_bias, attention_gain, attention_shift, down_bias, feedforward_gain, feedforward_shift]
    ).astype(bf16)
    vectors = lax.all_gather(
        jnp.concatenate([head_piece, row_piece]), ("tensor", "dp"), axis=0, tiled=False
    ).astype(f32)
    head_vectors = lax.dynamic_slice_in_dim(vectors, tensor.me * groups, groups)
    query_bias_here = group.order(head_vectors[:, :piece].reshape(-1), 0)
    value_bias_here = group.order(head_vectors[:, piece : 2 * piece].reshape(-1), 0)
    hidden_bias = group.order(head_vectors[:, 2 * piece : head_piece.shape[0]].reshape(-1), 0)
    row_vectors = vectors[:, head_piece.shape[0] :].reshape(-1, 6, piece)
    row_vectors = jnp.moveaxis(row_vectors, 1, 0).reshape(6, model_width)
    blank = jnp.zeros((half,), f32)
    qkv_bias = jnp.concatenate(
        [query_bias_here[:half], blank, value_bias_here[:half]]
        + [query_bias_here[half:], blank, value_bias_here[half:]]
    )

    slot_dealing = dealing.reshape(groups, slots)

    def arrive(slot):
        sent = jnp.take(tokens, slot_dealing[:, slot], axis=0)
        return lax.all_to_all(sent, "dp", split_axis=0, concat_axis=0, tiled=True).reshape(
            own_rows, model_width
        )

    arrived = [arrive(slot) for slot in range(slots)]

    parts = [split_columns(core, w.astype(bf16)) for w in (query_weight, key_weight, value_weight)]
    qkv_mine = jnp.concatenate([p[0] for p in parts], axis=1)
    qkv_theirs = jnp.concatenate([p[1] for p in parts], axis=1)
    output_mine, output_theirs = split_columns(core, output_weight.astype(bf16).T)
    up_mine, up_theirs = split_columns(core, up_weight.astype(bf16))
    down_mine, down_theirs = split_columns(core, down_weight.astype(bf16).T)
    qkv_block = group.gather(qkv_mine, qkv_theirs)
    output_block = group.gather(after(output_mine, qkv_block), output_theirs)
    up_block = group.gather(after(up_mine, output_block), up_theirs)
    down_block = group.gather(after(down_mine, up_block), down_theirs)

    positions = (tensor.origins[:, None] * own_rows + jnp.arange(own_rows)[None, :]).reshape(-1)
    slot_lengths = lax.dynamic_slice_in_dim(jnp.take(lengths, dealing, axis=0), group.me * slots, slots)
    over_slots = range(slots)
    biases = [
        jnp.where(positions < slot_lengths[slot], 0.0, masked_score).astype(f32)[:, None]
        for slot in over_slots
    ]

    full_rows = [tensor.gather(rows) for rows in arrived]
    qkv = [(dot(rows, qkv_block, ((1,), (0,))) + qkv_bias).astype(bf16) for rows in full_rows]
    attended = [attend(qkv[s], biases[s], 2) for s in over_slots]
    mixed = [a[0] for a in attended]
    logs = [a[1] for a in attended]
    head_sums = [tensor.scatter(dot(m, output_block, ((1,), (1,)), bf16)) for m in mixed]
    first = [
        norm(arrived[s].astype(f32) + (head_sums[s] + row_vectors[0]), row_vectors[1], row_vectors[2])
        for s in over_slots
    ]
    first_full = [tensor.gather(f[0].astype(bf16)) for f in first]
    hidden = [dot(rows, up_block, ((1,), (0,))) + hidden_bias for rows in first_full]
    active = [gelu(h).astype(bf16) for h in hidden]
    hidden_sums = [tensor.scatter(dot(a, down_block, ((1,), (1,)), bf16)) for a in active]
    second = [
        norm(first[s][0] + (hidden_sums[s] + row_vectors[3]), row_vectors[4], row_vectors[5])
        for s in over_slots
    ]

    def give_back(rows):
        return lax.all_to_all(
            rows.astype(bf16).reshape(groups, arrival_rows, model_width),
            "dp",
            split_axis=0,
            concat_axis=0,
            tiled=True,
        )

    returned_rows = [give_back(s[0]) for s in second]

    cotangents = [cotangent[s].astype(f32) for s in over_slots]
    grad_two = [norm_back(cotangents[s], second[s][1], second[s][2], row_vectors[4]) for s in over_slots]
    gain_two_grad = sum(jnp.sum(cotangents[s] * second[s][1], axis=0) for s in over_slots)
    shift_two_grad = sum(jnp.sum(cotangents[s], axis=0) for s in over_slots)
    down_bias_grad = sum(jnp.sum(grad_two[s], axis=0) for s in over_slots)
    down_full = [tensor.gather(g.astype(bf16)) for g in grad_two]
    hidden_grad = [
        (dot(down_full[s], down_block, ((1,), (0,))) * gelu_slope(hidden[s])).astype(bf16)
        for s in over_slots
    ]
    first_back = [tensor.scatter(dot(h, up_block, ((1,), (1,)), bf16)) for h in hidden_grad]
    first_grad = [grad_two[s] + first_back[s] for s in over_slots]
    grad_one = [norm_back(first_grad[s], first[s][1], first[s][2], row_vectors[1]) for s in over_slots]
    grad_one = [lax.optimization_barrier(g) for g in grad_one]
    gain_one_grad = sum(jnp.sum(first_grad[s] * first[s][1], axis=0) for s in over_slots)
    shift_one_grad = sum(jnp.sum(first_grad[s], axis=0) for s in over_slots)
    output_bias_grad = sum(jnp.sum(grad_one[s], axis=0) for s in over_slots)
    attended_full = [tensor.gather(g.astype(bf16)) for g in grad_one]

    def weight_grad(lefts, rights):
        return sum(dot(a, b, ((0,), (0,))) for a, b in zip(lefts, rights)).astype(bf16)

    down_sum = group.scatter(weight_grad(down_full, active))
    up_sum = group.scatter(weight_grad(first_full, hidden_grad))
    up_bias_grad = sum(jnp.sum(h.astype(f32), axis=0) for h in hidden_grad)

    mixed_grad = [dot(rows, output_block, ((1,), (0,)), bf16) for rows in attended_full]
    output_sum = group.scatter(weight_grad(attended_full, mixed))
    attended_back = [
        attend_back(qkv[s], biases[s], mixed[s], mixed_grad[s], logs[s], 2) for s in over_slots
    ]
    qkv_grad = [a[0] for a in attended_back]
    row_back = [tensor.scatter(dot(g, qkv_block, ((1,), (1,)), bf16)) for g in qkv_grad]
    returned_grads = [give_back(grad_one[s] + row_back[s]) for s in over_slots]
    qkv_sum = group.scatter(weight_grad(full_rows, qkv_grad))
    bias_grads = sum(a[1] for a in attended_back).reshape(2, 2, half)

    places = slot_dealing.T.reshape(-1)
    inverse = jnp.zeros(places.shape, jnp.int32).at[places].set(
        jnp.arange(places.shape[0], dtype=jnp.int32)
    )
    result = jnp.take(jnp.concatenate(returned_rows, axis=0), inverse, axis=0)
    token_gradient = jnp.take(jnp.concatenate(returned_grads, axis=0), inverse, axis=0)

    head_grads = jnp.concatenate(
        [
            group.order(bias_grads[:, 0].reshape(-1), 0).reshape(groups, -1),
            group.order(bias_grads[:, 1].reshape(-1), 0).reshape(groups, -1),
            group.order(up_bias_grad, 0).reshape(groups, -1),
        ],
        axis=1,
    )
    head_grads = lax.dynamic_update_slice(
        jnp.zeros((splits * groups, head_grads.shape[1]), f32), head_grads, (tensor.me * groups, 0)
    )
    row_grads = jnp.stack(
        [
            output_bias_grad,
            gain_one_grad,
            shift_one_grad,
            down_bias_grad,
            gain_two_grad,
            shift_two_grad,
        ]
    ).reshape(6, splits * groups, piece)
    row_grads = jnp.moveaxis(row_grads, 0, 1).reshape(splits * groups, -1)
    vector_sums = lax.psum_scatter(
        jnp.concatenate([head_grads, row_grads], axis=1),
        ("tensor", "dp"),
        scatter_dimension=0,
        tiled=True,
    ).reshape(-1)
    ends = [piece, 2 * piece, head_piece.shape[0]]
    ends += [head_piece.shape[0] + piece * (i + 1) for i in range(6)]
    query_share, value_share, up_share, *row_shares = [
        vector_sums[low:high] for low, high in zip([0] + ends, ends)
    ]

    qkv_sum = qkv_sum.reshape(-1, 2, 3, half)
    return (
        result,
        token_gradient,
        qkv_sum[:, :, 0].reshape(-1, head_width),
        qkv_sum[:, :, 1].reshape(-1, head_width),
        qkv_sum[:, :, 2].reshape(-1, head_width),
        output_sum.T,
        up_sum,
        down_sum.T,
        query_share,
        value_share,
        row_shares[0],
        row_shares[1],
        row_shares[2],
        up_share,
        row_shares[3],
        row_shares[4],
        row_shares[5],
    )


def solution(mesh):
    matrix = P("dp", "tensor")
    flipped = P("tensor", "dp")
    vector = P(("tensor", "dp"))
    arrival = P(None, ("tensor", "dp"), None)
    return jax.shard_map(
        local,
        mesh=mesh,
        in_specs=(arrival, P("dp", "tensor", None), P(), P())
        + (matrix, matrix, matrix, flipped, matrix, flipped)
        + (vector,) * 9,
        out_specs=(arrival, arrival) + (matrix, matrix, matrix, flipped, matrix, flipped) + (vector,) * 9,
        check_vma=False,
    )
```

```python
import functools
import math

import jax
import jax.numpy as jnp
from jax import lax
from jax.experimental import pallas as pl
from jax.experimental.pallas import tpu as pltpu
from jax.sharding import PartitionSpec as P

HEAD = 128
norm_epsilon = 1e-05
masked_score = -1e30
log2_e = math.log2(math.e)
head_scale = 1.0 / math.sqrt(HEAD)
gelu_root = math.sqrt(2.0 / math.pi)
bf16 = jnp.bfloat16
f32 = jnp.float32
MIB = 1024 * 1024
TALL = ((1,), (0,))
FLAT = ((1,), (1,))
DEEP = ((0,), (0,))


def dot(left, right, contract):
    return lax.dot_general(left, right, (contract, ((), ())), preferred_element_type=f32)


def shape(dims, dtype):
    return jax.ShapeDtypeStruct(tuple(dims), dtype)


def whole(array):
    return pl.BlockSpec(array.shape, lambda *i: (0,) * array.ndim)


def launch(body, grid, ins, in_specs, outs, out_specs, later=(), scratch=(), flops=0, nbytes=0, exps=0):
    later = tuple(later)
    count, skip = len(ins), len(later)

    def run(*refs):
        body(refs[:count], refs[count + skip :])

    return pl.pallas_call(
        run,
        grid=grid,
        in_specs=list(in_specs) + [pl.BlockSpec(memory_space=pl.ANY)] * skip,
        out_specs=list(out_specs),
        out_shape=list(outs),
        scratch_shapes=list(scratch),
        compiler_params=pltpu.CompilerParams(vmem_limit_bytes=56 * MIB),
        cost_estimate=pl.CostEstimate(flops=int(flops), bytes_accessed=int(nbytes), transcendentals=int(exps)),
    )(*ins, *later)


def attend(qkv, bias, halves, later=()):
    rows, columns = qkv.shape
    group = columns // halves
    heads = group // (3 * HEAD)
    width = heads * HEAD
    block = min(256, rows)

    def body(ins, outs):
        bias_ref, qkv_ref = ins
        mixed_ref, log_ref = outs
        shift = bias_ref[...]
        for head in range(heads):
            low = head * HEAD
            keys = qkv_ref[:, width + low : width + low + HEAD]
            values = qkv_ref[:, 2 * width + low : 2 * width + low + HEAD]
            for first in range(0, rows, block):
                part = slice(first, first + block)
                queries = qkv_ref[part, low : low + HEAD]
                scores = dot(keys, queries, FLAT) * (head_scale * log2_e) + shift
                peak = jnp.max(scores, axis=0, keepdims=True)
                weight = jnp.exp2(scores - peak)
                total = jnp.sum(weight, axis=0, keepdims=True)
                mixed = dot(values, weight.astype(bf16), DEEP) * (1.0 / total)
                mixed_ref[part, low : low + HEAD] = mixed.T.astype(bf16)
                log_ref[0, head : head + 1, part] = peak + jnp.log2(total)

    return launch(
        body,
        (halves,),
        [bias, qkv],
        [pl.BlockSpec((rows, 1), lambda i: (0, 0)), pl.BlockSpec((rows, group), lambda i: (0, i))],
        [shape((rows, halves * width), bf16), shape((halves, heads, rows), f32)],
        [pl.BlockSpec((rows, width), lambda i: (0, i)), pl.BlockSpec((1, heads, rows), lambda i: (i, 0, 0))],
        later,
        flops=4 * halves * heads * rows * rows * HEAD * 4,
        nbytes=rows * columns * 3,
        exps=halves * heads * rows * rows,
    )


def attend_back(qkv, bias, mixed, grads, logs, halves, later=()):
    rows, columns = qkv.shape
    group = columns // halves
    heads = group // (3 * HEAD)
    width = heads * HEAD
    block = min(256, rows)

    def body(ins, outs):
        bias_ref, qkv_ref, mixed_ref, grad_ref, log_ref = ins
        out_ref, sum_ref = outs
        shift = bias_ref[...]
        for head in range(heads):
            low = head * HEAD
            keys = qkv_ref[:, width + low : width + low + HEAD]
            values = qkv_ref[:, 2 * width + low : 2 * width + low + HEAD]
            key_total = jnp.zeros((rows, HEAD), f32)
            value_total = jnp.zeros((rows, HEAD), f32)
            query_sum = jnp.zeros((1, HEAD), f32)
            for first in range(0, rows, block):
                part = slice(first, first + block)
                queries = qkv_ref[part, low : low + HEAD]
                grad = grad_ref[part, low : low + HEAD]
                mix = mixed_ref[part, low : low + HEAD]
                centre = jnp.sum((grad.astype(f32) * mix.astype(f32)).T, axis=0, keepdims=True)
                scores = dot(keys, queries, FLAT) * (head_scale * log2_e) + shift
                weight = jnp.exp2(scores - log_ref[0, head : head + 1, part])
                weight_grad = dot(values, grad, FLAT)
                score_grad = (weight * (weight_grad - centre)).astype(bf16)
                value_total = value_total + dot(weight.astype(bf16), grad, TALL)
                key_total = key_total + dot(score_grad, queries, TALL)
                query_grad = (dot(keys, score_grad, DEEP) * head_scale).T.astype(bf16)
                out_ref[part, low : low + HEAD] = query_grad
                query_sum = query_sum + jnp.sum(query_grad.astype(f32), axis=0, keepdims=True)
            value_total = value_total.astype(bf16)
            out_ref[:, width + low : width + low + HEAD] = (key_total * head_scale).astype(bf16)
            out_ref[:, 2 * width + low : 2 * width + low + HEAD] = value_total
            sum_ref[0, :, low : low + HEAD] = query_sum
            sum_ref[0, :, width + low : width + low + HEAD] = jnp.sum(
                value_total.astype(f32), axis=0, keepdims=True
            )

    columns_of = lambda n: pl.BlockSpec((rows, n), lambda i: (0, i))
    return launch(
        body,
        (halves,),
        [bias, qkv, mixed, grads, logs],
        [
            pl.BlockSpec((rows, 1), lambda i: (0, 0)),
            columns_of(group),
            columns_of(width),
            columns_of(width),
            pl.BlockSpec((1, heads, rows), lambda i: (i, 0, 0)),
        ],
        [shape((rows, columns), bf16), shape((halves, 1, 2 * width), f32)],
        [columns_of(group), pl.BlockSpec((1, 1, 2 * width), lambda i: (i, 0, 0))],
        later,
        flops=10 * halves * heads * rows * rows * HEAD * 4,
        nbytes=rows * columns * 6,
        exps=halves * heads * rows * rows,
    )


def tile_of(width, most):
    tile = min(width, most)
    while width % tile:
        tile //= 2
    return tile


def rows_matmul(pieces, weights, finish, extras, kinds, later=(), most=512):
    rows = sum(p.shape[0] for p in pieces)
    inner, half = weights[0].shape
    tile = tile_of(half, most)
    steps = half // tile

    def body(ins, refs):
        piece_refs = ins[: len(pieces)]
        low_ref, high_ref = ins[len(pieces) : len(pieces) + 2]
        extra_refs = ins[len(pieces) + 2 :]
        out_refs, gathered = refs[: len(kinds)], refs[len(kinds)]
        step = pl.program_id(0)

        @pl.when(step == 0)
        def _():
            first = 0
            for ref in piece_refs:
                gathered[first : first + ref.shape[0], :] = ref[...]
                first += ref.shape[0]

        def part(weight_ref):
            product = dot(gathered[...], weight_ref[...], TALL)
            for ref, value in zip(out_refs, finish(product, *[r[...] for r in extra_refs])):
                ref[...] = value

        @pl.when(step < steps)
        def _():
            part(low_ref)

        @pl.when(step >= steps)
        def _():
            part(high_ref)

    def along(n):
        return pl.BlockSpec((n, tile), lambda j: (0, j))

    return launch(
        body,
        (2 * steps,),
        [*pieces, *weights, *extras],
        [whole(p) for p in pieces]
        + [
            pl.BlockSpec((inner, tile), lambda j: (0, jnp.minimum(j, steps - 1))),
            pl.BlockSpec((inner, tile), lambda j: (0, jnp.maximum(j - steps, 0))),
        ]
        + [along(e.shape[0]) for e in extras],
        [shape((n, 2 * half), dtype) for n, dtype in kinds],
        [along(n) for n, _ in kinds],
        later,
        scratch=[pltpu.VMEM((rows, inner), bf16)],
        flops=2 * rows * inner * half * 2,
        nbytes=2 * (rows * inner + 2 * inner * half) + sum(8 * n * half for n, _ in kinds),
    )


def terms_matmul(left, weights, count, later=(), most=512):
    rows, inner = left.shape
    outer, half = weights[0].shape
    tile = tile_of(outer // 2, most)
    steps = outer // 2 // tile
    piece = rows // count

    def body(ins, outs):
        left_ref, low_ref, high_ref = ins
        step = pl.program_id(0)
        product = dot(left_ref[:, :half], low_ref[...], FLAT) + dot(left_ref[:, half:], high_ref[...], FLAT)
        product = product.astype(bf16)
        for side in range(2):

            @pl.when((step < steps) if side == 0 else (step >= steps))
            def _():
                for i in range(count):
                    outs[2 * i + side][...] = product[i * piece : (i + 1) * piece]

    places = [
        lambda j: (0, jnp.minimum(j, steps - 1)),
        lambda j: (0, jnp.maximum(j - steps, 0)),
    ]
    outs = launch(
        body,
        (2 * steps,),
        [left, *weights],
        [whole(left)] + [pl.BlockSpec((tile, half), lambda j: (j, 0))] * 2,
        [shape((piece, outer // 2), bf16)] * (2 * count),
        [pl.BlockSpec((piece, tile), places[i % 2]) for i in range(2 * count)],
        later,
        flops=2 * rows * inner * outer,
        nbytes=2 * (rows * inner + outer * inner + rows * outer),
    )
    return [outs[2 * i : 2 * i + 2] for i in range(count)]


def weight_grad(lefts, rights, later=(), most=256):
    flat = [p for pieces in lefts for p in pieces]
    outer = flat[0].shape[1]
    rows, columns = rights[0].shape
    half = columns // 2
    tile = tile_of(outer, most)
    slots = len(rights)

    def body(ins, refs):
        piece_refs, right_refs = ins[: len(flat)], ins[len(flat) :]
        mine_ref, theirs_ref, gathered = refs
        first = 0
        for ref in piece_refs:
            gathered[first : first + ref.shape[0], :] = ref[...]
            first += ref.shape[0]
        total = None
        for slot in range(slots):
            term = dot(gathered[slot * rows : (slot + 1) * rows, :], right_refs[slot][...], DEEP)
            total = term if total is None else total + term
        mine_ref[...] = total[:, :half].astype(bf16)
        theirs_ref[...] = total[:, half:].astype(bf16)

    return launch(
        body,
        (outer // tile,),
        [*flat, *rights],
        [pl.BlockSpec((p.shape[0], tile), lambda j: (0, j)) for p in flat] + [whole(r) for r in rights],
        [shape((outer, half), bf16)] * 2,
        [pl.BlockSpec((tile, half), lambda j: (j, 0))] * 2,
        later,
        scratch=[pltpu.VMEM((slots * rows, tile), bf16)],
        flops=2 * slots * rows * outer * columns,
        nbytes=2 * (slots * rows * (outer + columns) + outer * columns),
    )


def norm_tiles(body, rows, width, left, right, tiled, vectors, outs, halves, sums, later):
    steps = 4
    tile = rows // steps
    n_left, n_right, n_tiled = len(left), len(right), len(tiled)

    def run(ins, refs):
        step = pl.program_id(0)
        left_refs = ins[:n_left]
        right_refs = ins[n_left : n_left + n_right]
        tiled_refs = ins[n_left + n_right : n_left + n_right + n_tiled]
        vector_ref = ins[-1] if vectors is not None else None

        def added(group):
            total = group[0][...].astype(f32)
            for ref in group[1:]:
                total = total + ref[...].astype(f32)
            return total

        both = jnp.concatenate([added(left_refs), added(right_refs)], axis=1)
        values, split, totals = body(both, [r[...] for r in tiled_refs], vector_ref)
        for ref, value in zip(refs, values):
            ref[...] = value.astype(ref.dtype)
        split_refs = refs[len(outs) : len(outs) + 2 * halves]
        for i, value in enumerate(split):
            top, bottom = split_refs[2 * i], split_refs[2 * i + 1]

            @pl.when(step < steps // 2)
            def _():
                top[...] = value.astype(bf16)

            @pl.when(step >= steps // 2)
            def _():
                bottom[...] = value.astype(bf16)

        if sums:
            sum_ref = refs[-1]

            @pl.when(step == 0)
            def _():
                sum_ref[...] = jnp.zeros_like(sum_ref)

            for i, value in enumerate(totals):
                sum_ref[i : i + 1, :] += jnp.sum(value, axis=0, keepdims=True)

    def of(columns):
        return pl.BlockSpec((tile, columns), lambda i: (i, 0))

    top = pl.BlockSpec((tile, width), lambda i: (jnp.minimum(i, steps // 2 - 1), 0))
    bottom = pl.BlockSpec((tile, width), lambda i: (jnp.maximum(i - steps // 2, 0), 0))
    ins = [*left, *right, *tiled] + ([vectors] if vectors is not None else [])
    return launch(
        run,
        (steps,),
        ins,
        [of(a.shape[1]) for a in (*left, *right, *tiled)] + ([whole(vectors)] if vectors is not None else []),
        [shape((rows, c), dtype) for c, dtype in outs]
        + [shape((rows // 2, width), bf16)] * (2 * halves)
        + ([shape((8, width), f32)] if sums else []),
        [of(c) for c, _ in outs]
        + [top, bottom] * halves
        + ([pl.BlockSpec((8, width), lambda i: (0, 0))] if sums else []),
        later,
        flops=rows * width * 20,
        nbytes=rows * width * 16,
    )


def normed(values):
    centred = values - jnp.mean(values, axis=-1, keepdims=True)
    inverse = lax.rsqrt(jnp.mean(centred * centred, axis=-1, keepdims=True) + norm_epsilon)
    return centred * inverse, inverse


def norm_back(grads, unit, inverse, gain):
    scaled = grads * gain
    return inverse * (
        scaled
        - jnp.mean(scaled, axis=-1, keepdims=True)
        - unit * jnp.mean(scaled * unit, axis=-1, keepdims=True)
    )


def first_norm(terms, rows, vectors, later=()):
    def body(both, tiled, v):
        unit, inverse = normed(tiled[0].astype(f32) + (both + v[0:1, :]))
        return [unit, inverse], [unit * v[1:2, :] + v[2:3, :]], []

    n, width = rows.shape
    unit, inverse, top, bottom = norm_tiles(
        body, n, width, *terms, [rows], vectors, [(width, f32), (1, f32)], 1, False, later
    )
    return (top, bottom), unit, inverse


def second_norm(terms, unit, cotangent, vectors, later=()):
    def body(both, tiled, v):
        first, grads = tiled[0] * v[1:2, :] + v[2:3, :], tiled[1].astype(f32)
        unit_two, inverse = normed(first + (both + v[3:4, :]))
        back = norm_back(grads, unit_two, inverse, v[4:5, :])
        return [unit_two * v[4:5, :] + v[5:6, :], back], [back], [back, grads * unit_two, grads]

    n, width = unit.shape
    rows, back, top, bottom, sums = norm_tiles(
        body, n, width, *terms, [unit, cotangent], vectors, [(width, bf16), (width, f32)], 1, True, later
    )
    return rows, back, (top, bottom), sums


def first_norm_back(terms, back_two, unit, inverse, vectors, later=()):
    def body(both, tiled, v):
        grads = tiled[0] + both
        back = norm_back(grads, tiled[1], tiled[2], v[1:2, :])
        return [back], [back], [back, grads * tiled[1], grads]

    n, width = unit.shape
    back, top, bottom, sums = norm_tiles(
        body, n, width, *terms, [back_two, unit, inverse], vectors, [(width, f32)], 1, True, later
    )
    return back, (top, bottom), sums


def input_grad(terms, back, later=()):
    def body(both, tiled, v):
        return [tiled[0] + both], [], []

    n, width = back.shape
    return norm_tiles(body, n, width, *terms, [back], None, [(width, bf16)], 0, False, later)[0]


class TensorAxis:
    def __init__(self):
        self.size = lax.axis_size("tensor")
        self.me = lax.axis_index("tensor")
        self.square = self.size == 4
        if self.square:
            self.origins = self.me ^ jnp.array([0, 1, 3, 2], jnp.int32)
        else:
            self.origins = jnp.arange(self.size, dtype=jnp.int32)

    def swap(self, array, bit):
        return lax.ppermute(array, "tensor", [(i, i ^ bit) for i in range(self.size)])

    def gather(self, halves):
        if not self.square:
            return [lax.all_gather(jnp.concatenate(halves, axis=0), "tensor", axis=0, tiled=True)]
        top, bottom = halves
        y_top, x_bottom = self.swap(top, 2), self.swap(bottom, 1)
        y_bottom, x_top = self.swap(bottom, 2), self.swap(top, 1)
        far_top, far_bottom = self.swap(y_top, 1), self.swap(x_bottom, 2)
        return [top, bottom, x_top, x_bottom, far_top, far_bottom, y_top, y_bottom]

    def scatter(self, terms):
        if not self.square:
            full = jnp.concatenate([jnp.concatenate(t, axis=1) for t in terms], axis=0)
            mine = lax.psum_scatter(full, "tensor", scatter_dimension=0, tiled=True)
            half = mine.shape[1] // 2
            return [mine[:, :half]], [mine[:, half:]]
        (left_0, right_0), (left_1, right_1), (left_3, right_3), (left_2, right_2) = terms
        left_onward, right_onward = self.swap(left_3, 1), self.swap(right_3, 2)
        left_near, right_near = self.swap(left_1, 1), self.swap(right_2, 2)
        left_far = self.swap((left_2.astype(f32) + left_onward.astype(f32)).astype(bf16), 2)
        right_far = self.swap((right_1.astype(f32) + right_onward.astype(f32)).astype(bf16), 1)
        return [left_0, left_near, left_far], [right_0, right_near, right_far]


class GroupAxis:
    def __init__(self):
        self.size = lax.axis_size("dp")
        self.me = lax.axis_index("dp")
        self.line = self.size == 8
        self.core = self.me % 2 if self.line else jnp.int32(0)
        self.z = self.me // 2
        n = self.size
        self.next = [(i, (i + 2) % n) for i in range(n)]
        self.last = [(i, (i - 2) % n) for i in range(n)]

    def send(self, array, pairs):
        return lax.ppermute(array, "dp", pairs)

    def other(self, array):
        return self.send(array, [(i, i ^ 1) for i in range(self.size)])

    def order(self, array, axis):
        half = array.shape[axis] // 2
        low = lax.slice_in_dim(array, 0, half, axis=axis)
        high = lax.slice_in_dim(array, half, 2 * half, axis=axis)
        first = self.core == 0
        return jnp.concatenate([jnp.where(first, low, high), jnp.where(first, high, low)], axis=axis)

    def pair(self, mine, got, later):
        rows, width = mine.shape

        def body(ins, outs):
            place, mine_ref, got_ref = ins
            outs[0][pl.ds(pl.multiple_of(place[0] * rows, rows), rows), :] = mine_ref[...]
            outs[0][pl.ds(pl.multiple_of((1 - place[0]) * rows, rows), rows), :] = got_ref[...]

        return launch(
            body,
            (1,),
            [self.core.reshape(1), mine, got],
            [pl.BlockSpec(memory_space=pltpu.SMEM), whole(mine), whole(got)],
            [shape((2 * rows, width), bf16)],
            [pl.BlockSpec((2 * rows, width), lambda i: (0, 0))],
            later,
            nbytes=8 * rows * width,
        )[0]

    def assemble(self, pair, behind, far_up, far_down, ahead):
        rows, width = pair.shape

        def body(place, *refs):
            out = refs[-1]
            step = pl.program_id(0)

            def put(ref, when):
                @pl.when(when)
                def _():
                    out[0] = ref[...]

            put(refs[0], step == 0)
            put(refs[1], step == 1)
            put(refs[2], (step == 2) & (place[0] >= 2))
            put(refs[3], (step == 2) & (place[0] < 2))
            put(refs[4], step == 3)

        return pl.pallas_call(
            body,
            grid_spec=pltpu.PrefetchScalarGridSpec(
                num_scalar_prefetch=1,
                grid=(4,),
                in_specs=[pl.BlockSpec((rows, width), lambda k, place: (0, 0))] * 5,
                out_specs=pl.BlockSpec((1, rows, width), lambda k, place: ((place[0] - k + 4) % 4, 0, 0)),
            ),
            out_shape=shape((4, rows, width), bf16),
            compiler_params=pltpu.CompilerParams(vmem_limit_bytes=56 * MIB),
            cost_estimate=pl.CostEstimate(flops=0, bytes_accessed=18 * rows * width, transcendentals=0),
        )(self.z.reshape(1), pair, behind, far_up, far_down, ahead)

    def gather(self, mine, theirs, later=()):
        if not self.line:
            full = lax.all_gather(jnp.concatenate([mine, theirs], axis=1), "dp", axis=0, tiled=True)
            half = mine.shape[1]
            return (full[:, :half], full[:, half:]), (), ()
        pair = self.pair(mine, self.other(theirs), later)
        behind = self.send(pair, self.next)
        ahead = self.send(pair, self.last)
        far_up = self.send(behind, [(2, 4), (3, 5), (4, 6), (5, 7)])
        far_down = self.send(ahead, [(2, 0), (3, 1), (4, 2), (5, 3)])
        full = self.assemble(pair, behind, far_up, far_down, ahead).reshape(-1, pair.shape[1])
        return (full, self.other(full)), (pair,), (behind, ahead)

    def scatter(self, mine, theirs):
        if not self.line:
            full = jnp.concatenate([mine, theirs], axis=1)
            return lax.psum_scatter(full, "dp", scatter_dimension=0, tiled=True).astype(f32), (), ()
        got = self.other(theirs)
        rows = mine.shape[0] // 4

        def toward(step):
            first = ((self.z + step) % 4) * rows
            parts = [lax.dynamic_slice_in_dim(a, first, rows).astype(f32) for a in (mine, got)]
            return parts[0] + parts[1]

        far = toward(2).astype(bf16)
        up = self.send(far, [(0, 2), (1, 3), (2, 4), (3, 5)])
        down = self.send(far, [(6, 4), (7, 5), (4, 2), (5, 3)])
        ahead = (toward(1) + up.astype(f32)).astype(bf16)
        behind = (toward(3) + down.astype(f32)).astype(bf16)
        total = (
            toward(0)
            + self.send(ahead, self.next).astype(f32)
            + self.send(behind, self.last).astype(f32)
        ).reshape(2, rows // 2, -1)
        own = lax.dynamic_index_in_dim(total, self.core, 0, False)
        others = self.other(lax.dynamic_index_in_dim(total, 1 - self.core, 0, False))
        first = self.core == 0
        out = jnp.concatenate([jnp.where(first, own, others), jnp.where(first, others, own)], axis=1)
        return out, (far,), (ahead, behind)


def add_up(array, axis):
    size = lax.axis_size(axis)
    bit = 1
    while bit < size:
        array = array + lax.ppermute(array, axis, [(i, i ^ bit) for i in range(size)])
        bit *= 2
    return array


def split_columns(core, block):
    half = block.shape[1] // 2
    low, high = block[:, :half], block[:, half:]
    return jnp.where(core == 0, low, high), jnp.where(core == 0, high, low)


def gelu(hidden):
    return 0.5 * hidden * (1.0 + jnp.tanh(gelu_root * (hidden + 0.044715 * hidden * hidden * hidden)))


def gelu_slope(hidden):
    square = hidden * hidden
    bend = jnp.tanh(gelu_root * (hidden + 0.044715 * hidden * square))
    return 0.5 * (1.0 + bend) + 0.5 * hidden * (1.0 - bend * bend) * gelu_root * (
        1.0 + 3 * 0.044715 * square
    )


def local(
    tokens,
    cotangent,
    lengths,
    dealing,
    query_weight,
    key_weight,
    value_weight,
    output_weight,
    up_weight,
    down_weight,
    query_bias,
    value_bias,
    output_bias,
    attention_gain,
    attention_shift,
    up_bias,
    down_bias,
    feedforward_gain,
    feedforward_shift,
):
    tensor, group = TensorAxis(), GroupAxis()
    groups, splits = group.size, tensor.size
    core = group.core
    slots, own_rows, model_width = cotangent.shape
    over = range(slots)
    slot_rows = own_rows * splits
    arrival_rows = tokens.shape[1]
    head_width = query_weight.shape[1]
    half = head_width // 2
    piece = query_bias.shape[0]
    count = splits

    parts = [split_columns(core, w.astype(bf16)) for w in (query_weight, key_weight, value_weight)]
    qkv_mine = jnp.concatenate([p[0] for p in parts], axis=1)
    qkv_theirs = jnp.concatenate([p[1] for p in parts], axis=1)
    qkv_weight, _, near = group.gather(qkv_mine, qkv_theirs)
    mid_weight, _, mid_near = group.gather(*split_columns(core, output_weight.astype(bf16).T), near)
    up_full, up_sent, up_near = group.gather(*split_columns(core, up_weight.astype(bf16)), mid_near)
    down_full, down_sent, _ = group.gather(*split_columns(core, down_weight.astype(bf16).T), up_near)

    slot_dealing = dealing.reshape(groups, slots)

    def arrive(slot):
        places = slot_dealing[:, slot]
        if slot > 0 and near:
            places = places + (near[0][0, 0].astype(f32) * 0.0).astype(jnp.int32)
        sent = jnp.take(tokens, places, axis=0, mode="clip")
        return lax.all_to_all(sent, "dp", split_axis=0, concat_axis=0, tiled=True).reshape(
            own_rows, model_width
        )

    arrived = [arrive(slot) for slot in over]

    head_piece = jnp.concatenate([query_bias, value_bias, up_bias]).astype(bf16)
    row_piece = jnp.concatenate(
        [output_bias, attention_gain, attention_shift, down_bias, feedforward_gain, feedforward_shift]
    ).astype(bf16)
    own_vectors = jnp.concatenate([head_piece, row_piece]).astype(f32)[None]
    table = lax.dynamic_update_slice(
        jnp.zeros((splits * groups, own_vectors.shape[1]), f32),
        own_vectors,
        (tensor.me * groups + group.me, 0),
    )
    vectors = add_up(add_up(table, "dp"), "tensor")
    head_vectors = lax.dynamic_slice_in_dim(vectors, tensor.me * groups, groups)
    query_bias_here = group.order(head_vectors[:, :piece].reshape(-1), 0)
    value_bias_here = group.order(head_vectors[:, piece : 2 * piece].reshape(-1), 0)
    hidden_bias = group.order(head_vectors[:, 2 * piece : head_piece.shape[0]].reshape(-1), 0)[None]
    row_vectors = vectors[:, head_piece.shape[0] :].reshape(-1, 6, piece)
    row_vectors = jnp.moveaxis(row_vectors, 1, 0).reshape(6, model_width)
    row_vectors = jnp.concatenate([row_vectors, jnp.zeros((2, model_width), f32)], axis=0)
    blank = jnp.zeros((half,), f32)
    qkv_bias = jnp.concatenate(
        [query_bias_here[:half], blank, value_bias_here[:half]]
        + [query_bias_here[half:], blank, value_bias_here[half:]]
    )[None]

    positions = (tensor.origins[:, None] * own_rows + jnp.arange(own_rows)[None, :]).reshape(-1)
    slot_lengths = lax.dynamic_slice_in_dim(jnp.take(lengths, dealing, axis=0), group.me * slots, slots)
    biases = [
        jnp.where(positions < slot_lengths[s], 0.0, masked_score).astype(f32)[:, None] for s in over
    ]

    rows_bf16 = [(slot_rows, bf16)]
    token_pieces = [tensor.gather((a[: own_rows // 2], a[own_rows // 2 :])) for a in arrived]
    qkv, mixed, logs, terms = [], [], [], []
    before = ()
    for s in over:
        qkv += rows_matmul(
            token_pieces[s],
            qkv_weight,
            lambda product, bias: ((product + bias).astype(bf16),),
            [qkv_bias],
            rows_bf16,
            before,
            most=256,
        )
        mix, log = attend(qkv[s], biases[s], 2)
        mixed.append(mix)
        logs.append(log)
        term = terms_matmul(mix, mid_weight, count, up_sent)
        terms.append(term)
        before = (term[0][0],)
    first = [
        first_norm(tensor.scatter(terms[s]), arrived[s], row_vectors, (terms[-1][0][0],) + tuple(down_sent))
        for s in over
    ]
    first_pieces = [tensor.gather(f[0]) for f in first]
    hidden, active, terms = [], [], []
    before = ()
    for s in over:
        wide, narrow = rows_matmul(
            first_pieces[s],
            up_full,
            lambda product, bias: (product + bias, gelu(product + bias).astype(bf16)),
            [hidden_bias],
            [(slot_rows, f32), (slot_rows, bf16)],
            before,
        )
        hidden.append(wide)
        active.append(narrow)
        term = terms_matmul(narrow, down_full, count)
        terms.append(term)
        before = (term[0][0],)
    second = [
        second_norm(tensor.scatter(terms[s]), first[s][1], cotangent[s], row_vectors, (terms[-1][0][0],))
        for s in over
    ]

    def give_back(rows):
        return lax.all_to_all(
            rows.reshape(groups, arrival_rows, model_width), "dp", split_axis=0, concat_axis=0, tiled=True
        )

    returned_rows = [give_back(s[0]) for s in second]

    down_pieces = [tensor.gather(s[2]) for s in second]
    hidden_grad, up_sums, terms = [], [], []
    before = ()

    def through_gelu(product, wide):
        grad = (product * gelu_slope(wide)).astype(bf16)
        return grad, jnp.sum(grad.astype(f32), axis=0, keepdims=True)

    for s in over:
        grad, total = rows_matmul(
            down_pieces[s],
            down_full,
            through_gelu,
            [hidden[s]],
            [(slot_rows, bf16), (1, f32)],
            before,
        )
        hidden_grad.append(grad)
        up_sums.append(total)
        term = terms_matmul(grad, up_full, count)
        terms.append(term)
        before = (term[0][0],)
    down_mine, down_theirs = weight_grad(down_pieces, active, before)
    down_sum, down_far, down_near = group.scatter(down_mine, down_theirs)
    up_mine, up_theirs = weight_grad(first_pieces, hidden_grad, (down_mine,))
    up_sum, up_far, up_near_grads = group.scatter(up_mine, up_theirs)
    first_back = [
        first_norm_back(
            tensor.scatter(terms[s]),
            second[s][1],
            first[s][1],
            first[s][2],
            row_vectors,
            (terms[-1][0][0],) if s == 0 else (up_mine,),
        )
        for s in over
    ]
    grad_pieces = [tensor.gather(f[1]) for f in first_back]

    qkv_grad, bias_sums, terms = [], [], []
    before = (up_mine,) + tuple(down_far)
    pending = [tuple(up_far), tuple(down_near)]
    for s in over:
        (mixed_grad,) = rows_matmul(
            grad_pieces[s], mid_weight, lambda product: (product.astype(bf16),), [], rows_bf16, before
        )
        held = pending[min(s, 1)]
        if s == slots - 1:
            mid_mine, mid_theirs = weight_grad(grad_pieces, mixed, (mixed_grad,))
            held = held + (mid_mine,)
        grad, sums = attend_back(qkv[s], biases[s], mixed[s], mixed_grad, logs[s], 2, held)
        qkv_grad.append(grad)
        bias_sums.append(sums)
        term = terms_matmul(grad, qkv_weight, count, tuple(up_near_grads) if s == slots - 1 else ())
        terms.append(term)
        before = (term[0][0],)
    mid_sum, _, _ = group.scatter(mid_mine, mid_theirs)
    returned_grads = [give_back(input_grad(tensor.scatter(terms[s]), first_back[s][0])) for s in over]
    qkv_sum, _, _ = group.scatter(*weight_grad(token_pieces, qkv_grad, before))

    places = slot_dealing.T.reshape(-1)
    inverse = jnp.zeros(places.shape, jnp.int32).at[places].set(
        jnp.arange(places.shape[0], dtype=jnp.int32)
    )
    result = jnp.take(jnp.concatenate(returned_rows, axis=0), inverse, axis=0, mode="clip")
    token_gradient = jnp.take(jnp.concatenate(returned_grads, axis=0), inverse, axis=0, mode="clip")

    bias_total = sum(bias_sums).reshape(2, 2, half)
    head_grads = jnp.concatenate(
        [
            group.order(bias_total[:, 0].reshape(-1), 0),
            group.order(bias_total[:, 1].reshape(-1), 0),
            group.order(sum(up_sums)[0], 0),
        ]
    )
    row_grads = jnp.concatenate(
        [sum(f[2] for f in first_back)[:3], sum(s[3] for s in second)[:3]], axis=0
    ).reshape(-1)
    row_grads = add_up(row_grads.reshape(-1, 128), "tensor")
    grads = add_up(jnp.concatenate([row_grads, head_grads.reshape(-1, 128)], axis=0), "dp").reshape(-1)
    row_shares = lax.dynamic_slice_in_dim(
        grads[: 6 * model_width].reshape(6, splits * groups, piece), tensor.me * groups + group.me, 1, axis=1
    )[:, 0]

    def share(low, width):
        return lax.dynamic_index_in_dim(grads[low : low + groups * width].reshape(groups, width), group.me, 0, False)

    base = 6 * model_width
    query_share = share(base, piece)
    value_share = share(base + head_width, piece)
    up_share = share(base + 2 * head_width, up_bias.shape[0])

    qkv_sum = qkv_sum.reshape(-1, 2, 3, half)
    return (
        result,
        token_gradient,
        qkv_sum[:, :, 0].reshape(-1, head_width),
        qkv_sum[:, :, 1].reshape(-1, head_width),
        qkv_sum[:, :, 2].reshape(-1, head_width),
        mid_sum.T,
        up_sum,
        down_sum.T,
        query_share,
        value_share,
        row_shares[0],
        row_shares[1],
        row_shares[2],
        up_share,
        row_shares[3],
        row_shares[4],
        row_shares[5],
    )


def solution(mesh):
    matrix = P("dp", "tensor")
    flipped = P("tensor", "dp")
    vector = P(("tensor", "dp"))
    arrival = P(None, ("tensor", "dp"), None)
    return jax.shard_map(
        local,
        mesh=mesh,
        in_specs=(arrival, P("dp", "tensor", None), P(), P())
        + (matrix, matrix, matrix, flipped, matrix, flipped)
        + (vector,) * 9,
        out_specs=(arrival, arrival) + (matrix, matrix, matrix, flipped, matrix, flipped) + (vector,) * 9,
        check_vma=False,
    )
```

```python
import functools
import math

import jax
import jax.numpy as jnp
from jax import lax
from jax.experimental import pallas as pl
from jax.experimental.pallas import tpu as pltpu
from jax.sharding import PartitionSpec as P

HEAD = 128
norm_epsilon = 1e-05
masked_score = -1e30
log2_e = math.log2(math.e)
head_scale = 1.0 / math.sqrt(HEAD)
gelu_root = math.sqrt(2.0 / math.pi)
bf16 = jnp.bfloat16
f32 = jnp.float32
MIB = 1024 * 1024
TALL = ((1,), (0,))
FLAT = ((1,), (1,))
DEEP = ((0,), (0,))


def dot(left, right, contract):
    return lax.dot_general(left, right, (contract, ((), ())), preferred_element_type=f32)


def shape(dims, dtype):
    return jax.ShapeDtypeStruct(tuple(dims), dtype)


def whole(array):
    return pl.BlockSpec(array.shape, lambda *i: (0,) * array.ndim)


def launch(body, grid, ins, in_specs, outs, out_specs, later=(), scratch=(), flops=0, nbytes=0, exps=0):
    later = tuple(later)
    count, skip = len(ins), len(later)

    def run(*refs):
        body(refs[:count], refs[count + skip :])

    return pl.pallas_call(
        run,
        grid=grid,
        in_specs=list(in_specs) + [pl.BlockSpec(memory_space=pl.ANY)] * skip,
        out_specs=list(out_specs),
        out_shape=list(outs),
        scratch_shapes=list(scratch),
        compiler_params=pltpu.CompilerParams(vmem_limit_bytes=60 * MIB),
        cost_estimate=pl.CostEstimate(flops=int(flops), bytes_accessed=int(nbytes), transcendentals=int(exps)),
    )(*ins, *later)


def attend(qkv, bias, halves, later=()):
    rows, columns = qkv.shape
    group = columns // halves
    heads = group // (3 * HEAD)
    width = heads * HEAD
    block = min(256, rows)

    def body(ins, outs):
        bias_ref, qkv_ref = ins
        mixed_ref, log_ref = outs
        shift = bias_ref[...]
        for head in range(heads):
            low = head * HEAD
            keys = qkv_ref[:, width + low : width + low + HEAD]
            values = qkv_ref[:, 2 * width + low : 2 * width + low + HEAD]
            for first in range(0, rows, block):
                part = slice(first, first + block)
                queries = qkv_ref[part, low : low + HEAD]
                scores = dot(keys, queries, FLAT) * (head_scale * log2_e) + shift
                peak = jnp.max(scores, axis=0, keepdims=True)
                weight = jnp.exp2(scores - peak)
                total = jnp.sum(weight, axis=0, keepdims=True)
                mixed = dot(values, weight.astype(bf16), DEEP) * (1.0 / total)
                mixed_ref[part, low : low + HEAD] = mixed.T.astype(bf16)
                log_ref[0, head : head + 1, part] = peak + jnp.log2(total)

    return launch(
        body,
        (halves,),
        [bias, qkv],
        [pl.BlockSpec((rows, 1), lambda i: (0, 0)), pl.BlockSpec((rows, group), lambda i: (0, i))],
        [shape((rows, halves * width), bf16), shape((halves, heads, rows), f32)],
        [pl.BlockSpec((rows, width), lambda i: (0, i)), pl.BlockSpec((1, heads, rows), lambda i: (i, 0, 0))],
        later,
        flops=4 * halves * heads * rows * rows * HEAD * 4,
        nbytes=rows * columns * 3,
        exps=halves * heads * rows * rows,
    )


def attend_back(qkv, bias, mixed, grads, logs, halves, later=()):
    rows, columns = qkv.shape
    group = columns // halves
    heads = group // (3 * HEAD)
    width = heads * HEAD
    block = min(256, rows)

    def body(ins, outs):
        bias_ref, qkv_ref, mixed_ref, grad_ref, log_ref = ins
        out_ref, sum_ref = outs
        shift = bias_ref[...]
        for head in range(heads):
            low = head * HEAD
            keys = qkv_ref[:, width + low : width + low + HEAD]
            values = qkv_ref[:, 2 * width + low : 2 * width + low + HEAD]
            key_total = jnp.zeros((rows, HEAD), f32)
            value_total = jnp.zeros((rows, HEAD), f32)
            query_sum = jnp.zeros((1, HEAD), f32)
            for first in range(0, rows, block):
                part = slice(first, first + block)
                queries = qkv_ref[part, low : low + HEAD]
                grad = grad_ref[part, low : low + HEAD]
                mix = mixed_ref[part, low : low + HEAD]
                centre = jnp.sum((grad.astype(f32) * mix.astype(f32)).T, axis=0, keepdims=True)
                scores = dot(keys, queries, FLAT) * (head_scale * log2_e) + shift
                weight = jnp.exp2(scores - log_ref[0, head : head + 1, part])
                weight_grad = dot(values, grad, FLAT)
                score_grad = (weight * (weight_grad - centre)).astype(bf16)
                value_total = value_total + dot(weight.astype(bf16), grad, TALL)
                key_total = key_total + dot(score_grad, queries, TALL)
                query_grad = (dot(keys, score_grad, DEEP) * head_scale).T.astype(bf16)
                out_ref[part, low : low + HEAD] = query_grad
                query_sum = query_sum + jnp.sum(query_grad.astype(f32), axis=0, keepdims=True)
            value_total = value_total.astype(bf16)
            out_ref[:, width + low : width + low + HEAD] = (key_total * head_scale).astype(bf16)
            out_ref[:, 2 * width + low : 2 * width + low + HEAD] = value_total
            sum_ref[0, :, low : low + HEAD] = query_sum
            sum_ref[0, :, width + low : width + low + HEAD] = jnp.sum(
                value_total.astype(f32), axis=0, keepdims=True
            )

    columns_of = lambda n: pl.BlockSpec((rows, n), lambda i: (0, i))
    return launch(
        body,
        (halves,),
        [bias, qkv, mixed, grads, logs],
        [
            pl.BlockSpec((rows, 1), lambda i: (0, 0)),
            columns_of(group),
            columns_of(width),
            columns_of(width),
            pl.BlockSpec((1, heads, rows), lambda i: (i, 0, 0)),
        ],
        [shape((rows, columns), bf16), shape((halves, 1, 2 * width), f32)],
        [columns_of(group), pl.BlockSpec((1, 1, 2 * width), lambda i: (i, 0, 0))],
        later,
        flops=10 * halves * heads * rows * rows * HEAD * 4,
        nbytes=rows * columns * 6,
        exps=halves * heads * rows * rows,
    )


def tile_of(width, most):
    tile = min(width, most)
    while width % tile:
        tile //= 2
    return tile


def rows_matmul(pieces, weight, width, finish, extras, kinds, later=(), most=512):
    rows = sum(p.shape[0] for p in pieces)
    inner = weight.shape[0]
    tile = tile_of(width, most)

    def body(ins, refs):
        piece_refs, weight_ref = ins[: len(pieces)], ins[len(pieces)]
        extra_refs = ins[len(pieces) + 1 :]
        out_refs, gathered = refs[: len(kinds)], refs[len(kinds)]

        @pl.when(pl.program_id(0) == 0)
        def _():
            first = 0
            for ref in piece_refs:
                gathered[first : first + ref.shape[0], :] = ref[...]
                first += ref.shape[0]

        product = dot(gathered[...], weight_ref[...], TALL)
        for ref, value in zip(out_refs, finish(product, *[r[...] for r in extra_refs])):
            ref[...] = value

    def along(n):
        return pl.BlockSpec((n, tile), lambda j: (0, j))

    return launch(
        body,
        (width // tile,),
        [*pieces, weight, *extras],
        [whole(p) for p in pieces] + [along(inner)] + [along(e.shape[0]) for e in extras],
        [shape((n, width), dtype) for n, dtype in kinds],
        [along(n) for n, _ in kinds],
        later,
        scratch=[pltpu.VMEM((rows, inner), bf16)],
        flops=2 * rows * inner * width,
        nbytes=2 * (rows * inner + inner * width) + sum(4 * n * width for n, _ in kinds),
    )


def terms_matmul(left, weight, spans, later=(), most=512):
    rows, inner = left.shape
    outer = weight.shape[0]
    tile = tile_of(outer // 2, most)
    steps = outer // 2 // tile

    def body(ins, outs):
        left_ref, weight_ref = ins
        step = pl.program_id(0)
        product = dot(left_ref[...], weight_ref[...], FLAT).astype(bf16)
        groups = outs[: len(spans[0])], outs[len(spans[0]) :]
        for side in range(2):

            @pl.when((step < steps) if side == 0 else (step >= steps))
            def _():
                for ref, (low, high) in zip(groups[side], spans[side]):
                    ref[...] = product[low:high]

    places = [
        lambda j: (0, jnp.minimum(j, steps - 1)),
        lambda j: (0, jnp.maximum(j - steps, 0)),
    ]
    sizes = [(side, high - low) for side in range(2) for low, high in spans[side]]
    outs = launch(
        body,
        (2 * steps,),
        [left, weight],
        [whole(left), pl.BlockSpec((tile, inner), lambda j: (j, 0))],
        [shape((n, outer // 2), bf16) for _, n in sizes],
        [pl.BlockSpec((n, tile), places[side]) for side, n in sizes],
        later,
        flops=2 * rows * inner * outer,
        nbytes=2 * (rows * inner + outer * inner + rows * outer),
    )
    return outs[: len(spans[0])], outs[len(spans[0]) :]


def weight_grad(lefts, rights, later=(), core=None, most=256):
    flat = [p for pieces in lefts for p in pieces]
    outer = flat[0].shape[1]
    rows, columns = rights[0].shape
    tile = tile_of(outer, most)
    slots = len(rights)
    scalars = [] if core is None else [core.reshape(1)]

    def body(ins, refs):
        ins = ins[len(scalars) :] if core is None else ins[1:]
        piece_refs, right_refs = ins[: len(flat)], ins[len(flat) :]
        gathered = refs[-1]
        first = 0
        for ref in piece_refs:
            gathered[first : first + ref.shape[0], :] = ref[...]
            first += ref.shape[0]
        total = None
        for slot in range(slots):
            term = dot(gathered[slot * rows : (slot + 1) * rows, :], right_refs[slot][...], DEEP)
            total = term if total is None else total + term
        refs[0][...] = total.astype(bf16)

    def body_apart(ins, refs):
        parity = lax.rem(pl.program_id(0), 2)
        total_ref = refs[2]
        body(ins, (total_ref, refs[3]))

        @pl.when(parity == ins[0][0])
        def _():
            refs[0][...] = total_ref[...]

        @pl.when(parity != ins[0][0])
        def _():
            refs[1][...] = total_ref[...]

    outs = [shape((outer, columns), bf16)] if core is None else [shape((outer // 2, columns), bf16)] * 2
    where = (lambda j: (j, 0)) if core is None else (lambda j: (j // 2, 0))
    result = launch(
        body if core is None else body_apart,
        (outer // tile,),
        [*scalars, *flat, *rights],
        [pl.BlockSpec(memory_space=pltpu.SMEM)] * len(scalars)
        + [pl.BlockSpec((p.shape[0], tile), lambda j: (0, j)) for p in flat]
        + [whole(r) for r in rights],
        outs,
        [pl.BlockSpec((tile, columns), where)] * len(outs),
        later,
        scratch=([] if core is None else [pltpu.VMEM((tile, columns), bf16)])
        + [pltpu.VMEM((slots * rows, tile), bf16)],
        flops=2 * slots * rows * outer * columns,
        nbytes=2 * (slots * rows * (outer + columns) + outer * columns),
    )
    return result[0] if core is None else result


def norm_tiles(body, rows, width, left, right, tiled, vectors, outs, sums, later):
    steps = 4
    tile = rows // steps
    n_left, n_right, n_tiled = len(left), len(right), len(tiled)

    def run(ins, refs):
        step = pl.program_id(0)
        left_refs = ins[:n_left]
        right_refs = ins[n_left : n_left + n_right]
        tiled_refs = ins[n_left + n_right : n_left + n_right + n_tiled]
        vector_ref = ins[-1] if vectors is not None else None

        def added(group):
            total = group[0][...].astype(f32)
            for ref in group[1:]:
                total = total + ref[...].astype(f32)
            return total

        both = jnp.concatenate([added(left_refs), added(right_refs)], axis=1)
        values, totals = body(both, [r[...] for r in tiled_refs], vector_ref)
        for ref, value in zip(refs, values):
            ref[...] = value.astype(ref.dtype)
        if sums:
            sum_ref = refs[-1]

            @pl.when(step == 0)
            def _():
                sum_ref[...] = jnp.zeros_like(sum_ref)

            for i, value in enumerate(totals):
                sum_ref[i : i + 1, :] += jnp.sum(value, axis=0, keepdims=True)

    def of(columns):
        return pl.BlockSpec((tile, columns), lambda i: (i, 0))

    ins = [*left, *right, *tiled] + ([vectors] if vectors is not None else [])
    return launch(
        run,
        (steps,),
        ins,
        [of(a.shape[1]) for a in (*left, *right, *tiled)] + ([whole(vectors)] if vectors is not None else []),
        [shape((rows, c), dtype) for c, dtype in outs]
        + ([shape((8, width), f32)] if sums else []),
        [of(c) for c, _ in outs]
        + ([pl.BlockSpec((8, width), lambda i: (0, 0))] if sums else []),
        later,
        flops=rows * width * 20,
        nbytes=rows * width * 16,
    )


def normed(values):
    centred = values - jnp.mean(values, axis=-1, keepdims=True)
    inverse = lax.rsqrt(jnp.mean(centred * centred, axis=-1, keepdims=True) + norm_epsilon)
    return centred * inverse, inverse


def norm_back(grads, unit, inverse, gain):
    scaled = grads * gain
    return inverse * (
        scaled
        - jnp.mean(scaled, axis=-1, keepdims=True)
        - unit * jnp.mean(scaled * unit, axis=-1, keepdims=True)
    )


def first_norm(terms, rows, vectors, later=()):
    def body(both, tiled, v):
        unit, inverse = normed(tiled[0].astype(f32) + (both + v[0:1, :]))
        return [unit * v[1:2, :] + v[2:3, :], unit, inverse], []

    n, width = rows.shape
    kinds = [(width, bf16), (width, f32), (1, f32)]
    return norm_tiles(body, n, width, *terms, [rows], vectors, kinds, False, later)


def second_norm(terms, unit, cotangent, vectors, later=()):
    def body(both, tiled, v):
        first, grads = tiled[0] * v[1:2, :] + v[2:3, :], tiled[1].astype(f32)
        unit_two, inverse = normed(first + (both + v[3:4, :]))
        back = norm_back(grads, unit_two, inverse, v[4:5, :])
        return [unit_two * v[4:5, :] + v[5:6, :], back, back], [back, grads * unit_two, grads]

    n, width = unit.shape
    kinds = [(width, bf16), (width, f32), (width, bf16)]
    return norm_tiles(body, n, width, *terms, [unit, cotangent], vectors, kinds, True, later)


def first_norm_back(terms, back_two, unit, inverse, vectors, later=()):
    def body(both, tiled, v):
        grads = tiled[0] + both
        back = norm_back(grads, tiled[1], tiled[2], v[1:2, :])
        return [back, back], [back, grads * tiled[1], grads]

    n, width = unit.shape
    kinds = [(width, f32), (width, bf16)]
    return norm_tiles(body, n, width, *terms, [back_two, unit, inverse], vectors, kinds, True, later)


def input_grad(terms, back, later=()):
    def body(both, tiled, v):
        return [tiled[0] + both], []

    n, width = back.shape
    return norm_tiles(body, n, width, *terms, [back], None, [(width, bf16)], False, later)[0]


class TensorAxis:
    def __init__(self):
        self.size = lax.axis_size("tensor")
        self.me = lax.axis_index("tensor")
        self.square = self.size == 4
        if self.square:
            self.origins = self.me ^ jnp.array([0, 1, 3, 2], jnp.int32)
        else:
            self.origins = jnp.arange(self.size, dtype=jnp.int32)

    def swap(self, array, bit):
        return lax.ppermute(array, "tensor", [(i, i ^ bit) for i in range(self.size)])

    def gather(self, block):
        if not self.square:
            return [lax.all_gather(block, "tensor", axis=0, tiled=True)]
        half = block.shape[0] // 2
        along_x, along_y = self.swap(block, 1), self.swap(block, 2)
        far_top, far_bottom = self.swap(along_y[:half], 1), self.swap(along_x[half:], 2)
        return [block, along_x, far_top, far_bottom, along_y]

    def spans(self, rows):
        if not self.square:
            return [(0, rows)], [(0, rows)]
        r = rows // 4
        return [(r, 3 * r), (3 * r, 4 * r), (0, r)], [(2 * r, 4 * r), (r, 2 * r), (0, r)]

    def line_up(self, block):
        if not self.square:
            return lax.all_gather(block, "tensor", axis=1, tiled=True)
        width = block.shape[1]
        full = jnp.zeros((block.shape[0], 4 * width), block.dtype)
        for bits in range(4):
            piece = self.swap(block, bits) if bits else block
            full = lax.dynamic_update_slice(full, piece, (0, (self.me ^ bits) * width))
        return full

    def scatter(self, terms):
        left, right = terms
        if not self.square:
            full = jnp.concatenate([left[0], right[0]], axis=1)
            mine = lax.psum_scatter(full, "tensor", scatter_dimension=0, tiled=True)
            half = mine.shape[1] // 2
            return ([mine[:, :half]], [mine[:, half:]]), ()
        rows = left[1].shape[0]
        from_x, from_y = self.swap(left[0], 1), self.swap(right[0], 2)
        left_far = self.swap((left[1].astype(f32) + from_x[rows:].astype(f32)).astype(bf16), 2)
        right_far = self.swap((right[1].astype(f32) + from_y[:rows].astype(f32)).astype(bf16), 1)
        return ([left[2], from_x, left_far], [right[2], from_y[rows:], right_far]), (from_x, from_y)


class GroupAxis:
    def __init__(self):
        self.size = lax.axis_size("dp")
        self.me = lax.axis_index("dp")
        self.line = self.size == 8
        self.z = self.me // 2
        n = self.size
        self.next = [(i, (i + 2) % n) for i in range(n)]
        self.last = [(i, (i - 2) % n) for i in range(n)]

    def send(self, array, pairs):
        return lax.ppermute(array, "dp", pairs)

    def gather(self, shard):
        return lax.all_gather(shard, "dp", axis=0, tiled=True)

    def scatter(self, terms):
        return lax.psum_scatter(terms, "dp", scatter_dimension=0, tiled=True).astype(f32)

    def weight_scatter(self, lefts, rights, later):
        if not self.line:
            terms = weight_grad(lefts, rights, later)
            return self.scatter(terms), terms, (), (), ()
        mine, theirs = weight_grad(lefts, rights, later, self.me % 2, lefts[0][0].shape[1] // self.size)
        got = self.send(theirs, [(i, i ^ 1) for i in range(self.size)])
        rows = mine.shape[0] // 4

        def toward(step):
            first = ((self.z + step) % 4) * rows
            parts = [lax.dynamic_slice_in_dim(a, first, rows).astype(f32) for a in (mine, got)]
            return parts[0] + parts[1]

        far = toward(2).astype(bf16)
        up = self.send(far, [(0, 2), (1, 3), (2, 4), (3, 5)])
        down = self.send(far, [(6, 4), (7, 5), (4, 2), (5, 3)])
        ahead = (toward(1) + up.astype(f32)).astype(bf16)
        behind = (toward(3) + down.astype(f32)).astype(bf16)
        ahead, behind = self.send(ahead, self.next), self.send(behind, self.last)
        total = toward(0) + ahead.astype(f32) + behind.astype(f32)
        return total, mine, (got,), (up, down), (ahead, behind)


def add_up(array, axis):
    size = lax.axis_size(axis)
    bit = 1
    while bit < size:
        array = array + lax.ppermute(array, axis, [(i, i ^ bit) for i in range(size)])
        bit *= 2
    return array


def gelu(hidden):
    return 0.5 * hidden * (1.0 + jnp.tanh(gelu_root * (hidden + 0.044715 * hidden * hidden * hidden)))


def gelu_slope(hidden):
    square = hidden * hidden
    bend = jnp.tanh(gelu_root * (hidden + 0.044715 * hidden * square))
    return 0.5 * (1.0 + bend) + 0.5 * hidden * (1.0 - bend * bend) * gelu_root * (
        1.0 + 3 * 0.044715 * square
    )


def local(
    tokens,
    cotangent,
    lengths,
    dealing,
    query_weight,
    key_weight,
    value_weight,
    output_weight,
    up_weight,
    down_weight,
    query_bias,
    value_bias,
    output_bias,
    attention_gain,
    attention_shift,
    up_bias,
    down_bias,
    feedforward_gain,
    feedforward_shift,
):
    tensor, group = TensorAxis(), GroupAxis()
    groups, splits = group.size, tensor.size
    slots, own_rows, model_width = cotangent.shape
    over = range(slots)
    slot_rows = own_rows * splits
    arrival_rows = tokens.shape[1]
    head_width = query_weight.shape[1]
    half = head_width // 2
    piece = query_bias.shape[0]
    hidden_width = up_weight.shape[1]
    spans = tensor.spans(slot_rows)

    slot_dealing = dealing.reshape(groups, slots)
    sent = jnp.take(tokens, dealing, axis=0, mode="clip").reshape(groups, slots, arrival_rows, model_width)
    came = lax.all_to_all(sent, "dp", split_axis=0, concat_axis=0, tiled=True)
    arrived = [came[:, s].reshape(own_rows, model_width) for s in over]

    head_piece = jnp.concatenate([query_bias, value_bias, up_bias]).astype(bf16)
    row_piece = jnp.concatenate(
        [output_bias, attention_gain, attention_shift, down_bias, feedforward_gain, feedforward_shift]
    ).astype(bf16)
    vector = jnp.concatenate([head_piece, row_piece])
    shard_rows, spare = query_weight.shape[0], 128
    padded = jnp.zeros((shard_rows * spare,), bf16).at[: vector.shape[0]].set(vector)
    three = [w.astype(bf16) for w in (query_weight, key_weight, value_weight)]
    qkv_weight = group.gather(
        jnp.concatenate(
            [w[:, :half] for w in three] + [w[:, half:] for w in three] + [padded.reshape(shard_rows, spare)],
            axis=1,
        )
    )
    mid_weight = group.gather(output_weight.astype(bf16).T)
    up_full = group.gather(up_weight.astype(bf16))
    down_full = group.gather(down_weight.astype(bf16).T)
    used = -(-vector.shape[0] // spare)
    table = qkv_weight[:, 3 * head_width :].reshape(groups, shard_rows, spare)[:, :used]
    table = table.reshape(groups, -1)[:, : vector.shape[0]]
    head_vectors = table.astype(f32)
    row_table = table[:, head_piece.shape[0] :].reshape(groups, 6, piece)
    row_table = jnp.moveaxis(row_table, 1, 0).reshape(6, groups * piece)
    row_vectors = tensor.line_up(row_table).astype(f32)
    query_bias_here = head_vectors[:, :piece].reshape(-1)
    value_bias_here = head_vectors[:, piece : 2 * piece].reshape(-1)
    hidden_bias = head_vectors[:, 2 * piece : head_piece.shape[0]].reshape(1, -1)
    row_vectors = jnp.concatenate([row_vectors, jnp.zeros((2, model_width), f32)], axis=0)
    blank = jnp.zeros((half,), f32)
    qkv_bias = jnp.concatenate(
        [query_bias_here[:half], blank, value_bias_here[:half]]
        + [query_bias_here[half:], blank, value_bias_here[half:]]
    )[None]

    positions = (tensor.origins[:, None] * own_rows + jnp.arange(own_rows)[None, :]).reshape(-1)
    slot_lengths = lax.dynamic_slice_in_dim(jnp.take(lengths, dealing, axis=0), group.me * slots, slots)
    biases = [
        jnp.where(positions < slot_lengths[s], 0.0, masked_score).astype(f32)[:, None] for s in over
    ]

    rows_bf16 = [(slot_rows, bf16)]
    token_pieces = [tensor.gather(a) for a in arrived]
    qkv, mixed, logs, terms = [], [], [], []
    before = ()
    for s in over:
        qkv += rows_matmul(
            token_pieces[s],
            qkv_weight,
            3 * head_width,
            lambda product, bias: ((product + bias).astype(bf16),),
            [qkv_bias],
            rows_bf16,
            before,
            most=256,
        )
        mix, log = attend(qkv[s], biases[s], 2)
        mixed.append(mix)
        logs.append(log)
        terms.append(terms_matmul(mix, mid_weight, spans))
        before = (terms[s][0][0],)
    first = [first_norm(tensor.scatter(terms[s])[0], arrived[s], row_vectors, before) for s in over]
    first_pieces = [tensor.gather(f[0]) for f in first]
    hidden, active, terms = [], [], []
    before = ()
    for s in over:
        wide, narrow = rows_matmul(
            first_pieces[s],
            up_full,
            hidden_width,
            lambda product, bias: (product + bias, gelu(product + bias).astype(bf16)),
            [hidden_bias],
            [(slot_rows, f32), (slot_rows, bf16)],
            before,
        )
        hidden.append(wide)
        active.append(narrow)
        terms.append(terms_matmul(narrow, down_full, spans))
        before = (terms[s][0][0],)
    second = [
        second_norm(tensor.scatter(terms[s])[0], first[s][1], cotangent[s], row_vectors, before) for s in over
    ]

    def give_back(rows):
        return lax.all_to_all(
            rows.reshape(groups, arrival_rows, model_width), "dp", split_axis=0, concat_axis=0, tiled=True
        )

    returned_rows = [give_back(s[0]) for s in second]

    down_pieces = [tensor.gather(s[2]) for s in second]
    hidden_grad, up_sums, terms = [], [], []
    before = ()

    def through_gelu(product, wide):
        grad = (product * gelu_slope(wide)).astype(bf16)
        return grad, jnp.sum(grad.astype(f32), axis=0, keepdims=True)

    for s in over:
        grad, total = rows_matmul(
            down_pieces[s],
            down_full,
            hidden_width,
            through_gelu,
            [hidden[s]],
            [(slot_rows, bf16), (1, f32)],
            before if s == 0 else before + (returned_rows[0],),
        )
        hidden_grad.append(grad)
        up_sums.append(total)
        terms.append(terms_matmul(grad, up_full, spans))
        before = (terms[s][0][0],)
    first_back = []

    first_sums = [tensor.scatter(t) for t in terms]

    def back_to_first(s, later):
        first_back.append(
            first_norm_back(
                first_sums[s][0], second[s][1], first[s][1], first[s][2], row_vectors, later
            )
        )
        return tensor.gather(first_back[s][1])

    grad_pieces = [back_to_first(0, before)]
    down_terms = weight_grad(down_pieces, active, (first_back[0][0], *returned_rows))
    down_sum = group.scatter(down_terms)
    up_terms = weight_grad(
        first_pieces, hidden_grad, (down_terms, *first_sums[-1][1], *grad_pieces[0][1:2], *grad_pieces[0][4:])
    )
    up_sum = group.scatter(up_terms)
    grad_pieces += [back_to_first(s, (up_terms,)) for s in over[1:]]

    def attention_in(s, later):
        return rows_matmul(
            grad_pieces[s],
            mid_weight,
            head_width,
            lambda product: (product.astype(bf16),),
            [],
            rows_bf16,
            later,
        )[0]

    def attention_back(s, mixed_grad, later):
        return attend_back(qkv[s], biases[s], mixed[s], mixed_grad, logs[s], 2, later)

    mixed_grad = [attention_in(0, (up_terms,))]
    backs, terms = [], []
    for s in over[:-1]:
        backs.append(attention_back(s, mixed_grad[s], ()))
        terms.append(terms_matmul(backs[s][0], qkv_weight, spans))
        mixed_grad.append(attention_in(s + 1, (terms[s][0][0],)))
    mid_terms = weight_grad(grad_pieces, mixed, (mixed_grad[-1],))
    mid_sum = group.scatter(mid_terms)
    backs.append(attention_back(slots - 1, mixed_grad[-1], (mid_terms, down_sum)))
    qkv_grad = [b[0] for b in backs]
    returned_grads = [
        give_back(input_grad(tensor.scatter(terms[s])[0], first_back[s][0])) for s in over[:-1]
    ]
    qkv_sum, qkv_terms, *qkv_stage = group.weight_scatter(token_pieces, qkv_grad, ())
    terms.append(terms_matmul(qkv_grad[-1], qkv_weight, spans, (qkv_terms, *returned_grads)))
    last_grad = input_grad(
        tensor.scatter(terms[-1])[0], first_back[-1][0], (*qkv_stage[1], up_sum)
    )
    returned_grads.append(give_back(last_grad))

    places = slot_dealing.T.reshape(-1)
    inverse = jnp.zeros(places.shape, jnp.int32).at[places].set(
        jnp.arange(places.shape[0], dtype=jnp.int32)
    )
    result = jnp.take(jnp.concatenate(returned_rows, axis=0), inverse, axis=0, mode="clip")
    token_gradient = jnp.take(jnp.concatenate(returned_grads, axis=0), inverse, axis=0, mode="clip")

    bias_total = sum(b[1] for b in backs).reshape(2, 2, half)
    head_grads = jnp.concatenate(
        [
            bias_total[:, 0].reshape(-1),
            bias_total[:, 1].reshape(-1),
            sum(up_sums)[0],
        ]
    )
    row_grads = jnp.concatenate(
        [sum(f[2] for f in first_back)[:3], sum(s[3] for s in second)[:3]], axis=0
    ).reshape(-1)
    row_grads = add_up(row_grads.reshape(-1, 128), "tensor")
    grads = add_up(jnp.concatenate([row_grads, head_grads.reshape(-1, 128)], axis=0), "dp").reshape(-1)
    row_shares = lax.dynamic_slice_in_dim(
        grads[: 6 * model_width].reshape(6, splits * groups, piece), tensor.me * groups + group.me, 1, axis=1
    )[:, 0]

    def share(low, width):
        return lax.dynamic_index_in_dim(grads[low : low + groups * width].reshape(groups, width), group.me, 0, False)

    base = 6 * model_width
    query_share = share(base, piece)
    value_share = share(base + head_width, piece)
    up_share = share(base + 2 * head_width, up_bias.shape[0])

    qkv_sum = qkv_sum.reshape(-1, 2, 3, half)
    return (
        result,
        token_gradient,
        qkv_sum[:, :, 0].reshape(-1, head_width),
        qkv_sum[:, :, 1].reshape(-1, head_width),
        qkv_sum[:, :, 2].reshape(-1, head_width),
        mid_sum.T,
        up_sum,
        down_sum.T,
        query_share,
        value_share,
        row_shares[0],
        row_shares[1],
        row_shares[2],
        up_share,
        row_shares[3],
        row_shares[4],
        row_shares[5],
    )


def solution(mesh):
    matrix = P("dp", "tensor")
    flipped = P("tensor", "dp")
    vector = P(("tensor", "dp"))
    arrival = P(None, ("tensor", "dp"), None)
    return jax.shard_map(
        local,
        mesh=mesh,
        in_specs=(arrival, P("dp", "tensor", None), P(), P())
        + (matrix, matrix, matrix, flipped, matrix, flipped)
        + (vector,) * 9,
        out_specs=(arrival, arrival) + (matrix, matrix, matrix, flipped, matrix, flipped) + (vector,) * 9,
        check_vma=False,
    )
```

```python
import functools
import math

import jax
import jax.numpy as jnp
from jax import lax
from jax.experimental import pallas as pl
from jax.experimental.pallas import tpu as pltpu
from jax.sharding import PartitionSpec as P

HEAD = 128
norm_epsilon = 1e-05
masked_score = -1e30
log2_e = math.log2(math.e)
head_scale = 1.0 / math.sqrt(HEAD)
gelu_root = math.sqrt(2.0 / math.pi)
bf16 = jnp.bfloat16
f32 = jnp.float32
MIB = 1024 * 1024
TALL = ((1,), (0,))
FLAT = ((1,), (1,))
DEEP = ((0,), (0,))


def dot(left, right, contract):
    return lax.dot_general(left, right, (contract, ((), ())), preferred_element_type=f32)


def shape(dims, dtype):
    return jax.ShapeDtypeStruct(tuple(dims), dtype)


def whole(array):
    return pl.BlockSpec(array.shape, lambda *i: (0,) * array.ndim)


def launch(body, grid, ins, in_specs, outs, out_specs, later=(), scratch=(), flops=0, nbytes=0, exps=0):
    later = tuple(later)
    count, skip = len(ins), len(later)

    def run(*refs):
        body(refs[:count], refs[count + skip :])

    return pl.pallas_call(
        run,
        grid=grid,
        in_specs=list(in_specs) + [pl.BlockSpec(memory_space=pl.ANY)] * skip,
        out_specs=list(out_specs),
        out_shape=list(outs),
        scratch_shapes=list(scratch),
        compiler_params=pltpu.CompilerParams(vmem_limit_bytes=60 * MIB),
        cost_estimate=pl.CostEstimate(
            flops=int(flops) // 10, bytes_accessed=int(nbytes) // 10, transcendentals=int(exps) // 10
        ),
    )(*ins, *later)


def attend(qkv, bias, halves, later=()):
    rows, columns = qkv.shape
    group = columns // halves
    heads = group // (3 * HEAD)
    width = heads * HEAD
    block = min(256, rows)

    def body(ins, outs):
        bias_ref, qkv_ref = ins
        mixed_ref, log_ref = outs
        shift = bias_ref[...]
        for head in range(heads):
            low = head * HEAD
            keys = qkv_ref[:, width + low : width + low + HEAD]
            values = qkv_ref[:, 2 * width + low : 2 * width + low + HEAD]
            for first in range(0, rows, block):
                part = slice(first, first + block)
                queries = qkv_ref[part, low : low + HEAD]
                scores = dot(keys, queries, FLAT) * (head_scale * log2_e) + shift
                peak = jnp.max(scores, axis=0, keepdims=True)
                weight = jnp.exp2(scores - peak)
                total = jnp.sum(weight, axis=0, keepdims=True)
                mixed = dot(values, weight.astype(bf16), DEEP) * (1.0 / total)
                mixed_ref[part, low : low + HEAD] = mixed.T.astype(bf16)
                log_ref[0, head : head + 1, part] = peak + jnp.log2(total)

    return launch(
        body,
        (halves,),
        [bias, qkv],
        [pl.BlockSpec((rows, 1), lambda i: (0, 0)), pl.BlockSpec((rows, group), lambda i: (0, i))],
        [shape((rows, halves * width), bf16), shape((halves, heads, rows), f32)],
        [pl.BlockSpec((rows, width), lambda i: (0, i)), pl.BlockSpec((1, heads, rows), lambda i: (i, 0, 0))],
        later,
        flops=4 * halves * heads * rows * rows * HEAD * 4,
        nbytes=rows * columns * 3,
        exps=halves * heads * rows * rows,
    )


def attend_back(qkv, bias, mixed, grads, logs, halves, later=()):
    rows, columns = qkv.shape
    group = columns // halves
    heads = group // (3 * HEAD)
    width = heads * HEAD
    block = min(256, rows)

    def body(ins, outs):
        bias_ref, qkv_ref, mixed_ref, grad_ref, log_ref = ins
        out_ref, sum_ref = outs
        shift = bias_ref[...]
        for head in range(heads):
            low = head * HEAD
            keys = qkv_ref[:, width + low : width + low + HEAD]
            values = qkv_ref[:, 2 * width + low : 2 * width + low + HEAD]
            key_total = jnp.zeros((rows, HEAD), f32)
            value_total = jnp.zeros((rows, HEAD), f32)
            query_sum = jnp.zeros((1, HEAD), f32)
            for first in range(0, rows, block):
                part = slice(first, first + block)
                queries = qkv_ref[part, low : low + HEAD]
                grad = grad_ref[part, low : low + HEAD]
                mix = mixed_ref[part, low : low + HEAD]
                centre = jnp.sum((grad.astype(f32) * mix.astype(f32)).T, axis=0, keepdims=True)
                scores = dot(keys, queries, FLAT) * (head_scale * log2_e) + shift
                weight = jnp.exp2(scores - log_ref[0, head : head + 1, part])
                weight_grad = dot(values, grad, FLAT)
                score_grad = (weight * (weight_grad - centre)).astype(bf16)
                value_total = value_total + dot(weight.astype(bf16), grad, TALL)
                key_total = key_total + dot(score_grad, queries, TALL)
                query_grad = (dot(keys, score_grad, DEEP) * head_scale).T.astype(bf16)
                out_ref[part, low : low + HEAD] = query_grad
                query_sum = query_sum + jnp.sum(query_grad.astype(f32), axis=0, keepdims=True)
            value_total = value_total.astype(bf16)
            out_ref[:, width + low : width + low + HEAD] = (key_total * head_scale).astype(bf16)
            out_ref[:, 2 * width + low : 2 * width + low + HEAD] = value_total
            sum_ref[0, :, low : low + HEAD] = query_sum
            sum_ref[0, :, width + low : width + low + HEAD] = jnp.zeros_like(query_sum)
            sum_ref[0, :, 2 * width + low : 2 * width + low + HEAD] = jnp.sum(
                value_total.astype(f32), axis=0, keepdims=True
            )

    columns_of = lambda n: pl.BlockSpec((rows, n), lambda i: (0, i))
    return launch(
        body,
        (halves,),
        [bias, qkv, mixed, grads, logs],
        [
            pl.BlockSpec((rows, 1), lambda i: (0, 0)),
            columns_of(group),
            columns_of(width),
            columns_of(width),
            pl.BlockSpec((1, heads, rows), lambda i: (i, 0, 0)),
        ],
        [shape((rows, columns), bf16), shape((halves, 1, group), f32)],
        [columns_of(group), pl.BlockSpec((1, 1, group), lambda i: (i, 0, 0))],
        later,
        flops=10 * halves * heads * rows * rows * HEAD * 4,
        nbytes=rows * columns * 6,
        exps=halves * heads * rows * rows,
    )


def tile_of(width, most):
    tile = min(width, most)
    while width % tile:
        tile //= 2
    return tile


def rows_matmul(pieces, weight, width, finish, extras, kinds, later=(), most=512):
    rows = sum(p.shape[0] for p in pieces)
    inner = weight.shape[0]
    tile = tile_of(width, most)

    def body(ins, refs):
        piece_refs, weight_ref = ins[: len(pieces)], ins[len(pieces)]
        extra_refs = ins[len(pieces) + 1 :]
        out_refs, gathered = refs[: len(kinds)], refs[len(kinds)]

        @pl.when(pl.program_id(0) == 0)
        def _():
            first = 0
            for ref in piece_refs:
                gathered[first : first + ref.shape[0], :] = ref[...]
                first += ref.shape[0]

        product = dot(gathered[...], weight_ref[...], TALL)
        for ref, value in zip(out_refs, finish(product, *[r[...] for r in extra_refs])):
            ref[...] = value

    def along(n):
        return pl.BlockSpec((n, tile), lambda j: (0, j))

    return launch(
        body,
        (width // tile,),
        [*pieces, weight, *extras],
        [whole(p) for p in pieces] + [along(inner)] + [along(e.shape[0]) for e in extras],
        [shape((n, width), dtype) for n, dtype in kinds],
        [along(n) for n, _ in kinds],
        later,
        scratch=[pltpu.VMEM((rows, inner), bf16)],
        flops=2 * rows * inner * width,
        nbytes=2 * (rows * inner + inner * width) + sum(4 * n * width for n, _ in kinds),
    )


def terms_matmul(left, weight, spans, later=(), most=512):
    rows, inner = left.shape
    outer = weight.shape[0]
    tile = tile_of(outer // 2, most)
    steps = outer // 2 // tile

    def body(ins, outs):
        left_ref, weight_ref = ins
        step = pl.program_id(0)
        product = dot(left_ref[...], weight_ref[...], FLAT).astype(bf16)
        groups = outs[: len(spans[0])], outs[len(spans[0]) :]
        for side in range(2):

            @pl.when((step < steps) if side == 0 else (step >= steps))
            def _():
                for ref, (low, high) in zip(groups[side], spans[side]):
                    ref[...] = product[low:high]

    places = [
        lambda j: (0, jnp.minimum(j, steps - 1)),
        lambda j: (0, jnp.maximum(j - steps, 0)),
    ]
    sizes = [(side, high - low) for side in range(2) for low, high in spans[side]]
    outs = launch(
        body,
        (2 * steps,),
        [left, weight],
        [whole(left), pl.BlockSpec((tile, inner), lambda j: (j, 0))],
        [shape((n, outer // 2), bf16) for _, n in sizes],
        [pl.BlockSpec((n, tile), places[side]) for side, n in sizes],
        later,
        flops=2 * rows * inner * outer,
        nbytes=2 * (rows * inner + outer * inner + rows * outer),
    )
    return outs[: len(spans[0])], outs[len(spans[0]) :]


def weight_grad(lefts, rights, later=(), core=None, most=256, row=None):
    flat = [p for pieces in lefts for p in pieces]
    outer = flat[0].shape[1]
    rows, columns = rights[0].shape
    tile = tile_of(outer, most)
    slots = len(rights)
    scalars = [] if core is None else [core.reshape(1)]
    rows_added = [] if core is None else [row]
    spare = 0 if core is None else 16

    def body(ins, refs):
        piece_refs, right_refs = ins[: len(flat)], ins[len(flat) :]
        gathered = refs[-1]
        first = 0
        for ref in piece_refs:
            gathered[first : first + ref.shape[0], :] = ref[...]
            first += ref.shape[0]
        total = None
        for slot in range(slots):
            term = dot(gathered[slot * rows : (slot + 1) * rows, :], right_refs[slot][...], DEEP)
            total = term if total is None else total + term
        refs[0][...] = total.astype(bf16)

    def body_apart(ins, refs):
        parity = lax.rem(pl.program_id(0), 2)
        total_ref = refs[2]
        body(ins[2:], (total_ref, refs[3]))
        added = jnp.broadcast_to(ins[1][...].astype(bf16), (spare, columns))

        def put(ref):
            ref[:tile, :] = total_ref[...]
            ref[tile:, :] = added

        @pl.when(parity == ins[0][0])
        def _():
            put(refs[0])

        @pl.when(parity != ins[0][0])
        def _():
            put(refs[1])

    outs = [shape((outer, columns), bf16)] if core is None else [shape((outer // tile // 2 * (tile + spare), columns), bf16)] * 2
    where = (lambda j: (j, 0)) if core is None else (lambda j: (j // 2, 0))
    result = launch(
        body if core is None else body_apart,
        (outer // tile,),
        [*scalars, *rows_added, *flat, *rights],
        [pl.BlockSpec(memory_space=pltpu.SMEM)] * len(scalars)
        + [whole(r) for r in rows_added]
        + [pl.BlockSpec((p.shape[0], tile), lambda j: (0, j)) for p in flat]
        + [whole(r) for r in rights],
        outs,
        [pl.BlockSpec((tile + spare, columns), where)] * len(outs),
        later,
        scratch=([] if core is None else [pltpu.VMEM((tile, columns), bf16)])
        + [pltpu.VMEM((slots * rows, tile), bf16)],
        flops=2 * slots * rows * outer * columns,
        nbytes=2 * (slots * rows * (outer + columns) + outer * columns),
    )
    return result[0] if core is None else result


def norm_tiles(body, rows, width, left, right, tiled, vectors, outs, sums, later):
    steps = 4
    tile = rows // steps
    n_left, n_right, n_tiled = len(left), len(right), len(tiled)

    def run(ins, refs):
        step = pl.program_id(0)
        left_refs = ins[:n_left]
        right_refs = ins[n_left : n_left + n_right]
        tiled_refs = ins[n_left + n_right : n_left + n_right + n_tiled]
        vector_ref = ins[-1] if vectors is not None else None

        def added(group):
            total = group[0][...].astype(f32)
            for ref in group[1:]:
                total = total + ref[...].astype(f32)
            return total

        both = jnp.concatenate([added(left_refs), added(right_refs)], axis=1)
        values, totals = body(both, [r[...] for r in tiled_refs], vector_ref)
        for ref, value in zip(refs, values):
            ref[...] = value.astype(ref.dtype)
        if sums:
            sum_ref = refs[-1]

            @pl.when(step == 0)
            def _():
                sum_ref[...] = jnp.zeros_like(sum_ref)

            for i, value in enumerate(totals):
                sum_ref[i : i + 1, :] += jnp.sum(value, axis=0, keepdims=True)

    def of(columns):
        return pl.BlockSpec((tile, columns), lambda i: (i, 0))

    def start(array, first):
        return pl.BlockSpec((tile, array.shape[1]), lambda i: (i + first // tile, 0))

    ins = [a for a, _ in (*left, *right)] + [*tiled] + ([vectors] if vectors is not None else [])
    return launch(
        run,
        (steps,),
        ins,
        [start(*a) for a in (*left, *right)]
        + [of(a.shape[1]) for a in tiled]
        + ([whole(vectors)] if vectors is not None else []),
        [shape((rows, c), dtype) for c, dtype in outs]
        + ([shape((8, width), f32)] if sums else []),
        [of(c) for c, _ in outs]
        + ([pl.BlockSpec((8, width), lambda i: (0, 0))] if sums else []),
        later,
        flops=rows * width * 20,
        nbytes=rows * width * 16,
    )


def normed(values):
    centred = values - jnp.mean(values, axis=-1, keepdims=True)
    inverse = lax.rsqrt(jnp.mean(centred * centred, axis=-1, keepdims=True) + norm_epsilon)
    return centred * inverse, inverse


def norm_back(grads, unit, inverse, gain):
    scaled = grads * gain
    return inverse * (
        scaled
        - jnp.mean(scaled, axis=-1, keepdims=True)
        - unit * jnp.mean(scaled * unit, axis=-1, keepdims=True)
    )


def first_norm(terms, rows, vectors, later=()):
    def body(both, tiled, v):
        unit, inverse = normed(tiled[0].astype(f32) + (both + v[0:1, :]))
        return [unit * v[1:2, :] + v[2:3, :], unit, inverse], []

    n, width = rows.shape
    kinds = [(width, bf16), (width, f32), (1, f32)]
    return norm_tiles(body, n, width, *terms, [rows], vectors, kinds, False, later)


def second_norm(terms, unit, cotangent, vectors, later=()):
    def body(both, tiled, v):
        first, grads = tiled[0] * v[1:2, :] + v[2:3, :], tiled[1].astype(f32)
        unit_two, inverse = normed(first + (both + v[3:4, :]))
        back = norm_back(grads, unit_two, inverse, v[4:5, :])
        return [unit_two * v[4:5, :] + v[5:6, :], back, back], [back, grads * unit_two, grads]

    n, width = unit.shape
    kinds = [(width, bf16), (width, f32), (width, bf16)]
    return norm_tiles(body, n, width, *terms, [unit, cotangent], vectors, kinds, True, later)


def first_norm_back(terms, back_two, unit, inverse, vectors, later=()):
    def body(both, tiled, v):
        grads = tiled[0] + both
        back = norm_back(grads, tiled[1], tiled[2], v[1:2, :])
        return [back, back], [back, grads * tiled[1], grads]

    n, width = unit.shape
    kinds = [(width, f32), (width, bf16)]
    return norm_tiles(body, n, width, *terms, [back_two, unit, inverse], vectors, kinds, True, later)


def input_grad(terms, back, later=()):
    def body(both, tiled, v):
        return [tiled[0] + both], []

    n, width = back.shape
    return norm_tiles(body, n, width, *terms, [back], None, [(width, bf16)], False, later)[0]


class TensorAxis:
    def __init__(self):
        self.size = lax.axis_size("tensor")
        self.me = lax.axis_index("tensor")
        self.square = self.size == 4
        if self.square:
            self.origins = self.me ^ jnp.array([0, 1, 3, 2], jnp.int32)
        else:
            self.origins = jnp.arange(self.size, dtype=jnp.int32)

    def swap(self, array, bit):
        return lax.ppermute(array, "tensor", [(i, i ^ bit) for i in range(self.size)])

    def gather(self, block):
        if not self.square:
            return [lax.all_gather(block, "tensor", axis=0, tiled=True)]
        half = block.shape[0] // 2
        along_x, along_y = self.swap(block, 1), self.swap(block, 2)
        far_top, far_bottom = self.swap(along_y[:half], 1), self.swap(along_x[half:], 2)
        return [block, along_x, far_top, far_bottom, along_y]

    def spans(self, rows):
        if not self.square:
            return [(0, rows)], [(0, rows)]
        r = rows // 4
        return [(r, 3 * r), (3 * r, 4 * r), (0, r)], [(2 * r, 4 * r), (r, 2 * r), (0, r)]

    def line_up(self, block):
        if not self.square:
            return lax.all_gather(block, "tensor", axis=1, tiled=True)
        width = block.shape[1]
        full = jnp.zeros((block.shape[0], 4 * width), block.dtype)
        for bits in range(4):
            piece = self.swap(block, bits) if bits else block
            full = lax.dynamic_update_slice(full, piece, (0, (self.me ^ bits) * width))
        return full

    def scatter(self, terms):
        left, right = terms
        if not self.square:
            full = jnp.concatenate([left[0], right[0]], axis=1)
            mine = lax.psum_scatter(full, "tensor", scatter_dimension=0, tiled=True)
            half = mine.shape[1] // 2
            return ([(mine[:, :half], 0)], [(mine[:, half:], 0)]), (), ()
        rows = left[1].shape[0]
        from_x, from_y = self.swap(left[0], 1), self.swap(right[0], 2)
        left_far = self.swap((left[1].astype(f32) + from_x[rows:].astype(f32)).astype(bf16), 2)
        right_far = self.swap((right[1].astype(f32) + from_y[:rows].astype(f32)).astype(bf16), 1)
        left = [(left[2], 0), (from_x, 0), (left_far, 0)]
        right = [(right[2], 0), (from_y, rows), (right_far, 0)]
        return (left, right), (from_x, from_y), (left_far, right_far)


class GroupAxis:
    def __init__(self):
        self.size = lax.axis_size("dp")
        self.me = lax.axis_index("dp")
        self.line = self.size == 8
        self.z = self.me // 2
        n = self.size
        self.next = [(i, (i + 2) % n) for i in range(n)]
        self.last = [(i, (i - 2) % n) for i in range(n)]

    def send(self, array, pairs):
        return lax.ppermute(array, "dp", pairs)

    def gather(self, shard):
        return lax.all_gather(shard, "dp", axis=0, tiled=True)

    def scatter(self, terms):
        return lax.psum_scatter(terms, "dp", scatter_dimension=0, tiled=True).astype(f32)

    def weight_scatter(self, lefts, rights, row, later):
        if not self.line:
            terms = weight_grad(lefts, rights, later)
            return self.scatter(terms), lax.psum(row, "dp")[0], terms, (), (), ()
        block = lefts[0][0].shape[1] // self.size
        mine, theirs = weight_grad(lefts, rights, later, self.me % 2, block, row)
        got = self.send(theirs, [(i, i ^ 1) for i in range(self.size)])
        rows = mine.shape[0] // 4

        def toward(step):
            first = ((self.z + step) % 4) * rows
            parts = [lax.dynamic_slice_in_dim(a, first, rows).astype(f32) for a in (mine, got)]
            return parts[0] + parts[1]

        far = toward(2).astype(bf16)
        up = self.send(far, [(0, 2), (1, 3), (2, 4), (3, 5)])
        down = self.send(far, [(6, 4), (7, 5), (4, 2), (5, 3)])
        ahead = (toward(1) + up.astype(f32)).astype(bf16)
        behind = (toward(3) + down.astype(f32)).astype(bf16)
        ahead, behind = self.send(ahead, self.next), self.send(behind, self.last)
        total = toward(0) + ahead.astype(f32) + behind.astype(f32)
        return total[:block], total[block], mine, (got,), (up, down), (ahead, behind)


def nothing(*arrays):
    return sum(a[(0,) * a.ndim].astype(f32) * 0.0 for a in arrays)


def touched(array, *arrays):
    if not arrays:
        return array
    corner = array[:16, :128]
    return lax.dynamic_update_slice(array, corner + nothing(*arrays).astype(array.dtype), (0, 0))


def add_up(array, axis, earlier=()):
    size = lax.axis_size(axis)
    bit, stages = 1, []
    while bit < size:
        if len(stages) < len(earlier) and earlier[len(stages)] is not None:
            array = array + nothing(earlier[len(stages)])
        stages.append(lax.ppermute(array, axis, [(i, i ^ bit) for i in range(size)]))
        array = array + stages[-1]
        bit *= 2
    return array, stages


def gelu(hidden):
    return 0.5 * hidden * (1.0 + jnp.tanh(gelu_root * (hidden + 0.044715 * hidden * hidden * hidden)))


def gelu_slope(hidden):
    square = hidden * hidden
    bend = jnp.tanh(gelu_root * (hidden + 0.044715 * hidden * square))
    return 0.5 * (1.0 + bend) + 0.5 * hidden * (1.0 - bend * bend) * gelu_root * (
        1.0 + 3 * 0.044715 * square
    )


def local(
    tokens,
    cotangent,
    lengths,
    dealing,
    query_weight,
    key_weight,
    value_weight,
    output_weight,
    up_weight,
    down_weight,
    query_bias,
    value_bias,
    output_bias,
    attention_gain,
    attention_shift,
    up_bias,
    down_bias,
    feedforward_gain,
    feedforward_shift,
):
    tensor, group = TensorAxis(), GroupAxis()
    groups, splits = group.size, tensor.size
    slots, own_rows, model_width = cotangent.shape
    over = range(slots)
    slot_rows = own_rows * splits
    arrival_rows = tokens.shape[1]
    head_width = query_weight.shape[1]
    half = head_width // 2
    piece = query_bias.shape[0]
    hidden_width = up_weight.shape[1]
    spans = tensor.spans(slot_rows)

    slot_dealing = dealing.reshape(groups, slots)
    sent = jnp.take(tokens, dealing, axis=0, mode="clip").reshape(groups, slots, arrival_rows, model_width)
    came = lax.all_to_all(sent, "dp", split_axis=0, concat_axis=0, tiled=True)
    zero = came[0, 0, 0, 0] * 0.0
    token_pieces, arrived = [], []
    for s in over:
        rows = came[:, s].reshape(own_rows, model_width)
        if s > 0 and tensor.square:
            rows = rows + token_pieces[0][1][0, 0] * 0.0
        arrived.append(rows)
        token_pieces.append(tensor.gather(rows))

    head_piece = jnp.concatenate([query_bias, value_bias, up_bias]).astype(bf16)
    row_piece = jnp.concatenate(
        [output_bias, attention_gain, attention_shift, down_bias, feedforward_gain, feedforward_shift]
    ).astype(bf16)
    vector = jnp.concatenate([head_piece, row_piece])
    shard_rows, spare = query_weight.shape[0], 128
    padded = jnp.zeros((shard_rows * spare,), bf16).at[: vector.shape[0]].set(vector) + zero
    three = [w.astype(bf16) for w in (query_weight, key_weight, value_weight)]
    qkv_weight = group.gather(
        jnp.concatenate(
            [w[:, :half] for w in three] + [w[:, half:] for w in three] + [padded.reshape(shard_rows, spare)],
            axis=1,
        )
    )
    mid_weight = group.gather(touched(output_weight.astype(bf16).T, came))
    up_full = group.gather(touched(up_weight.astype(bf16), came))
    down_full = group.gather(touched(down_weight.astype(bf16).T, came))
    used = -(-vector.shape[0] // spare)
    table = qkv_weight[:, 3 * head_width :].reshape(groups, shard_rows, spare)[:, :used]
    table = table.reshape(groups, -1)[:, : vector.shape[0]]
    head_vectors = table.astype(f32)
    row_table = table[:, head_piece.shape[0] :].reshape(groups, 6, piece)
    row_table = jnp.moveaxis(row_table, 1, 0).reshape(6, groups * piece)
    row_vectors = tensor.line_up(row_table).astype(f32)
    query_bias_here = head_vectors[:, :piece].reshape(-1)
    value_bias_here = head_vectors[:, piece : 2 * piece].reshape(-1)
    hidden_bias = head_vectors[:, 2 * piece : head_piece.shape[0]].reshape(1, -1)
    row_vectors = jnp.concatenate([row_vectors, jnp.zeros((2, model_width), f32)], axis=0)
    blank = jnp.zeros((half,), f32)
    qkv_bias = jnp.concatenate(
        [query_bias_here[:half], blank, value_bias_here[:half]]
        + [query_bias_here[half:], blank, value_bias_here[half:]]
    )[None]

    positions = (tensor.origins[:, None] * own_rows + jnp.arange(own_rows)[None, :]).reshape(-1)
    slot_lengths = lax.dynamic_slice_in_dim(jnp.take(lengths, dealing, axis=0), group.me * slots, slots)
    biases = [
        jnp.where(positions < slot_lengths[s], 0.0, masked_score).astype(f32)[:, None] for s in over
    ]

    rows_bf16 = [(slot_rows, bf16)]
    qkv, mixed, logs, terms, sums = [], [], [], [], []
    before = ()
    for s in over:
        qkv += rows_matmul(
            token_pieces[s],
            qkv_weight,
            3 * head_width,
            lambda product, bias: ((product + bias).astype(bf16),),
            [qkv_bias],
            rows_bf16,
            before,
            most=256,
        )
        mix, log = attend(qkv[s], biases[s], 2)
        mixed.append(mix)
        logs.append(log)
        terms.append(terms_matmul(mix, mid_weight, spans, sums[-1][1] if sums else ()))
        sums.append(tensor.scatter(terms[s]))
        before = (terms[s][0][0],)
    first, first_pieces = [], []
    for s in over:
        first.append(first_norm(sums[s][0], arrived[s], row_vectors, before))
        first_pieces.append(tensor.gather(first[s][0]))
        before = tuple(first_pieces[s][1:2] + first_pieces[s][4:])
    hidden, active, terms, sums = [], [], [], []
    before = ()
    for s in over:
        wide, narrow = rows_matmul(
            first_pieces[s],
            up_full,
            hidden_width,
            lambda product, bias: (product + bias, gelu(product + bias).astype(bf16)),
            [hidden_bias],
            [(slot_rows, f32), (slot_rows, bf16)],
            before,
        )
        hidden.append(wide)
        active.append(narrow)
        terms.append(terms_matmul(narrow, down_full, spans, sums[-1][1] if sums else ()))
        sums.append(tensor.scatter(terms[s]))
        before = (terms[s][0][0],)
    second, down_pieces = [], []
    for s in over:
        second.append(second_norm(sums[s][0], first[s][1], cotangent[s], row_vectors, before))
        down_pieces.append(tensor.gather(second[s][2]))
        before = tuple(down_pieces[s][1:2] + down_pieces[s][4:])

    def give_back(rows):
        return lax.all_to_all(
            rows.reshape(groups, arrival_rows, model_width), "dp", split_axis=0, concat_axis=0, tiled=True
        )

    returned_rows = [give_back(s[0]) for s in second]

    hidden_grad, up_sums, terms, first_sums = [], [], [], []
    before = ()

    def through_gelu(product, wide):
        grad = (product * gelu_slope(wide)).astype(bf16)
        return grad, jnp.sum(grad.astype(f32), axis=0, keepdims=True)

    for s in over:
        grad, total = rows_matmul(
            down_pieces[s],
            down_full,
            hidden_width,
            through_gelu,
            [hidden[s]],
            [(slot_rows, bf16), (1, f32)],
            before if s == 0 else before + (returned_rows[0],),
        )
        hidden_grad.append(grad)
        up_sums.append(total)
        terms.append(terms_matmul(grad, up_full, spans, first_sums[-1][1] if first_sums else ()))
        first_sums.append(tensor.scatter(terms[s]))
        before = (terms[s][0][0],)
    first_back = []

    def back_to_first(s, later):
        first_back.append(
            first_norm_back(
                first_sums[s][0], second[s][1], first[s][1], first[s][2], row_vectors, later
            )
        )
        return tensor.gather(first_back[s][1])

    grad_pieces = [back_to_first(0, before)]
    near = grad_pieces[0][1:2] + grad_pieces[0][4:]
    down_terms = weight_grad(down_pieces, active, (first_back[0][0], *returned_rows))
    down_terms = touched(down_terms, *first_sums[-1][1], *near)
    down_sum = group.scatter(down_terms)
    up_terms = weight_grad(first_pieces, hidden_grad, (down_terms,))
    up_terms = touched(up_terms, *first_sums[-1][2], *grad_pieces[0][2:4])
    up_sum = group.scatter(up_terms)
    grad_pieces += [back_to_first(s, (up_terms,)) for s in over[1:]]

    def attention_in(s, later):
        return rows_matmul(
            grad_pieces[s],
            mid_weight,
            head_width,
            lambda product: (product.astype(bf16),),
            [],
            rows_bf16,
            later,
        )[0]

    def attention_back(s, mixed_grad, later):
        return attend_back(qkv[s], biases[s], mixed[s], mixed_grad, logs[s], 2, later)

    mixed_grad = [attention_in(0, (up_terms,))]
    row_grads = jnp.concatenate(
        [sum(f[2] for f in first_back)[:3], sum(s[3] for s in second)[:3]], axis=0
    ).reshape(-1, 128)
    row_grads, stages = add_up(row_grads, "tensor", (mixed_grad[0],))
    stages = [(stage,) for stage in stages] + [(), ()]
    backs = [attention_back(0, mixed_grad[0], ())]
    terms = [terms_matmul(backs[0][0], qkv_weight, spans, stages[0])]
    sums = [tensor.scatter(terms[0])]
    mixed_grad.append(attention_in(1, (terms[0][0][0], *stages[1])))
    mid_terms = weight_grad(grad_pieces, mixed, (mixed_grad[1], *sums[0][1]))
    small = jnp.concatenate([row_grads, sum(up_sums).reshape(-1, 128)], axis=0)
    small, stages = add_up(small, "dp", (mixed_grad[1], mid_terms, None))
    mid_sum = group.scatter(mid_terms)
    token_grad = [input_grad(sums[0][0], first_back[0][0], (mid_terms,))]
    returned_grads = [give_back(token_grad[0])]
    backs.append(
        attention_back(1, mixed_grad[1], (mid_terms, token_grad[0], down_sum, stages[0]))
    )
    qkv_grad = [b[0] for b in backs]
    bias_terms = sum(b[1] for b in backs).reshape(1, -1)
    qkv_sum, bias_sum, qkv_terms, *qkv_stage = group.weight_scatter(token_pieces, qkv_grad, bias_terms, (stages[1],))
    terms.append(terms_matmul(qkv_grad[-1], qkv_weight, spans, (qkv_terms, *qkv_stage[0], *returned_grads)))
    last_grad = input_grad(
        tensor.scatter(terms[-1])[0], first_back[-1][0], (*qkv_stage[1], stages[2], up_sum)
    )
    returned_grads.append(give_back(last_grad))

    places = slot_dealing.T.reshape(-1)
    inverse = jnp.zeros(places.shape, jnp.int32).at[places].set(
        jnp.arange(places.shape[0], dtype=jnp.int32)
    )
    result = jnp.take(jnp.concatenate(returned_rows, axis=0), inverse, axis=0, mode="clip")
    token_gradient = jnp.take(jnp.concatenate(returned_grads, axis=0), inverse, axis=0, mode="clip")

    row_shares = lax.dynamic_slice_in_dim(
        small.reshape(-1)[: 6 * model_width].reshape(6, splits * groups, piece),
        tensor.me * groups + group.me,
        1,
        axis=1,
    )[:, 0]

    def share(values):
        return lax.dynamic_index_in_dim(values.reshape(groups, -1), group.me, 0, False)

    bias_sum = bias_sum.reshape(2, 3, half)
    query_share = share(bias_sum[:, 0])
    value_share = share(bias_sum[:, 2])
    up_share = share(small.reshape(-1)[6 * model_width :])

    qkv_sum = qkv_sum.reshape(-1, 2, 3, half)
    return (
        result,
        token_gradient,
        qkv_sum[:, :, 0].reshape(-1, head_width),
        qkv_sum[:, :, 1].reshape(-1, head_width),
        qkv_sum[:, :, 2].reshape(-1, head_width),
        mid_sum.T,
        up_sum,
        down_sum.T,
        query_share,
        value_share,
        row_shares[0],
        row_shares[1],
        row_shares[2],
        up_share,
        row_shares[3],
        row_shares[4],
        row_shares[5],
    )


def solution(mesh):
    matrix = P("dp", "tensor")
    flipped = P("tensor", "dp")
    vector = P(("tensor", "dp"))
    arrival = P(None, ("tensor", "dp"), None)
    return jax.shard_map(
        local,
        mesh=mesh,
        in_specs=(arrival, P("dp", "tensor", None), P(), P())
        + (matrix, matrix, matrix, flipped, matrix, flipped)
        + (vector,) * 9,
        out_specs=(arrival, arrival) + (matrix, matrix, matrix, flipped, matrix, flipped) + (vector,) * 9,
        check_vma=False,
    )
```

```python
import functools
import math

import jax
import jax.numpy as jnp
from jax import lax
from jax.experimental import pallas as pl
from jax.experimental.pallas import tpu as pltpu
from jax.sharding import PartitionSpec as P

HEAD = 128
norm_epsilon = 1e-05
masked_score = -1e30
log2_e = math.log2(math.e)
head_scale = 1.0 / math.sqrt(HEAD)
gelu_root = math.sqrt(2.0 / math.pi)
bf16 = jnp.bfloat16
f32 = jnp.float32
MIB = 1024 * 1024
cost = 2.0
TALL = ((1,), (0,))
FLAT = ((1,), (1,))
DEEP = ((0,), (0,))


def dot(left, right, contract):
    return lax.dot_general(left, right, (contract, ((), ())), preferred_element_type=f32)


def shape(dims, dtype):
    return jax.ShapeDtypeStruct(tuple(dims), dtype)


def whole(array):
    return pl.BlockSpec(array.shape, lambda *i: (0,) * array.ndim)


def launch(body, grid, ins, in_specs, outs, out_specs, later=(), scratch=(), flops=0, nbytes=0, exps=0):
    later = tuple(later)
    count, skip = len(ins), len(later)

    def run(*refs):
        body(refs[:count], refs[count + skip :])

    return pl.pallas_call(
        run,
        grid=grid,
        in_specs=list(in_specs) + [pl.BlockSpec(memory_space=pl.ANY)] * skip,
        out_specs=list(out_specs),
        out_shape=list(outs),
        scratch_shapes=list(scratch),
        compiler_params=pltpu.CompilerParams(vmem_limit_bytes=60 * MIB),
        cost_estimate=pl.CostEstimate(
            flops=int(cost * flops), bytes_accessed=int(cost * nbytes), transcendentals=int(cost * exps)
        ),
    )(*ins, *later)


def attend(qkv, bias, halves, later=()):
    rows, columns = qkv.shape
    group = columns // halves
    heads = group // (3 * HEAD)
    width = heads * HEAD
    block = min(256, rows)

    def body(ins, outs):
        bias_ref, qkv_ref = ins
        mixed_ref, log_ref = outs
        shift = bias_ref[...]
        for head in range(heads):
            low = head * HEAD
            keys = qkv_ref[:, width + low : width + low + HEAD]
            values = qkv_ref[:, 2 * width + low : 2 * width + low + HEAD]
            for first in range(0, rows, block):
                part = slice(first, first + block)
                queries = qkv_ref[part, low : low + HEAD]
                scores = dot(keys, queries, FLAT) * (head_scale * log2_e) + shift
                peak = jnp.max(scores, axis=0, keepdims=True)
                weight = jnp.exp2(scores - peak)
                total = jnp.sum(weight, axis=0, keepdims=True)
                mixed = dot(values, weight.astype(bf16), DEEP) * (1.0 / total)
                mixed_ref[part, low : low + HEAD] = mixed.T.astype(bf16)
                log_ref[0, head : head + 1, part] = peak + jnp.log2(total)

    return launch(
        body,
        (halves,),
        [bias, qkv],
        [pl.BlockSpec((rows, 1), lambda i: (0, 0)), pl.BlockSpec((rows, group), lambda i: (0, i))],
        [shape((rows, halves * width), bf16), shape((halves, heads, rows), f32)],
        [pl.BlockSpec((rows, width), lambda i: (0, i)), pl.BlockSpec((1, heads, rows), lambda i: (i, 0, 0))],
        later,
        flops=4 * halves * heads * rows * rows * HEAD * 4,
        nbytes=rows * columns * 3,
        exps=halves * heads * rows * rows,
    )


def attend_back(qkv, bias, mixed, grads, logs, halves, later=()):
    rows, columns = qkv.shape
    group = columns // halves
    heads = group // (3 * HEAD)
    width = heads * HEAD
    block = min(256, rows)

    def body(ins, outs):
        bias_ref, qkv_ref, mixed_ref, grad_ref, log_ref = ins
        out_ref, sum_ref = outs
        shift = bias_ref[...]
        for head in range(heads):
            low = head * HEAD
            keys = qkv_ref[:, width + low : width + low + HEAD]
            values = qkv_ref[:, 2 * width + low : 2 * width + low + HEAD]
            key_total = jnp.zeros((rows, HEAD), f32)
            value_total = jnp.zeros((rows, HEAD), f32)
            query_sum = jnp.zeros((1, HEAD), f32)
            for first in range(0, rows, block):
                part = slice(first, first + block)
                queries = qkv_ref[part, low : low + HEAD]
                grad = grad_ref[part, low : low + HEAD]
                mix = mixed_ref[part, low : low + HEAD]
                centre = jnp.sum((grad.astype(f32) * mix.astype(f32)).T, axis=0, keepdims=True)
                scores = dot(keys, queries, FLAT) * (head_scale * log2_e) + shift
                weight = jnp.exp2(scores - log_ref[0, head : head + 1, part])
                weight_grad = dot(values, grad, FLAT)
                score_grad = (weight * (weight_grad - centre)).astype(bf16)
                value_total = value_total + dot(weight.astype(bf16), grad, TALL)
                key_total = key_total + dot(score_grad, queries, TALL)
                query_grad = (dot(keys, score_grad, DEEP) * head_scale).T.astype(bf16)
                out_ref[part, low : low + HEAD] = query_grad
                query_sum = query_sum + jnp.sum(query_grad.astype(f32), axis=0, keepdims=True)
            value_total = value_total.astype(bf16)
            out_ref[:, width + low : width + low + HEAD] = (key_total * head_scale).astype(bf16)
            out_ref[:, 2 * width + low : 2 * width + low + HEAD] = value_total
            sum_ref[0, :, low : low + HEAD] = query_sum
            sum_ref[0, :, width + low : width + low + HEAD] = jnp.zeros_like(query_sum)
            sum_ref[0, :, 2 * width + low : 2 * width + low + HEAD] = jnp.sum(
                value_total.astype(f32), axis=0, keepdims=True
            )

    columns_of = lambda n: pl.BlockSpec((rows, n), lambda i: (0, i))
    return launch(
        body,
        (halves,),
        [bias, qkv, mixed, grads, logs],
        [
            pl.BlockSpec((rows, 1), lambda i: (0, 0)),
            columns_of(group),
            columns_of(width),
            columns_of(width),
            pl.BlockSpec((1, heads, rows), lambda i: (i, 0, 0)),
        ],
        [shape((rows, columns), bf16), shape((halves, 1, group), f32)],
        [columns_of(group), pl.BlockSpec((1, 1, group), lambda i: (i, 0, 0))],
        later,
        flops=10 * halves * heads * rows * rows * HEAD * 4,
        nbytes=rows * columns * 6,
        exps=halves * heads * rows * rows,
    )


def tile_of(width, most):
    tile = min(width, most)
    while width % tile:
        tile //= 2
    return tile


def rows_matmul(pieces, weight, width, finish, extras, kinds, later=(), most=512):
    rows = sum(p.shape[0] for p in pieces)
    inner = weight.shape[0]
    tile = tile_of(width, most)

    def body(ins, refs):
        piece_refs, weight_ref = ins[: len(pieces)], ins[len(pieces)]
        extra_refs = ins[len(pieces) + 1 :]
        out_refs, gathered = refs[: len(kinds)], refs[len(kinds)]

        @pl.when(pl.program_id(0) == 0)
        def _():
            first = 0
            for ref in piece_refs:
                gathered[first : first + ref.shape[0], :] = ref[...]
                first += ref.shape[0]

        product = dot(gathered[...], weight_ref[...], TALL)
        for ref, value in zip(out_refs, finish(product, *[r[...] for r in extra_refs])):
            ref[...] = value

    def along(n):
        return pl.BlockSpec((n, tile), lambda j: (0, j))

    return launch(
        body,
        (width // tile,),
        [*pieces, weight, *extras],
        [whole(p) for p in pieces] + [along(inner)] + [along(e.shape[0]) for e in extras],
        [shape((n, width), dtype) for n, dtype in kinds],
        [along(n) for n, _ in kinds],
        later,
        scratch=[pltpu.VMEM((rows, inner), bf16)],
        flops=2 * rows * inner * width,
        nbytes=2 * (rows * inner + inner * width) + sum(4 * n * width for n, _ in kinds),
    )


def terms_matmul(left, weight, spans, later=(), most=512):
    rows, inner = left.shape
    outer = weight.shape[0]
    tile = tile_of(outer // 2, most)
    steps = outer // 2 // tile

    def body(ins, outs):
        left_ref, weight_ref = ins
        step = pl.program_id(0)
        product = dot(left_ref[...], weight_ref[...], FLAT).astype(bf16)
        groups = outs[: len(spans[0])], outs[len(spans[0]) :]
        for side in range(2):

            @pl.when((step < steps) if side == 0 else (step >= steps))
            def _():
                for ref, (low, high) in zip(groups[side], spans[side]):
                    ref[...] = product[low:high]

    places = [
        lambda j: (0, jnp.minimum(j, steps - 1)),
        lambda j: (0, jnp.maximum(j - steps, 0)),
    ]
    sizes = [(side, high - low) for side in range(2) for low, high in spans[side]]
    outs = launch(
        body,
        (2 * steps,),
        [left, weight],
        [whole(left), pl.BlockSpec((tile, inner), lambda j: (j, 0))],
        [shape((n, outer // 2), bf16) for _, n in sizes],
        [pl.BlockSpec((n, tile), places[side]) for side, n in sizes],
        later,
        flops=2 * rows * inner * outer,
        nbytes=2 * (rows * inner + outer * inner + rows * outer),
    )
    return outs[: len(spans[0])], outs[len(spans[0]) :]


def weight_grad(lefts, rights, later=(), core=None, most=256, row=None):
    flat = [p for pieces in lefts for p in pieces]
    outer = flat[0].shape[1]
    rows, columns = rights[0].shape
    tile = tile_of(outer, most)
    slots = len(rights)
    scalars = [] if core is None else [core.reshape(1)]
    rows_added = [] if core is None else [row]
    spare = 0 if core is None else 16

    def body(ins, refs):
        piece_refs, right_refs = ins[: len(flat)], ins[len(flat) :]
        gathered = refs[-1]
        first = 0
        for ref in piece_refs:
            gathered[first : first + ref.shape[0], :] = ref[...]
            first += ref.shape[0]
        total = None
        for slot in range(slots):
            term = dot(gathered[slot * rows : (slot + 1) * rows, :], right_refs[slot][...], DEEP)
            total = term if total is None else total + term
        refs[0][...] = total.astype(bf16)

    def body_apart(ins, refs):
        parity = lax.rem(pl.program_id(0), 2)
        total_ref = refs[2]
        body(ins[2:], (total_ref, refs[3]))
        added = jnp.broadcast_to(ins[1][...].astype(bf16), (spare, columns))

        def put(ref):
            ref[:tile, :] = total_ref[...]
            ref[tile:, :] = added

        @pl.when(parity == ins[0][0])
        def _():
            put(refs[0])

        @pl.when(parity != ins[0][0])
        def _():
            put(refs[1])

    outs = [shape((outer, columns), bf16)] if core is None else [shape((outer // tile // 2 * (tile + spare), columns), bf16)] * 2
    where = (lambda j: (j, 0)) if core is None else (lambda j: (j // 2, 0))
    result = launch(
        body if core is None else body_apart,
        (outer // tile,),
        [*scalars, *rows_added, *flat, *rights],
        [pl.BlockSpec(memory_space=pltpu.SMEM)] * len(scalars)
        + [whole(r) for r in rows_added]
        + [pl.BlockSpec((p.shape[0], tile), lambda j: (0, j)) for p in flat]
        + [whole(r) for r in rights],
        outs,
        [pl.BlockSpec((tile + spare, columns), where)] * len(outs),
        later,
        scratch=([] if core is None else [pltpu.VMEM((tile, columns), bf16)])
        + [pltpu.VMEM((slots * rows, tile), bf16)],
        flops=2 * slots * rows * outer * columns,
        nbytes=2 * (slots * rows * (outer + columns) + outer * columns),
    )
    return result[0] if core is None else result


def norm_tiles(body, rows, width, left, right, tiled, vectors, outs, sums, later):
    steps = 4
    tile = rows // steps
    n_left, n_right, n_tiled = len(left), len(right), len(tiled)

    def run(ins, refs):
        step = pl.program_id(0)
        left_refs = ins[:n_left]
        right_refs = ins[n_left : n_left + n_right]
        tiled_refs = ins[n_left + n_right : n_left + n_right + n_tiled]
        vector_ref = ins[-1] if vectors is not None else None

        def added(group):
            total = group[0][...].astype(f32)
            for ref in group[1:]:
                total = total + ref[...].astype(f32)
            return total

        both = jnp.concatenate([added(left_refs), added(right_refs)], axis=1)
        values, totals = body(both, [r[...] for r in tiled_refs], vector_ref)
        for ref, value in zip(refs, values):
            ref[...] = value.astype(ref.dtype)
        if sums:
            sum_ref = refs[-1]

            @pl.when(step == 0)
            def _():
                sum_ref[...] = jnp.zeros_like(sum_ref)

            for i, value in enumerate(totals):
                sum_ref[i : i + 1, :] += jnp.sum(value, axis=0, keepdims=True)

    def of(columns):
        return pl.BlockSpec((tile, columns), lambda i: (i, 0))

    def start(array, first):
        return pl.BlockSpec((tile, array.shape[1]), lambda i: (i + first // tile, 0))

    ins = [a for a, _ in (*left, *right)] + [*tiled] + ([vectors] if vectors is not None else [])
    return launch(
        run,
        (steps,),
        ins,
        [start(*a) for a in (*left, *right)]
        + [of(a.shape[1]) for a in tiled]
        + ([whole(vectors)] if vectors is not None else []),
        [shape((rows, c), dtype) for c, dtype in outs]
        + ([shape((8, width), f32)] if sums else []),
        [of(c) for c, _ in outs]
        + ([pl.BlockSpec((8, width), lambda i: (0, 0))] if sums else []),
        later,
        flops=rows * width * 20,
        nbytes=rows * width * 16,
    )


def normed(values):
    centred = values - jnp.mean(values, axis=-1, keepdims=True)
    inverse = lax.rsqrt(jnp.mean(centred * centred, axis=-1, keepdims=True) + norm_epsilon)
    return centred * inverse, inverse


def norm_back(grads, unit, inverse, gain):
    scaled = grads * gain
    return inverse * (
        scaled
        - jnp.mean(scaled, axis=-1, keepdims=True)
        - unit * jnp.mean(scaled * unit, axis=-1, keepdims=True)
    )


def first_norm(terms, rows, vectors, later=()):
    def body(both, tiled, v):
        unit, inverse = normed(tiled[0].astype(f32) + (both + v[0:1, :]))
        return [unit * v[1:2, :] + v[2:3, :], unit, inverse], []

    n, width = rows.shape
    kinds = [(width, bf16), (width, f32), (1, f32)]
    return norm_tiles(body, n, width, *terms, [rows], vectors, kinds, False, later)


def second_norm(terms, unit, cotangent, vectors, later=()):
    def body(both, tiled, v):
        first, grads = tiled[0] * v[1:2, :] + v[2:3, :], tiled[1].astype(f32)
        unit_two, inverse = normed(first + (both + v[3:4, :]))
        back = norm_back(grads, unit_two, inverse, v[4:5, :])
        return [unit_two * v[4:5, :] + v[5:6, :], back, back], [back, grads * unit_two, grads]

    n, width = unit.shape
    kinds = [(width, bf16), (width, f32), (width, bf16)]
    return norm_tiles(body, n, width, *terms, [unit, cotangent], vectors, kinds, True, later)


def first_norm_back(terms, back_two, unit, inverse, vectors, later=()):
    def body(both, tiled, v):
        grads = tiled[0] + both
        back = norm_back(grads, tiled[1], tiled[2], v[1:2, :])
        return [back, back], [back, grads * tiled[1], grads]

    n, width = unit.shape
    kinds = [(width, f32), (width, bf16)]
    return norm_tiles(body, n, width, *terms, [back_two, unit, inverse], vectors, kinds, True, later)


def input_grad(terms, back, later=()):
    def body(both, tiled, v):
        return [tiled[0] + both], []

    n, width = back.shape
    return norm_tiles(body, n, width, *terms, [back], None, [(width, bf16)], False, later)[0]


class TensorAxis:
    def __init__(self):
        self.size = lax.axis_size("tensor")
        self.me = lax.axis_index("tensor")
        self.square = self.size == 4
        if self.square:
            self.origins = self.me ^ jnp.array([0, 1, 3, 2], jnp.int32)
        else:
            self.origins = jnp.arange(self.size, dtype=jnp.int32)

    def swap(self, array, bit):
        return lax.ppermute(array, "tensor", [(i, i ^ bit) for i in range(self.size)])

    def gather(self, block):
        if not self.square:
            return [lax.all_gather(block, "tensor", axis=0, tiled=True)]
        half = block.shape[0] // 2
        along_x, along_y = self.swap(block, 1), self.swap(block, 2)
        far_top, far_bottom = self.swap(along_y[:half], 1), self.swap(along_x[half:], 2)
        return [block, along_x, far_top, far_bottom, along_y]

    def spans(self, rows):
        if not self.square:
            return [(0, rows)], [(0, rows)]
        r = rows // 4
        return [(r, 3 * r), (3 * r, 4 * r), (0, r)], [(2 * r, 4 * r), (r, 2 * r), (0, r)]

    def line_up(self, block):
        if not self.square:
            return lax.all_gather(block, "tensor", axis=1, tiled=True)
        width = block.shape[1]
        full = jnp.zeros((block.shape[0], 4 * width), block.dtype)
        for bits in range(4):
            piece = self.swap(block, bits) if bits else block
            full = lax.dynamic_update_slice(full, piece, (0, (self.me ^ bits) * width))
        return full

    def scatter(self, terms):
        left, right = terms
        if not self.square:
            full = jnp.concatenate([left[0], right[0]], axis=1)
            mine = lax.psum_scatter(full, "tensor", scatter_dimension=0, tiled=True)
            half = mine.shape[1] // 2
            return ([(mine[:, :half], 0)], [(mine[:, half:], 0)]), (), ()
        rows = left[1].shape[0]
        from_x, from_y = self.swap(left[0], 1), self.swap(right[0], 2)
        left_far = self.swap((left[1].astype(f32) + from_x[rows:].astype(f32)).astype(bf16), 2)
        right_far = self.swap((right[1].astype(f32) + from_y[:rows].astype(f32)).astype(bf16), 1)
        left = [(left[2], 0), (from_x, 0), (left_far, 0)]
        right = [(right[2], 0), (from_y, rows), (right_far, 0)]
        return (left, right), (from_x, from_y), (left_far, right_far)


class GroupAxis:
    def __init__(self):
        self.size = lax.axis_size("dp")
        self.me = lax.axis_index("dp")
        self.line = self.size == 8
        self.z = self.me // 2
        n = self.size
        self.next = [(i, (i + 2) % n) for i in range(n)]
        self.last = [(i, (i - 2) % n) for i in range(n)]

    def send(self, array, pairs):
        return lax.ppermute(array, "dp", pairs)

    def gather(self, shard):
        return lax.all_gather(shard, "dp", axis=0, tiled=True)

    def scatter(self, terms):
        return lax.psum_scatter(terms, "dp", scatter_dimension=0, tiled=True).astype(f32)

    def weight_scatter(self, lefts, rights, row, later):
        if not self.line:
            terms = weight_grad(lefts, rights, later)
            return self.scatter(terms), lax.psum(row, "dp")[0], terms, (), (), ()
        block = lefts[0][0].shape[1] // self.size
        mine, theirs = weight_grad(lefts, rights, later, self.me % 2, block, row)
        got = self.send(theirs, [(i, i ^ 1) for i in range(self.size)])
        rows = mine.shape[0] // 4

        def toward(step):
            first = ((self.z + step) % 4) * rows
            parts = [lax.dynamic_slice_in_dim(a, first, rows).astype(f32) for a in (mine, got)]
            return parts[0] + parts[1]

        far = toward(2).astype(bf16)
        up = self.send(far, [(0, 2), (1, 3), (2, 4), (3, 5)])
        down = self.send(far, [(6, 4), (7, 5), (4, 2), (5, 3)])
        ahead = (toward(1) + up.astype(f32)).astype(bf16)
        behind = (toward(3) + down.astype(f32)).astype(bf16)
        ahead, behind = self.send(ahead, self.next), self.send(behind, self.last)
        total = toward(0) + ahead.astype(f32) + behind.astype(f32)
        return total[:block], total[block], mine, (got,), (up, down), (ahead, behind)


def nothing(*arrays):
    return sum(a[(0,) * a.ndim].astype(f32) * 0.0 for a in arrays)


def touched(array, *arrays):
    if not arrays:
        return array
    corner = array[:16, :128]
    return lax.dynamic_update_slice(array, corner + nothing(*arrays).astype(array.dtype), (0, 0))


def add_up(array, axis, earlier=()):
    size = lax.axis_size(axis)
    bit, stages = 1, []
    while bit < size:
        if len(stages) < len(earlier) and earlier[len(stages)] is not None:
            array = array + nothing(earlier[len(stages)])
        stages.append(lax.ppermute(array, axis, [(i, i ^ bit) for i in range(size)]))
        array = array + stages[-1]
        bit *= 2
    return array, stages


def gelu(hidden):
    return 0.5 * hidden * (1.0 + jnp.tanh(gelu_root * (hidden + 0.044715 * hidden * hidden * hidden)))


def gelu_slope(hidden):
    square = hidden * hidden
    bend = jnp.tanh(gelu_root * (hidden + 0.044715 * hidden * square))
    return 0.5 * (1.0 + bend) + 0.5 * hidden * (1.0 - bend * bend) * gelu_root * (
        1.0 + 3 * 0.044715 * square
    )


def local(
    tokens,
    cotangent,
    lengths,
    dealing,
    query_weight,
    key_weight,
    value_weight,
    output_weight,
    up_weight,
    down_weight,
    query_bias,
    value_bias,
    output_bias,
    attention_gain,
    attention_shift,
    up_bias,
    down_bias,
    feedforward_gain,
    feedforward_shift,
):
    tensor, group = TensorAxis(), GroupAxis()
    groups, splits = group.size, tensor.size
    slots, own_rows, model_width = cotangent.shape
    over = range(slots)
    slot_rows = own_rows * splits
    arrival_rows = tokens.shape[1]
    head_width = query_weight.shape[1]
    half = head_width // 2
    piece = query_bias.shape[0]
    hidden_width = up_weight.shape[1]
    spans = tensor.spans(slot_rows)

    slot_dealing = dealing.reshape(groups, slots)
    sent = jnp.take(tokens, dealing, axis=0, mode="clip").reshape(groups, slots, arrival_rows, model_width)
    came = lax.all_to_all(sent, "dp", split_axis=0, concat_axis=0, tiled=True)
    zero = came[0, 0, 0, 0] * 0.0
    token_pieces, arrived = [], []
    for s in over:
        rows = came[:, s].reshape(own_rows, model_width)
        if s > 0 and tensor.square:
            rows = rows + token_pieces[0][1][0, 0] * 0.0
        arrived.append(rows)
        token_pieces.append(tensor.gather(rows))

    head_piece = jnp.concatenate([query_bias, value_bias, up_bias]).astype(bf16)
    row_piece = jnp.concatenate(
        [output_bias, attention_gain, attention_shift, down_bias, feedforward_gain, feedforward_shift]
    ).astype(bf16)
    vector = jnp.concatenate([head_piece, row_piece])
    shard_rows, spare = query_weight.shape[0], 128
    padded = jnp.zeros((shard_rows * spare,), bf16).at[: vector.shape[0]].set(vector) + zero
    three = [w.astype(bf16) for w in (query_weight, key_weight, value_weight)]
    qkv_weight = group.gather(
        jnp.concatenate(
            [w[:, :half] for w in three] + [w[:, half:] for w in three] + [padded.reshape(shard_rows, spare)],
            axis=1,
        )
    )
    mid_weight = group.gather(touched(output_weight.astype(bf16).T, came))
    up_full = group.gather(touched(up_weight.astype(bf16), came))
    down_full = group.gather(touched(down_weight.astype(bf16).T, came))
    used = -(-vector.shape[0] // spare)
    table = qkv_weight[:, 3 * head_width :].reshape(groups, shard_rows, spare)[:, :used]
    table = table.reshape(groups, -1)[:, : vector.shape[0]]
    head_vectors = table.astype(f32)
    row_table = table[:, head_piece.shape[0] :].reshape(groups, 6, piece)
    row_table = jnp.moveaxis(row_table, 1, 0).reshape(6, groups * piece)
    row_vectors = tensor.line_up(row_table).astype(f32)
    query_bias_here = head_vectors[:, :piece].reshape(-1)
    value_bias_here = head_vectors[:, piece : 2 * piece].reshape(-1)
    hidden_bias = head_vectors[:, 2 * piece : head_piece.shape[0]].reshape(1, -1)
    row_vectors = jnp.concatenate([row_vectors, jnp.zeros((2, model_width), f32)], axis=0)
    blank = jnp.zeros((half,), f32)
    qkv_bias = jnp.concatenate(
        [query_bias_here[:half], blank, value_bias_here[:half]]
        + [query_bias_here[half:], blank, value_bias_here[half:]]
    )[None]

    positions = (tensor.origins[:, None] * own_rows + jnp.arange(own_rows)[None, :]).reshape(-1)
    slot_lengths = lax.dynamic_slice_in_dim(jnp.take(lengths, dealing, axis=0), group.me * slots, slots)
    biases = [
        jnp.where(positions < slot_lengths[s], 0.0, masked_score).astype(f32)[:, None] for s in over
    ]

    def near(pieces):
        return tuple(pieces[1:2] + pieces[4:])

    rows_bf16 = [(slot_rows, bf16)]
    qkv, mixed, logs, terms, sums = [], [], [], [], []
    before = near(token_pieces[1])
    for s in over:
        qkv += rows_matmul(
            token_pieces[s],
            qkv_weight,
            3 * head_width,
            lambda product, bias: ((product + bias).astype(bf16),),
            [qkv_bias],
            rows_bf16,
            before,
            most=256,
        )
        mix, log = attend(qkv[s], biases[s], 2)
        mixed.append(mix)
        logs.append(log)
        terms.append(terms_matmul(mix, mid_weight, spans, sums[-1][1] if sums else ()))
        sums.append(tensor.scatter(terms[s]))
        before = (terms[s][0][0],)
    first, first_pieces = [], []
    for s in over:
        first.append(first_norm(sums[s][0], arrived[s], row_vectors, before))
        first_pieces.append(tensor.gather(first[s][0]))
        before = near(first_pieces[s])
    hidden, active, terms, sums = [], [], [], []
    before = ()
    for s in over:
        wide, narrow = rows_matmul(
            first_pieces[s],
            up_full,
            hidden_width,
            lambda product, bias: (product + bias, gelu(product + bias).astype(bf16)),
            [hidden_bias],
            [(slot_rows, f32), (slot_rows, bf16)],
            before,
        )
        hidden.append(wide)
        active.append(narrow)
        terms.append(terms_matmul(narrow, down_full, spans, sums[-1][1] if sums else near(first_pieces[1])))
        sums.append(tensor.scatter(terms[s]))
        before = (terms[s][0][0],)
    second, down_pieces = [], []
    for s in over:
        second.append(second_norm(sums[s][0], first[s][1], cotangent[s], row_vectors, before))
        down_pieces.append(tensor.gather(second[s][2]))
        before = near(down_pieces[s])

    def give_back(rows):
        return lax.all_to_all(
            rows.reshape(groups, arrival_rows, model_width), "dp", split_axis=0, concat_axis=0, tiled=True
        )

    returned_rows = [give_back(s[0]) for s in second]

    hidden_grad, up_sums, terms, first_sums = [], [], [], []
    before = ()

    def through_gelu(product, wide):
        grad = (product * gelu_slope(wide)).astype(bf16)
        return grad, jnp.sum(grad.astype(f32), axis=0, keepdims=True)

    for s in over:
        grad, total = rows_matmul(
            down_pieces[s],
            down_full,
            hidden_width,
            through_gelu,
            [hidden[s]],
            [(slot_rows, bf16), (1, f32)],
            before,
        )
        hidden_grad.append(grad)
        up_sums.append(total)
        held = first_sums[-1][1] if first_sums else (*near(down_pieces[1]), returned_rows[0])
        terms.append(terms_matmul(grad, up_full, spans, held))
        first_sums.append(tensor.scatter(terms[s]))
        before = (terms[s][0][0],)
    first_back = []

    def back_to_first(s, later):
        first_back.append(
            first_norm_back(
                first_sums[s][0], second[s][1], first[s][1], first[s][2], row_vectors, later
            )
        )
        return tensor.gather(first_back[s][1])

    grad_pieces = [back_to_first(0, before)]
    flying = (*first_sums[1][1], *near(grad_pieces[0]))
    down_terms = weight_grad(down_pieces, active, (first_back[0][0], *returned_rows))
    up_terms = weight_grad(first_pieces, hidden_grad, (down_terms,))
    down_sum = group.scatter(touched(down_terms, up_terms, *flying))
    up_sum = group.scatter(touched(up_terms, *flying))
    grad_pieces.append(back_to_first(1, (up_terms,)))

    def attention_in(s, later):
        return rows_matmul(
            grad_pieces[s],
            mid_weight,
            head_width,
            lambda product: (product.astype(bf16),),
            [],
            rows_bf16,
            later,
        )[0]

    def attention_back(s, mixed_grad, later):
        return attend_back(qkv[s], biases[s], mixed[s], mixed_grad, logs[s], 2, later)

    mixed_grad = [attention_in(0, (up_terms,))]
    row_grads = jnp.concatenate(
        [sum(f[2] for f in first_back)[:3], sum(s[3] for s in second)[:3]], axis=0
    ).reshape(-1, 128)
    row_grads, stages = add_up(row_grads, "tensor", (mixed_grad[0],))
    stages = [(stage,) for stage in stages] + [(), ()]
    backs = [attention_back(0, mixed_grad[0], ())]
    terms = [terms_matmul(backs[0][0], qkv_weight, spans, (*stages[0], *near(grad_pieces[1])))]
    sums = [tensor.scatter(terms[0])]
    mixed_grad.append(attention_in(1, (terms[0][0][0], *stages[1])))
    mid_terms = weight_grad(grad_pieces, mixed, (mixed_grad[1],))
    small = jnp.concatenate([row_grads, sum(up_sums).reshape(-1, 128)], axis=0)
    small, stages = add_up(small, "dp", (mixed_grad[1], mid_terms, None))
    mid_sum = group.scatter(touched(mid_terms, *sums[0][1]))
    backs.append(attention_back(1, mixed_grad[1], (mid_terms, *sums[0][1], stages[0])))
    token_grad = [input_grad(sums[0][0], first_back[0][0], (backs[1][0],))]
    returned_grads = [give_back(token_grad[0])]
    qkv_grad = [b[0] for b in backs]
    bias_terms = sum(b[1] for b in backs).reshape(1, -1)
    qkv_sum, bias_sum, qkv_terms, *qkv_stage = group.weight_scatter(
        token_pieces, qkv_grad, bias_terms, (token_grad[0], down_sum, stages[1])
    )
    terms.append(terms_matmul(qkv_grad[-1], qkv_weight, spans, (qkv_terms,)))
    last_grad = input_grad(
        tensor.scatter(terms[-1])[0], first_back[-1][0], (*qkv_stage[1], *returned_grads, stages[2])
    )
    returned_grads.append(give_back(last_grad))

    places = slot_dealing.T.reshape(-1)
    inverse = jnp.zeros(places.shape, jnp.int32).at[places].set(
        jnp.arange(places.shape[0], dtype=jnp.int32)
    )
    result = jnp.take(jnp.concatenate(returned_rows, axis=0), inverse, axis=0, mode="clip")
    inverse = inverse + nothing(up_sum, mid_sum).astype(jnp.int32)
    token_gradient = jnp.take(jnp.concatenate(returned_grads, axis=0), inverse, axis=0, mode="clip")

    row_shares = lax.dynamic_slice_in_dim(
        small.reshape(-1)[: 6 * model_width].reshape(6, splits * groups, piece),
        tensor.me * groups + group.me,
        1,
        axis=1,
    )[:, 0]

    def share(values):
        return lax.dynamic_index_in_dim(values.reshape(groups, -1), group.me, 0, False)

    bias_sum = bias_sum.reshape(2, 3, half)
    query_share = share(bias_sum[:, 0])
    value_share = share(bias_sum[:, 2])
    up_share = share(small.reshape(-1)[6 * model_width :])

    qkv_sum = qkv_sum.reshape(-1, 2, 3, half)
    return (
        result,
        token_gradient,
        qkv_sum[:, :, 0].reshape(-1, head_width),
        qkv_sum[:, :, 1].reshape(-1, head_width),
        qkv_sum[:, :, 2].reshape(-1, head_width),
        mid_sum.T,
        up_sum,
        down_sum.T,
        query_share,
        value_share,
        row_shares[0],
        row_shares[1],
        row_shares[2],
        up_share,
        row_shares[3],
        row_shares[4],
        row_shares[5],
    )


def solution(mesh):
    matrix = P("dp", "tensor")
    flipped = P("tensor", "dp")
    vector = P(("tensor", "dp"))
    arrival = P(None, ("tensor", "dp"), None)
    return jax.shard_map(
        local,
        mesh=mesh,
        in_specs=(arrival, P("dp", "tensor", None), P(), P())
        + (matrix, matrix, matrix, flipped, matrix, flipped)
        + (vector,) * 9,
        out_specs=(arrival, arrival) + (matrix, matrix, matrix, flipped, matrix, flipped) + (vector,) * 9,
        check_vma=False,
    )
```

```python
import functools
import math

import jax
import jax.numpy as jnp
from jax import lax
from jax.experimental import pallas as pl
from jax.experimental.pallas import tpu as pltpu
from jax.sharding import PartitionSpec as P

HEAD = 128
norm_epsilon = 1e-05
masked_score = -1e30
log2_e = math.log2(math.e)
head_scale = 1.0 / math.sqrt(HEAD)
gelu_root = math.sqrt(2.0 / math.pi)
bf16 = jnp.bfloat16
f32 = jnp.float32
MIB = 1024 * 1024
cost = 2.0
TALL = ((1,), (0,))
FLAT = ((1,), (1,))
DEEP = ((0,), (0,))


def dot(left, right, contract):
    return lax.dot_general(left, right, (contract, ((), ())), preferred_element_type=f32)


def shape(dims, dtype):
    return jax.ShapeDtypeStruct(tuple(dims), dtype)


def whole(array):
    return pl.BlockSpec(array.shape, lambda *i: (0,) * array.ndim)


def launch(body, grid, ins, in_specs, outs, out_specs, later=(), scratch=(), flops=0, nbytes=0, exps=0):
    later = tuple(later)
    count, skip = len(ins), len(later)

    def run(*refs):
        body(refs[:count], refs[count + skip :])

    return pl.pallas_call(
        run,
        grid=grid,
        in_specs=list(in_specs) + [pl.BlockSpec(memory_space=pl.ANY)] * skip,
        out_specs=list(out_specs),
        out_shape=list(outs),
        scratch_shapes=list(scratch),
        compiler_params=pltpu.CompilerParams(vmem_limit_bytes=60 * MIB),
        cost_estimate=pl.CostEstimate(
            flops=int(cost * flops), bytes_accessed=int(cost * nbytes), transcendentals=int(cost * exps)
        ),
    )(*ins, *later)


def attend(qkv, bias, halves, later=()):
    rows, columns = qkv.shape
    group = columns // halves
    heads = group // (3 * HEAD)
    width = heads * HEAD
    block = min(256, rows)

    def body(ins, outs):
        bias_ref, qkv_ref = ins
        mixed_ref, log_ref = outs
        shift = bias_ref[...]
        for head in range(heads):
            low = head * HEAD
            keys = qkv_ref[:, width + low : width + low + HEAD]
            values = qkv_ref[:, 2 * width + low : 2 * width + low + HEAD]
            for first in range(0, rows, block):
                part = slice(first, first + block)
                queries = qkv_ref[part, low : low + HEAD]
                scores = dot(keys, queries, FLAT) * (head_scale * log2_e) + shift
                peak = jnp.max(scores, axis=0, keepdims=True)
                weight = jnp.exp2(scores - peak)
                total = jnp.sum(weight, axis=0, keepdims=True)
                mixed = dot(values, weight.astype(bf16), DEEP) * (1.0 / total)
                mixed_ref[part, low : low + HEAD] = mixed.T.astype(bf16)
                log_ref[0, head : head + 1, part] = peak + jnp.log2(total)

    return launch(
        body,
        (halves,),
        [bias, qkv],
        [pl.BlockSpec((rows, 1), lambda i: (0, 0)), pl.BlockSpec((rows, group), lambda i: (0, i))],
        [shape((rows, halves * width), bf16), shape((halves, heads, rows), f32)],
        [pl.BlockSpec((rows, width), lambda i: (0, i)), pl.BlockSpec((1, heads, rows), lambda i: (i, 0, 0))],
        later,
        flops=4 * halves * heads * rows * rows * HEAD * 4,
        nbytes=rows * columns * 3,
        exps=halves * heads * rows * rows,
    )


def attend_back(qkv, bias, mixed, grads, logs, halves, later=()):
    rows, columns = qkv.shape
    group = columns // halves
    heads = group // (3 * HEAD)
    width = heads * HEAD
    block = min(256, rows)

    def body(ins, outs):
        bias_ref, qkv_ref, mixed_ref, grad_ref, log_ref = ins
        out_ref, sum_ref = outs
        shift = bias_ref[...]
        for head in range(heads):
            low = head * HEAD
            keys = qkv_ref[:, width + low : width + low + HEAD]
            values = qkv_ref[:, 2 * width + low : 2 * width + low + HEAD]
            key_total = jnp.zeros((rows, HEAD), f32)
            value_total = jnp.zeros((rows, HEAD), f32)
            query_sum = jnp.zeros((1, HEAD), f32)
            for first in range(0, rows, block):
                part = slice(first, first + block)
                queries = qkv_ref[part, low : low + HEAD]
                grad = grad_ref[part, low : low + HEAD]
                mix = mixed_ref[part, low : low + HEAD]
                centre = jnp.sum((grad.astype(f32) * mix.astype(f32)).T, axis=0, keepdims=True)
                scores = dot(keys, queries, FLAT) * (head_scale * log2_e) + shift
                weight = jnp.exp2(scores - log_ref[0, head : head + 1, part])
                weight_grad = dot(values, grad, FLAT)
                score_grad = (weight * (weight_grad - centre)).astype(bf16)
                value_total = value_total + dot(weight.astype(bf16), grad, TALL)
                key_total = key_total + dot(score_grad, queries, TALL)
                query_grad = (dot(keys, score_grad, DEEP) * head_scale).T.astype(bf16)
                out_ref[part, low : low + HEAD] = query_grad
                query_sum = query_sum + jnp.sum(query_grad.astype(f32), axis=0, keepdims=True)
            value_total = value_total.astype(bf16)
            out_ref[:, width + low : width + low + HEAD] = (key_total * head_scale).astype(bf16)
            out_ref[:, 2 * width + low : 2 * width + low + HEAD] = value_total
            sum_ref[0, :, low : low + HEAD] = query_sum
            sum_ref[0, :, width + low : width + low + HEAD] = jnp.zeros_like(query_sum)
            sum_ref[0, :, 2 * width + low : 2 * width + low + HEAD] = jnp.sum(
                value_total.astype(f32), axis=0, keepdims=True
            )

    columns_of = lambda n: pl.BlockSpec((rows, n), lambda i: (0, i))
    return launch(
        body,
        (halves,),
        [bias, qkv, mixed, grads, logs],
        [
            pl.BlockSpec((rows, 1), lambda i: (0, 0)),
            columns_of(group),
            columns_of(width),
            columns_of(width),
            pl.BlockSpec((1, heads, rows), lambda i: (i, 0, 0)),
        ],
        [shape((rows, columns), bf16), shape((halves, 1, group), f32)],
        [columns_of(group), pl.BlockSpec((1, 1, group), lambda i: (i, 0, 0))],
        later,
        flops=10 * halves * heads * rows * rows * HEAD * 4,
        nbytes=rows * columns * 6,
        exps=halves * heads * rows * rows,
    )


def tile_of(width, most):
    tile = min(width, most)
    while width % tile:
        tile //= 2
    return tile


def rows_matmul(pieces, weight, width, finish, extras, kinds, later=(), most=512):
    rows = sum(p.shape[0] for p in pieces)
    inner = weight.shape[0]
    tile = tile_of(width, most)

    def body(ins, refs):
        piece_refs, weight_ref = ins[: len(pieces)], ins[len(pieces)]
        extra_refs = ins[len(pieces) + 1 :]
        out_refs, gathered = refs[: len(kinds)], refs[len(kinds)]

        @pl.when(pl.program_id(0) == 0)
        def _():
            first = 0
            for ref in piece_refs:
                gathered[first : first + ref.shape[0], :] = ref[...]
                first += ref.shape[0]

        product = dot(gathered[...], weight_ref[...], TALL)
        for ref, value in zip(out_refs, finish(product, *[r[...] for r in extra_refs])):
            ref[...] = value

    def along(n):
        return pl.BlockSpec((n, tile), lambda j: (0, j))

    return launch(
        body,
        (width // tile,),
        [*pieces, weight, *extras],
        [whole(p) for p in pieces] + [along(inner)] + [along(e.shape[0]) for e in extras],
        [shape((n, width), dtype) for n, dtype in kinds],
        [along(n) for n, _ in kinds],
        later,
        scratch=[pltpu.VMEM((rows, inner), bf16)],
        flops=2 * rows * inner * width,
        nbytes=2 * (rows * inner + inner * width) + sum(4 * n * width for n, _ in kinds),
    )


def terms_matmul(left, weight, spans, later=(), most=512):
    rows, inner = left.shape
    outer = weight.shape[0]
    tile = tile_of(outer // 2, most)
    steps = outer // 2 // tile

    def body(ins, outs):
        left_ref, weight_ref = ins
        step = pl.program_id(0)
        product = dot(left_ref[...], weight_ref[...], FLAT).astype(bf16)
        groups = outs[: len(spans[0])], outs[len(spans[0]) :]
        for side in range(2):

            @pl.when((step < steps) if side == 0 else (step >= steps))
            def _():
                for ref, (low, high) in zip(groups[side], spans[side]):
                    ref[...] = product[low:high]

    places = [
        lambda j: (0, jnp.minimum(j, steps - 1)),
        lambda j: (0, jnp.maximum(j - steps, 0)),
    ]
    sizes = [(side, high - low) for side in range(2) for low, high in spans[side]]
    outs = launch(
        body,
        (2 * steps,),
        [left, weight],
        [whole(left), pl.BlockSpec((tile, inner), lambda j: (j, 0))],
        [shape((n, outer // 2), bf16) for _, n in sizes],
        [pl.BlockSpec((n, tile), places[side]) for side, n in sizes],
        later,
        flops=2 * rows * inner * outer,
        nbytes=2 * (rows * inner + outer * inner + rows * outer),
    )
    return outs[: len(spans[0])], outs[len(spans[0]) :]


def weight_grad(lefts, rights, later=(), core=None, most=256, row=None):
    flat = [p for pieces in lefts for p in pieces]
    outer = flat[0].shape[1]
    rows, columns = rights[0].shape
    tile = tile_of(outer, most)
    slots = len(rights)
    scalars = [] if core is None else [core.reshape(1)]
    rows_added = [] if core is None else [row]
    spare = 0 if core is None else 16

    def body(ins, refs):
        piece_refs, right_refs = ins[: len(flat)], ins[len(flat) :]
        gathered = refs[-1]
        first = 0
        for ref in piece_refs:
            gathered[first : first + ref.shape[0], :] = ref[...]
            first += ref.shape[0]
        total = None
        for slot in range(slots):
            term = dot(gathered[slot * rows : (slot + 1) * rows, :], right_refs[slot][...], DEEP)
            total = term if total is None else total + term
        refs[0][...] = total.astype(bf16)

    def body_apart(ins, refs):
        parity = lax.rem(pl.program_id(0), 2)
        total_ref = refs[2]
        body(ins[2:], (total_ref, refs[3]))
        added = jnp.broadcast_to(ins[1][...].astype(bf16), (spare, columns))

        def put(ref):
            ref[:tile, :] = total_ref[...]
            ref[tile:, :] = added

        @pl.when(parity == ins[0][0])
        def _():
            put(refs[0])

        @pl.when(parity != ins[0][0])
        def _():
            put(refs[1])

    outs = [shape((outer, columns), bf16)] if core is None else [shape((outer // tile // 2 * (tile + spare), columns), bf16)] * 2
    where = (lambda j: (j, 0)) if core is None else (lambda j: (j // 2, 0))
    result = launch(
        body if core is None else body_apart,
        (outer // tile,),
        [*scalars, *rows_added, *flat, *rights],
        [pl.BlockSpec(memory_space=pltpu.SMEM)] * len(scalars)
        + [whole(r) for r in rows_added]
        + [pl.BlockSpec((p.shape[0], tile), lambda j: (0, j)) for p in flat]
        + [whole(r) for r in rights],
        outs,
        [pl.BlockSpec((tile + spare, columns), where)] * len(outs),
        later,
        scratch=([] if core is None else [pltpu.VMEM((tile, columns), bf16)])
        + [pltpu.VMEM((slots * rows, tile), bf16)],
        flops=2 * slots * rows * outer * columns,
        nbytes=2 * (slots * rows * (outer + columns) + outer * columns),
    )
    return result[0] if core is None else result


def norm_tiles(body, rows, width, left, right, tiled, vectors, outs, sums, later):
    steps = 4
    tile = rows // steps
    n_left, n_right, n_tiled = len(left), len(right), len(tiled)

    def run(ins, refs):
        step = pl.program_id(0)
        left_refs = ins[:n_left]
        right_refs = ins[n_left : n_left + n_right]
        tiled_refs = ins[n_left + n_right : n_left + n_right + n_tiled]
        vector_ref = ins[-1] if vectors is not None else None

        def added(group):
            total = group[0][...].astype(f32)
            for ref in group[1:]:
                total = total + ref[...].astype(f32)
            return total

        both = jnp.concatenate([added(left_refs), added(right_refs)], axis=1)
        values, totals = body(both, [r[...] for r in tiled_refs], vector_ref)
        for ref, value in zip(refs, values):
            ref[...] = value.astype(ref.dtype)
        if sums:
            sum_ref = refs[-1]

            @pl.when(step == 0)
            def _():
                sum_ref[...] = jnp.zeros_like(sum_ref)

            for i, value in enumerate(totals):
                sum_ref[i : i + 1, :] += jnp.sum(value, axis=0, keepdims=True)

    def of(columns):
        return pl.BlockSpec((tile, columns), lambda i: (i, 0))

    def start(array, first):
        return pl.BlockSpec((tile, array.shape[1]), lambda i: (i + first // tile, 0))

    ins = [a for a, _ in (*left, *right)] + [*tiled] + ([vectors] if vectors is not None else [])
    return launch(
        run,
        (steps,),
        ins,
        [start(*a) for a in (*left, *right)]
        + [of(a.shape[1]) for a in tiled]
        + ([whole(vectors)] if vectors is not None else []),
        [shape((rows, c), dtype) for c, dtype in outs]
        + ([shape((8, width), f32)] if sums else []),
        [of(c) for c, _ in outs]
        + ([pl.BlockSpec((8, width), lambda i: (0, 0))] if sums else []),
        later,
        flops=rows * width * 20,
        nbytes=rows * width * 16,
    )


def normed(values):
    centred = values - jnp.mean(values, axis=-1, keepdims=True)
    inverse = lax.rsqrt(jnp.mean(centred * centred, axis=-1, keepdims=True) + norm_epsilon)
    return centred * inverse, inverse


def norm_back(grads, unit, inverse, gain):
    scaled = grads * gain
    return inverse * (
        scaled
        - jnp.mean(scaled, axis=-1, keepdims=True)
        - unit * jnp.mean(scaled * unit, axis=-1, keepdims=True)
    )


def first_norm(terms, rows, vectors, later=()):
    def body(both, tiled, v):
        unit, inverse = normed(tiled[0].astype(f32) + (both + v[0:1, :]))
        return [unit * v[1:2, :] + v[2:3, :], unit, inverse], []

    n, width = rows.shape
    kinds = [(width, bf16), (width, f32), (1, f32)]
    return norm_tiles(body, n, width, *terms, [rows], vectors, kinds, False, later)


def second_norm(terms, unit, cotangent, vectors, later=()):
    def body(both, tiled, v):
        first, grads = tiled[0] * v[1:2, :] + v[2:3, :], tiled[1].astype(f32)
        unit_two, inverse = normed(first + (both + v[3:4, :]))
        back = norm_back(grads, unit_two, inverse, v[4:5, :])
        return [unit_two * v[4:5, :] + v[5:6, :], back, back], [back, grads * unit_two, grads]

    n, width = unit.shape
    kinds = [(width, bf16), (width, f32), (width, bf16)]
    return norm_tiles(body, n, width, *terms, [unit, cotangent], vectors, kinds, True, later)


def first_norm_back(terms, back_two, unit, inverse, vectors, later=()):
    def body(both, tiled, v):
        grads = tiled[0] + both
        back = norm_back(grads, tiled[1], tiled[2], v[1:2, :])
        return [back, back], [back, grads * tiled[1], grads]

    n, width = unit.shape
    kinds = [(width, f32), (width, bf16)]
    return norm_tiles(body, n, width, *terms, [back_two, unit, inverse], vectors, kinds, True, later)


def input_grad(terms, back, later=()):
    def body(both, tiled, v):
        return [tiled[0] + both], []

    n, width = back.shape
    return norm_tiles(body, n, width, *terms, [back], None, [(width, bf16)], False, later)[0]


class TensorAxis:
    def __init__(self):
        self.size = lax.axis_size("tensor")
        self.me = lax.axis_index("tensor")
        self.square = self.size == 4
        if self.square:
            self.origins = self.me ^ jnp.array([0, 1, 3, 2], jnp.int32)
        else:
            self.origins = jnp.arange(self.size, dtype=jnp.int32)

    def swap(self, array, bit):
        return lax.ppermute(array, "tensor", [(i, i ^ bit) for i in range(self.size)])

    def gather(self, block):
        if not self.square:
            return [lax.all_gather(block, "tensor", axis=0, tiled=True)]
        half = block.shape[0] // 2
        along_x, along_y = self.swap(block, 1), self.swap(block, 2)
        far_top, far_bottom = self.swap(along_y[:half], 1), self.swap(along_x[half:], 2)
        return [block, along_x, far_top, far_bottom, along_y]

    def spans(self, rows):
        if not self.square:
            return [(0, rows)], [(0, rows)]
        r = rows // 4
        return [(r, 3 * r), (3 * r, 4 * r), (0, r)], [(2 * r, 4 * r), (r, 2 * r), (0, r)]

    def line_up(self, block):
        if not self.square:
            return lax.all_gather(block, "tensor", axis=1, tiled=True)
        width = block.shape[1]
        full = jnp.zeros((block.shape[0], 4 * width), block.dtype)
        for bits in range(4):
            piece = self.swap(block, bits) if bits else block
            full = lax.dynamic_update_slice(full, piece, (0, (self.me ^ bits) * width))
        return full

    def scatter(self, terms):
        left, right = terms
        if not self.square:
            full = jnp.concatenate([left[0], right[0]], axis=1)
            mine = lax.psum_scatter(full, "tensor", scatter_dimension=0, tiled=True)
            half = mine.shape[1] // 2
            return ([(mine[:, :half], 0)], [(mine[:, half:], 0)]), (), ()
        rows = left[1].shape[0]
        from_x, from_y = self.swap(left[0], 1), self.swap(right[0], 2)
        left_far = self.swap((left[1].astype(f32) + from_x[rows:].astype(f32)).astype(bf16), 2)
        right_far = self.swap((right[1].astype(f32) + from_y[:rows].astype(f32)).astype(bf16), 1)
        left = [(left[2], 0), (from_x, 0), (left_far, 0)]
        right = [(right[2], 0), (from_y, rows), (right_far, 0)]
        return (left, right), (from_x, from_y), (left_far, right_far)


class GroupAxis:
    def __init__(self):
        self.size = lax.axis_size("dp")
        self.me = lax.axis_index("dp")
        self.line = self.size == 8
        self.z = self.me // 2
        n = self.size
        self.next = [(i, (i + 2) % n) for i in range(n)]
        self.last = [(i, (i - 2) % n) for i in range(n)]

    def send(self, array, pairs):
        return lax.ppermute(array, "dp", pairs)

    def gather(self, shard):
        return lax.all_gather(shard, "dp", axis=0, tiled=True)

    def scatter(self, terms):
        return lax.psum_scatter(terms, "dp", scatter_dimension=0, tiled=True).astype(f32)

    def weight_scatter(self, lefts, rights, row, later):
        if not self.line:
            terms = weight_grad(lefts, rights, later)
            return self.scatter(terms), lax.psum(row, "dp")[0], terms, (), (), ()
        block = lefts[0][0].shape[1] // self.size
        mine, theirs = weight_grad(lefts, rights, later, self.me % 2, block, row)
        got = self.send(theirs, [(i, i ^ 1) for i in range(self.size)])
        rows = mine.shape[0] // 4

        def toward(step):
            first = ((self.z + step) % 4) * rows
            parts = [lax.dynamic_slice_in_dim(a, first, rows).astype(f32) for a in (mine, got)]
            return parts[0] + parts[1]

        far = toward(2).astype(bf16)
        up = self.send(far, [(0, 2), (1, 3), (2, 4), (3, 5)])
        down = self.send(far, [(6, 4), (7, 5), (4, 2), (5, 3)])
        ahead = (toward(1) + up.astype(f32)).astype(bf16)
        behind = (toward(3) + down.astype(f32)).astype(bf16)
        ahead, behind = self.send(ahead, self.next), self.send(behind, self.last)
        total = toward(0) + ahead.astype(f32) + behind.astype(f32)
        return total[:block], total[block], mine, (got,), (up, down), (ahead, behind)


def nothing(*arrays):
    return sum(a[(0,) * a.ndim].astype(f32) * 0.0 for a in arrays)


def touched(array, *arrays):
    if not arrays:
        return array
    corner = array[:16, :128]
    return lax.dynamic_update_slice(array, corner + nothing(*arrays).astype(array.dtype), (0, 0))


def add_up(array, axis, earlier=()):
    size = lax.axis_size(axis)
    bit, stages = 1, []
    while bit < size:
        if len(stages) < len(earlier) and earlier[len(stages)] is not None:
            array = array + nothing(earlier[len(stages)])
        stages.append(lax.ppermute(array, axis, [(i, i ^ bit) for i in range(size)]))
        array = array + stages[-1]
        bit *= 2
    return array, stages


def gelu(hidden):
    return 0.5 * hidden * (1.0 + jnp.tanh(gelu_root * (hidden + 0.044715 * hidden * hidden * hidden)))


def gelu_slope(hidden):
    square = hidden * hidden
    bend = jnp.tanh(gelu_root * (hidden + 0.044715 * hidden * square))
    return 0.5 * (1.0 + bend) + 0.5 * hidden * (1.0 - bend * bend) * gelu_root * (
        1.0 + 3 * 0.044715 * square
    )


def local(
    tokens,
    cotangent,
    lengths,
    dealing,
    query_weight,
    key_weight,
    value_weight,
    output_weight,
    up_weight,
    down_weight,
    query_bias,
    value_bias,
    output_bias,
    attention_gain,
    attention_shift,
    up_bias,
    down_bias,
    feedforward_gain,
    feedforward_shift,
):
    tensor, group = TensorAxis(), GroupAxis()
    groups, splits = group.size, tensor.size
    slots, own_rows, model_width = cotangent.shape
    over = range(slots)
    slot_rows = own_rows * splits
    arrival_rows = tokens.shape[1]
    head_width = query_weight.shape[1]
    half = head_width // 2
    piece = query_bias.shape[0]
    hidden_width = up_weight.shape[1]
    spans = tensor.spans(slot_rows)

    slot_dealing = dealing.reshape(groups, slots)
    sent = jnp.take(tokens, dealing, axis=0, mode="clip").reshape(groups, slots, arrival_rows, model_width)
    came = lax.all_to_all(sent, "dp", split_axis=0, concat_axis=0, tiled=True)
    zero = came[0, 0, 0, 0] * 0.0
    token_pieces, arrived = [], []
    for s in over:
        rows = came[:, s].reshape(own_rows, model_width)
        if s > 0 and tensor.square:
            rows = rows + token_pieces[0][1][0, 0] * 0.0
        arrived.append(rows)
        token_pieces.append(tensor.gather(rows))

    head_piece = jnp.concatenate([query_bias, value_bias, up_bias]).astype(bf16)
    row_piece = jnp.concatenate(
        [output_bias, attention_gain, attention_shift, down_bias, feedforward_gain, feedforward_shift]
    ).astype(bf16)
    vector = jnp.concatenate([head_piece, row_piece])
    shard_rows, spare = query_weight.shape[0], 128
    padded = jnp.zeros((shard_rows * spare,), bf16).at[: vector.shape[0]].set(vector) + zero
    three = [w.astype(bf16) for w in (query_weight, key_weight, value_weight)]
    qkv_weight = group.gather(
        jnp.concatenate(
            [w[:, :half] for w in three] + [w[:, half:] for w in three] + [padded.reshape(shard_rows, spare)],
            axis=1,
        )
    )
    mid_weight = group.gather(touched(output_weight.astype(bf16).T, came))
    up_full = group.gather(touched(up_weight.astype(bf16), came))
    down_full = group.gather(touched(down_weight.astype(bf16).T, came))
    used = -(-vector.shape[0] // spare)
    table = qkv_weight[:, 3 * head_width :].reshape(groups, shard_rows, spare)[:, :used]
    table = table.reshape(groups, -1)[:, : vector.shape[0]]
    head_vectors = table.astype(f32)
    row_table = table[:, head_piece.shape[0] :].reshape(groups, 6, piece)
    row_table = jnp.moveaxis(row_table, 1, 0).reshape(6, groups * piece)
    row_vectors = tensor.line_up(row_table).astype(f32)
    query_bias_here = head_vectors[:, :piece].reshape(-1)
    value_bias_here = head_vectors[:, piece : 2 * piece].reshape(-1)
    hidden_bias = head_vectors[:, 2 * piece : head_piece.shape[0]].reshape(1, -1)
    row_vectors = jnp.concatenate([row_vectors, jnp.zeros((2, model_width), f32)], axis=0)
    blank = jnp.zeros((half,), f32)
    qkv_bias = jnp.concatenate(
        [query_bias_here[:half], blank, value_bias_here[:half]]
        + [query_bias_here[half:], blank, value_bias_here[half:]]
    )[None]

    positions = (tensor.origins[:, None] * own_rows + jnp.arange(own_rows)[None, :]).reshape(-1)
    slot_lengths = lax.dynamic_slice_in_dim(jnp.take(lengths, dealing, axis=0), group.me * slots, slots)
    biases = [
        jnp.where(positions < slot_lengths[s], 0.0, masked_score).astype(f32)[:, None] for s in over
    ]

    def near(pieces):
        return tuple(pieces[1:2] + pieces[4:])

    rows_bf16 = [(slot_rows, bf16)]
    qkv, mixed, logs, terms, sums = [], [], [], [], []
    before = near(token_pieces[1])
    for s in over:
        qkv += rows_matmul(
            token_pieces[s],
            qkv_weight,
            3 * head_width,
            lambda product, bias: ((product + bias).astype(bf16),),
            [qkv_bias],
            rows_bf16,
            before,
            most=256,
        )
        mix, log = attend(qkv[s], biases[s], 2)
        mixed.append(mix)
        logs.append(log)
        terms.append(terms_matmul(mix, mid_weight, spans, sums[-1][1] if sums else ()))
        sums.append(tensor.scatter(terms[s]))
        before = (terms[s][0][0],)
    first, first_pieces = [], []
    for s in over:
        first.append(first_norm(sums[s][0], arrived[s], row_vectors, before))
        first_pieces.append(tensor.gather(first[s][0]))
        before = near(first_pieces[s])
    hidden, active, terms, sums = [], [], [], []
    before = ()
    for s in over:
        wide, narrow = rows_matmul(
            first_pieces[s],
            up_full,
            hidden_width,
            lambda product, bias: (product + bias, gelu(product + bias).astype(bf16)),
            [hidden_bias],
            [(slot_rows, f32), (slot_rows, bf16)],
            before,
        )
        hidden.append(wide)
        active.append(narrow)
        before = (narrow,)
    for s in over:
        terms.append(terms_matmul(active[s], down_full, spans, before))
        sums.append(tensor.scatter(terms[s]))
        before = (terms[s][0][0],)
    second, down_pieces = [], []
    for s in over:
        second.append(second_norm(sums[s][0], first[s][1], cotangent[s], row_vectors, before))
        down_pieces.append(tensor.gather(second[s][2]))
        before = near(down_pieces[s])

    def give_back(rows):
        return lax.all_to_all(
            rows.reshape(groups, arrival_rows, model_width), "dp", split_axis=0, concat_axis=0, tiled=True
        )

    returned_rows = [give_back(s[0]) for s in second]

    hidden_grad, up_sums, terms, first_sums = [], [], [], []
    before = ()

    def through_gelu(product, wide):
        grad = (product * gelu_slope(wide)).astype(bf16)
        return grad, jnp.sum(grad.astype(f32), axis=0, keepdims=True)

    for s in over:
        grad, total = rows_matmul(
            down_pieces[s],
            down_full,
            hidden_width,
            through_gelu,
            [hidden[s]],
            [(slot_rows, bf16), (1, f32)],
            before,
        )
        hidden_grad.append(grad)
        up_sums.append(total)
        if s == 0:
            terms.append(terms_matmul(grad, up_full, spans, (*near(down_pieces[1]), returned_rows[0])))
            first_sums.append(tensor.scatter(terms[s]))
            before = (terms[s][0][0],)
    first_back = []

    def back_to_first(s, later):
        first_back.append(
            first_norm_back(
                first_sums[s][0], second[s][1], first[s][1], first[s][2], row_vectors, later
            )
        )
        return tensor.gather(first_back[s][1])

    down_terms = weight_grad(down_pieces, active, (hidden_grad[1], *first_sums[0][1], *returned_rows))
    down_terms = touched(down_terms, *first_sums[0][2])
    down_sum = group.scatter(down_terms)
    grad_pieces = [back_to_first(0, (down_terms,))]
    terms.append(terms_matmul(hidden_grad[1], up_full, spans, (first_back[0][0],)))
    first_sums.append(tensor.scatter(terms[1]))
    up_terms = weight_grad(first_pieces, hidden_grad, (terms[1][0][0],))
    up_terms = touched(up_terms, *first_sums[1][1], *near(grad_pieces[0]))
    up_sum = group.scatter(up_terms)
    grad_pieces.append(back_to_first(1, (up_terms,)))

    def attention_in(s, later):
        return rows_matmul(
            grad_pieces[s],
            mid_weight,
            head_width,
            lambda product: (product.astype(bf16),),
            [],
            rows_bf16,
            later,
        )[0]

    def attention_back(s, mixed_grad, later):
        return attend_back(qkv[s], biases[s], mixed[s], mixed_grad, logs[s], 2, later)

    mixed_grad = [attention_in(0, (up_terms,))]
    row_grads = jnp.concatenate(
        [sum(f[2] for f in first_back)[:3], sum(s[3] for s in second)[:3]], axis=0
    ).reshape(-1, 128)
    row_grads, stages = add_up(row_grads, "tensor", (mixed_grad[0],))
    stages = [(stage,) for stage in stages] + [(), ()]
    backs = [attention_back(0, mixed_grad[0], ())]
    terms = [terms_matmul(backs[0][0], qkv_weight, spans, (*stages[0], *near(grad_pieces[1])))]
    sums = [tensor.scatter(terms[0])]
    mixed_grad.append(attention_in(1, (terms[0][0][0], *stages[1])))
    mid_terms = weight_grad(grad_pieces, mixed, (mixed_grad[1],))
    small = jnp.concatenate([row_grads, sum(up_sums).reshape(-1, 128)], axis=0)
    small, stages = add_up(small, "dp", (mixed_grad[1], mid_terms, None))
    mid_sum = group.scatter(touched(mid_terms, *sums[0][1]))
    backs.append(attention_back(1, mixed_grad[1], (mid_terms, *sums[0][1], stages[0])))
    token_grad = [input_grad(sums[0][0], first_back[0][0], (backs[1][0],))]
    returned_grads = [give_back(token_grad[0])]
    qkv_grad = [b[0] for b in backs]
    bias_terms = sum(b[1] for b in backs).reshape(1, -1)
    qkv_sum, bias_sum, qkv_terms, *qkv_stage = group.weight_scatter(
        token_pieces, qkv_grad, bias_terms, (token_grad[0], down_sum, stages[1])
    )
    terms.append(terms_matmul(qkv_grad[-1], qkv_weight, spans, (qkv_terms, *returned_grads)))
    last_grad = input_grad(
        tensor.scatter(terms[-1])[0], first_back[-1][0], (*qkv_stage[1], up_sum, stages[2])
    )
    returned_grads.append(give_back(last_grad))

    places = slot_dealing.T.reshape(-1)
    inverse = jnp.zeros(places.shape, jnp.int32).at[places].set(
        jnp.arange(places.shape[0], dtype=jnp.int32)
    )
    result = jnp.take(jnp.concatenate(returned_rows, axis=0), inverse, axis=0, mode="clip")
    inverse = inverse + nothing(mid_sum).astype(jnp.int32)
    token_gradient = jnp.take(jnp.concatenate(returned_grads, axis=0), inverse, axis=0, mode="clip")

    row_shares = lax.dynamic_slice_in_dim(
        small.reshape(-1)[: 6 * model_width].reshape(6, splits * groups, piece),
        tensor.me * groups + group.me,
        1,
        axis=1,
    )[:, 0]

    def share(values):
        return lax.dynamic_index_in_dim(values.reshape(groups, -1), group.me, 0, False)

    bias_sum = bias_sum.reshape(2, 3, half)
    query_share = share(bias_sum[:, 0])
    value_share = share(bias_sum[:, 2])
    up_share = share(small.reshape(-1)[6 * model_width :])

    qkv_sum = qkv_sum.reshape(-1, 2, 3, half)
    return (
        result,
        token_gradient,
        qkv_sum[:, :, 0].reshape(-1, head_width),
        qkv_sum[:, :, 1].reshape(-1, head_width),
        qkv_sum[:, :, 2].reshape(-1, head_width),
        mid_sum.T,
        up_sum,
        down_sum.T,
        query_share,
        value_share,
        row_shares[0],
        row_shares[1],
        row_shares[2],
        up_share,
        row_shares[3],
        row_shares[4],
        row_shares[5],
    )


def solution(mesh):
    matrix = P("dp", "tensor")
    flipped = P("tensor", "dp")
    vector = P(("tensor", "dp"))
    arrival = P(None, ("tensor", "dp"), None)
    return jax.shard_map(
        local,
        mesh=mesh,
        in_specs=(arrival, P("dp", "tensor", None), P(), P())
        + (matrix, matrix, matrix, flipped, matrix, flipped)
        + (vector,) * 9,
        out_specs=(arrival, arrival) + (matrix, matrix, matrix, flipped, matrix, flipped) + (vector,) * 9,
        check_vma=False,
    )
```

```python
import functools
import math

import jax
import jax.numpy as jnp
from jax import lax
from jax.experimental import pallas as pl
from jax.experimental.pallas import tpu as pltpu
from jax.sharding import PartitionSpec as P

HEAD = 128
norm_epsilon = 1e-05
masked_score = -1e30
log2_e = math.log2(math.e)
head_scale = 1.0 / math.sqrt(HEAD)
gelu_root = math.sqrt(2.0 / math.pi)
bf16 = jnp.bfloat16
f32 = jnp.float32
MIB = 1024 * 1024
cost = 2.0
TALL = ((1,), (0,))
FLAT = ((1,), (1,))
DEEP = ((0,), (0,))


def dot(left, right, contract):
    return lax.dot_general(left, right, (contract, ((), ())), preferred_element_type=f32)


def shape(dims, dtype):
    return jax.ShapeDtypeStruct(tuple(dims), dtype)


def whole(array):
    return pl.BlockSpec(array.shape, lambda *i: (0,) * array.ndim)


def launch(body, grid, ins, in_specs, outs, out_specs, later=(), scratch=(), flops=0, nbytes=0, exps=0):
    later = tuple(later)
    count, skip = len(ins), len(later)

    def run(*refs):
        body(refs[:count], refs[count + skip :])

    return pl.pallas_call(
        run,
        grid=grid,
        in_specs=list(in_specs) + [pl.BlockSpec(memory_space=pl.ANY)] * skip,
        out_specs=list(out_specs),
        out_shape=list(outs),
        scratch_shapes=list(scratch),
        compiler_params=pltpu.CompilerParams(vmem_limit_bytes=60 * MIB),
        cost_estimate=pl.CostEstimate(
            flops=int(cost * flops), bytes_accessed=int(cost * nbytes), transcendentals=int(cost * exps)
        ),
    )(*ins, *later)


def attend(qkv, bias, halves, later=()):
    rows, columns = qkv.shape
    group = columns // halves
    heads = group // (3 * HEAD)
    width = heads * HEAD
    block = min(256, rows)

    def body(ins, outs):
        bias_ref, qkv_ref = ins
        mixed_ref, log_ref = outs
        shift = bias_ref[...]
        for head in range(heads):
            low = head * HEAD
            keys = qkv_ref[:, width + low : width + low + HEAD]
            values = qkv_ref[:, 2 * width + low : 2 * width + low + HEAD]
            for first in range(0, rows, block):
                part = slice(first, first + block)
                queries = qkv_ref[part, low : low + HEAD]
                scores = dot(keys, queries, FLAT) * (head_scale * log2_e) + shift
                peak = jnp.max(scores, axis=0, keepdims=True)
                weight = jnp.exp2(scores - peak)
                total = jnp.sum(weight, axis=0, keepdims=True)
                mixed = dot(values, weight.astype(bf16), DEEP) * (1.0 / total)
                mixed_ref[part, low : low + HEAD] = mixed.T.astype(bf16)
                log_ref[0, head : head + 1, part] = peak + jnp.log2(total)

    return launch(
        body,
        (halves,),
        [bias, qkv],
        [pl.BlockSpec((rows, 1), lambda i: (0, 0)), pl.BlockSpec((rows, group), lambda i: (0, i))],
        [shape((rows, halves * width), bf16), shape((halves, heads, rows), f32)],
        [pl.BlockSpec((rows, width), lambda i: (0, i)), pl.BlockSpec((1, heads, rows), lambda i: (i, 0, 0))],
        later,
        flops=4 * halves * heads * rows * rows * HEAD * 4,
        nbytes=rows * columns * 3,
        exps=halves * heads * rows * rows,
    )


def attend_back(qkv, bias, mixed, grads, logs, halves, later=()):
    rows, columns = qkv.shape
    group = columns // halves
    heads = group // (3 * HEAD)
    width = heads * HEAD
    block = min(256, rows)

    def body(ins, outs):
        bias_ref, qkv_ref, mixed_ref, grad_ref, log_ref = ins
        out_ref, sum_ref = outs
        shift = bias_ref[...]
        for head in range(heads):
            low = head * HEAD
            keys = qkv_ref[:, width + low : width + low + HEAD]
            values = qkv_ref[:, 2 * width + low : 2 * width + low + HEAD]
            key_total = jnp.zeros((rows, HEAD), f32)
            value_total = jnp.zeros((rows, HEAD), f32)
            query_sum = jnp.zeros((1, HEAD), f32)
            for first in range(0, rows, block):
                part = slice(first, first + block)
                queries = qkv_ref[part, low : low + HEAD]
                grad = grad_ref[part, low : low + HEAD]
                mix = mixed_ref[part, low : low + HEAD]
                centre = jnp.sum((grad.astype(f32) * mix.astype(f32)).T, axis=0, keepdims=True)
                scores = dot(keys, queries, FLAT) * (head_scale * log2_e) + shift
                weight = jnp.exp2(scores - log_ref[0, head : head + 1, part])
                weight_grad = dot(values, grad, FLAT)
                score_grad = (weight * (weight_grad - centre)).astype(bf16)
                value_total = value_total + dot(weight.astype(bf16), grad, TALL)
                key_total = key_total + dot(score_grad, queries, TALL)
                query_grad = (dot(keys, score_grad, DEEP) * head_scale).T.astype(bf16)
                out_ref[part, low : low + HEAD] = query_grad
                query_sum = query_sum + jnp.sum(query_grad.astype(f32), axis=0, keepdims=True)
            value_total = value_total.astype(bf16)
            out_ref[:, width + low : width + low + HEAD] = (key_total * head_scale).astype(bf16)
            out_ref[:, 2 * width + low : 2 * width + low + HEAD] = value_total
            sum_ref[0, :, low : low + HEAD] = query_sum
            sum_ref[0, :, width + low : width + low + HEAD] = jnp.zeros_like(query_sum)
            sum_ref[0, :, 2 * width + low : 2 * width + low + HEAD] = jnp.sum(
                value_total.astype(f32), axis=0, keepdims=True
            )

    columns_of = lambda n: pl.BlockSpec((rows, n), lambda i: (0, i))
    return launch(
        body,
        (halves,),
        [bias, qkv, mixed, grads, logs],
        [
            pl.BlockSpec((rows, 1), lambda i: (0, 0)),
            columns_of(group),
            columns_of(width),
            columns_of(width),
            pl.BlockSpec((1, heads, rows), lambda i: (i, 0, 0)),
        ],
        [shape((rows, columns), bf16), shape((halves, 1, group), f32)],
        [columns_of(group), pl.BlockSpec((1, 1, group), lambda i: (i, 0, 0))],
        later,
        flops=10 * halves * heads * rows * rows * HEAD * 4,
        nbytes=rows * columns * 6,
        exps=halves * heads * rows * rows,
    )


def tile_of(width, most):
    tile = min(width, most)
    while width % tile:
        tile //= 2
    return tile


def rows_matmul(pieces, weight, width, finish, extras, kinds, later=(), most=512):
    rows = sum(p.shape[0] for p in pieces)
    inner = weight.shape[0]
    tile = tile_of(width, most)

    def body(ins, refs):
        piece_refs, weight_ref = ins[: len(pieces)], ins[len(pieces)]
        extra_refs = ins[len(pieces) + 1 :]
        out_refs, gathered = refs[: len(kinds)], refs[len(kinds)]

        @pl.when(pl.program_id(0) == 0)
        def _():
            first = 0
            for ref in piece_refs:
                gathered[first : first + ref.shape[0], :] = ref[...]
                first += ref.shape[0]

        product = dot(gathered[...], weight_ref[...], TALL)
        for ref, value in zip(out_refs, finish(product, *[r[...] for r in extra_refs])):
            ref[...] = value

    def along(n):
        return pl.BlockSpec((n, tile), lambda j: (0, j))

    return launch(
        body,
        (width // tile,),
        [*pieces, weight, *extras],
        [whole(p) for p in pieces] + [along(inner)] + [along(e.shape[0]) for e in extras],
        [shape((n, width), dtype) for n, dtype in kinds],
        [along(n) for n, _ in kinds],
        later,
        scratch=[pltpu.VMEM((rows, inner), bf16)],
        flops=2 * rows * inner * width,
        nbytes=2 * (rows * inner + inner * width) + sum(4 * n * width for n, _ in kinds),
    )


def terms_matmul(left, weight, spans, later=(), most=512):
    rows, inner = left.shape
    outer = weight.shape[0]
    tile = tile_of(outer // 2, most)
    steps = outer // 2 // tile

    def body(ins, outs):
        left_ref, weight_ref = ins
        step = pl.program_id(0)
        product = dot(left_ref[...], weight_ref[...], FLAT).astype(bf16)
        groups = outs[: len(spans[0])], outs[len(spans[0]) :]
        for side in range(2):

            @pl.when((step < steps) if side == 0 else (step >= steps))
            def _():
                for ref, (low, high) in zip(groups[side], spans[side]):
                    ref[...] = product[low:high]

    places = [
        lambda j: (0, jnp.minimum(j, steps - 1)),
        lambda j: (0, jnp.maximum(j - steps, 0)),
    ]
    sizes = [(side, high - low) for side in range(2) for low, high in spans[side]]
    outs = launch(
        body,
        (2 * steps,),
        [left, weight],
        [whole(left), pl.BlockSpec((tile, inner), lambda j: (j, 0))],
        [shape((n, outer // 2), bf16) for _, n in sizes],
        [pl.BlockSpec((n, tile), places[side]) for side, n in sizes],
        later,
        flops=2 * rows * inner * outer,
        nbytes=2 * (rows * inner + outer * inner + rows * outer),
    )
    return outs[: len(spans[0])], outs[len(spans[0]) :]


def weight_grad(lefts, rights, later=(), core=None, most=256, row=None):
    flat = [p for pieces in lefts for p in pieces]
    outer = flat[0].shape[1]
    rows, columns = rights[0].shape
    tile = tile_of(outer, most)
    slots = len(rights)
    scalars = [] if core is None else [core.reshape(1)]
    rows_added = [] if core is None else [row]
    spare = 0 if core is None else 16

    def body(ins, refs):
        piece_refs, right_refs = ins[: len(flat)], ins[len(flat) :]
        gathered = refs[-1]
        first = 0
        for ref in piece_refs:
            gathered[first : first + ref.shape[0], :] = ref[...]
            first += ref.shape[0]
        total = None
        for slot in range(slots):
            term = dot(gathered[slot * rows : (slot + 1) * rows, :], right_refs[slot][...], DEEP)
            total = term if total is None else total + term
        refs[0][...] = total.astype(bf16)

    def body_apart(ins, refs):
        parity = lax.rem(pl.program_id(0), 2)
        total_ref = refs[2]
        body(ins[2:], (total_ref, refs[3]))
        added = jnp.broadcast_to(ins[1][...].astype(bf16), (spare, columns))

        def put(ref):
            ref[:tile, :] = total_ref[...]
            ref[tile:, :] = added

        @pl.when(parity == ins[0][0])
        def _():
            put(refs[0])

        @pl.when(parity != ins[0][0])
        def _():
            put(refs[1])

    outs = [shape((outer, columns), bf16)] if core is None else [shape((outer // tile // 2 * (tile + spare), columns), bf16)] * 2
    where = (lambda j: (j, 0)) if core is None else (lambda j: (j // 2, 0))
    result = launch(
        body if core is None else body_apart,
        (outer // tile,),
        [*scalars, *rows_added, *flat, *rights],
        [pl.BlockSpec(memory_space=pltpu.SMEM)] * len(scalars)
        + [whole(r) for r in rows_added]
        + [pl.BlockSpec((p.shape[0], tile), lambda j: (0, j)) for p in flat]
        + [whole(r) for r in rights],
        outs,
        [pl.BlockSpec((tile + spare, columns), where)] * len(outs),
        later,
        scratch=([] if core is None else [pltpu.VMEM((tile, columns), bf16)])
        + [pltpu.VMEM((slots * rows, tile), bf16)],
        flops=2 * slots * rows * outer * columns,
        nbytes=2 * (slots * rows * (outer + columns) + outer * columns),
    )
    return result[0] if core is None else result


def norm_tiles(body, rows, width, left, right, tiled, vectors, outs, sums, later):
    steps = 4
    tile = rows // steps
    n_left, n_right, n_tiled = len(left), len(right), len(tiled)

    def run(ins, refs):
        step = pl.program_id(0)
        left_refs = ins[:n_left]
        right_refs = ins[n_left : n_left + n_right]
        tiled_refs = ins[n_left + n_right : n_left + n_right + n_tiled]
        vector_ref = ins[-1] if vectors is not None else None

        def added(group):
            total = group[0][...].astype(f32)
            for ref in group[1:]:
                total = total + ref[...].astype(f32)
            return total

        both = jnp.concatenate([added(left_refs), added(right_refs)], axis=1)
        values, totals = body(both, [r[...] for r in tiled_refs], vector_ref)
        for ref, value in zip(refs, values):
            ref[...] = value.astype(ref.dtype)
        if sums:
            sum_ref = refs[-1]

            @pl.when(step == 0)
            def _():
                sum_ref[...] = jnp.zeros_like(sum_ref)

            for i, value in enumerate(totals):
                sum_ref[i : i + 1, :] += jnp.sum(value, axis=0, keepdims=True)

    def of(columns):
        return pl.BlockSpec((tile, columns), lambda i: (i, 0))

    def start(array, first):
        return pl.BlockSpec((tile, array.shape[1]), lambda i: (i + first // tile, 0))

    ins = [a for a, _ in (*left, *right)] + [*tiled] + ([vectors] if vectors is not None else [])
    return launch(
        run,
        (steps,),
        ins,
        [start(*a) for a in (*left, *right)]
        + [of(a.shape[1]) for a in tiled]
        + ([whole(vectors)] if vectors is not None else []),
        [shape((rows, c), dtype) for c, dtype in outs]
        + ([shape((8, width), f32)] if sums else []),
        [of(c) for c, _ in outs]
        + ([pl.BlockSpec((8, width), lambda i: (0, 0))] if sums else []),
        later,
        flops=rows * width * 20,
        nbytes=rows * width * 16,
    )


def normed(values):
    centred = values - jnp.mean(values, axis=-1, keepdims=True)
    inverse = lax.rsqrt(jnp.mean(centred * centred, axis=-1, keepdims=True) + norm_epsilon)
    return centred * inverse, inverse


def norm_back(grads, unit, inverse, gain):
    scaled = grads * gain
    return inverse * (
        scaled
        - jnp.mean(scaled, axis=-1, keepdims=True)
        - unit * jnp.mean(scaled * unit, axis=-1, keepdims=True)
    )


def first_norm(terms, rows, vectors, later=()):
    def body(both, tiled, v):
        unit, inverse = normed(tiled[0].astype(f32) + (both + v[0:1, :]))
        return [unit * v[1:2, :] + v[2:3, :], unit, inverse], []

    n, width = rows.shape
    kinds = [(width, bf16), (width, f32), (1, f32)]
    return norm_tiles(body, n, width, *terms, [rows], vectors, kinds, False, later)


def second_norm(terms, unit, cotangent, vectors, later=()):
    def body(both, tiled, v):
        first, grads = tiled[0] * v[1:2, :] + v[2:3, :], tiled[1].astype(f32)
        unit_two, inverse = normed(first + (both + v[3:4, :]))
        back = norm_back(grads, unit_two, inverse, v[4:5, :])
        return [unit_two * v[4:5, :] + v[5:6, :], back, back], [back, grads * unit_two, grads]

    n, width = unit.shape
    kinds = [(width, bf16), (width, f32), (width, bf16)]
    return norm_tiles(body, n, width, *terms, [unit, cotangent], vectors, kinds, True, later)


def first_norm_back(terms, back_two, unit, inverse, vectors, later=()):
    def body(both, tiled, v):
        grads = tiled[0] + both
        back = norm_back(grads, tiled[1], tiled[2], v[1:2, :])
        return [back, back], [back, grads * tiled[1], grads]

    n, width = unit.shape
    kinds = [(width, f32), (width, bf16)]
    return norm_tiles(body, n, width, *terms, [back_two, unit, inverse], vectors, kinds, True, later)


def input_grad(terms, back, later=()):
    def body(both, tiled, v):
        return [tiled[0] + both], []

    n, width = back.shape
    return norm_tiles(body, n, width, *terms, [back], None, [(width, bf16)], False, later)[0]


class TensorAxis:
    def __init__(self):
        self.size = lax.axis_size("tensor")
        self.me = lax.axis_index("tensor")
        self.square = self.size == 4
        if self.square:
            self.origins = self.me ^ jnp.array([0, 1, 3, 2], jnp.int32)
        else:
            self.origins = jnp.arange(self.size, dtype=jnp.int32)

    def swap(self, array, bit):
        return lax.ppermute(array, "tensor", [(i, i ^ bit) for i in range(self.size)])

    def gather(self, block):
        if not self.square:
            return [lax.all_gather(block, "tensor", axis=0, tiled=True)]
        half = block.shape[0] // 2
        along_x, along_y = self.swap(block, 1), self.swap(block, 2)
        far_top, far_bottom = self.swap(along_y[:half], 1), self.swap(along_x[half:], 2)
        return [block, along_x, far_top, far_bottom, along_y]

    def spans(self, rows):
        if not self.square:
            return [(0, rows)], [(0, rows)]
        r = rows // 4
        return [(r, 3 * r), (3 * r, 4 * r), (0, r)], [(2 * r, 4 * r), (r, 2 * r), (0, r)]

    def line_up(self, block):
        if not self.square:
            return lax.all_gather(block, "tensor", axis=1, tiled=True)
        width = block.shape[1]
        full = jnp.zeros((block.shape[0], 4 * width), block.dtype)
        for bits in range(4):
            piece = self.swap(block, bits) if bits else block
            full = lax.dynamic_update_slice(full, piece, (0, (self.me ^ bits) * width))
        return full

    def scatter(self, terms):
        left, right = terms
        if not self.square:
            full = jnp.concatenate([left[0], right[0]], axis=1)
            mine = lax.psum_scatter(full, "tensor", scatter_dimension=0, tiled=True)
            half = mine.shape[1] // 2
            return ([(mine[:, :half], 0)], [(mine[:, half:], 0)]), (), ()
        rows = left[1].shape[0]
        from_x, from_y = self.swap(left[0], 1), self.swap(right[0], 2)
        left_far = self.swap((left[1].astype(f32) + from_x[rows:].astype(f32)).astype(bf16), 2)
        right_far = self.swap((right[1].astype(f32) + from_y[:rows].astype(f32)).astype(bf16), 1)
        left = [(left[2], 0), (from_x, 0), (left_far, 0)]
        right = [(right[2], 0), (from_y, rows), (right_far, 0)]
        return (left, right), (from_x, from_y), (left_far, right_far)


class GroupAxis:
    def __init__(self):
        self.size = lax.axis_size("dp")
        self.me = lax.axis_index("dp")
        self.line = self.size == 8
        self.z = self.me // 2
        n = self.size
        self.next = [(i, (i + 2) % n) for i in range(n)]
        self.last = [(i, (i - 2) % n) for i in range(n)]

    def send(self, array, pairs):
        return lax.ppermute(array, "dp", pairs)

    def gather(self, shard):
        return lax.all_gather(shard, "dp", axis=0, tiled=True)

    def scatter(self, terms):
        return lax.psum_scatter(terms, "dp", scatter_dimension=0, tiled=True).astype(f32)

    def weight_scatter(self, lefts, rights, row, later):
        if not self.line:
            terms = weight_grad(lefts, rights, later)
            return self.scatter(terms), lax.psum(row, "dp")[0], terms, (), (), ()
        block = lefts[0][0].shape[1] // self.size
        mine, theirs = weight_grad(lefts, rights, later, self.me % 2, block, row)
        got = self.send(theirs, [(i, i ^ 1) for i in range(self.size)])
        rows = mine.shape[0] // 4

        def toward(step):
            first = ((self.z + step) % 4) * rows
            parts = [lax.dynamic_slice_in_dim(a, first, rows).astype(f32) for a in (mine, got)]
            return parts[0] + parts[1]

        far = toward(2).astype(bf16)
        up = self.send(far, [(0, 2), (1, 3), (2, 4), (3, 5)])
        down = self.send(far, [(6, 4), (7, 5), (4, 2), (5, 3)])
        ahead = (toward(1) + up.astype(f32)).astype(bf16)
        behind = (toward(3) + down.astype(f32)).astype(bf16)
        ahead, behind = self.send(ahead, self.next), self.send(behind, self.last)
        total = toward(0) + ahead.astype(f32) + behind.astype(f32)
        return total[:block], total[block], mine, (got,), (up, down), (ahead, behind)


def nothing(*arrays):
    return sum(a[(0,) * a.ndim].astype(f32) * 0.0 for a in arrays)


def touched(array, *arrays):
    if not arrays:
        return array
    corner = array[:16, :128]
    return lax.dynamic_update_slice(array, corner + nothing(*arrays).astype(array.dtype), (0, 0))


def add_up(array, axis, earlier=()):
    size = lax.axis_size(axis)
    bit, stages = 1, []
    while bit < size:
        if len(stages) < len(earlier) and earlier[len(stages)] is not None:
            array = array + nothing(earlier[len(stages)])
        stages.append(lax.ppermute(array, axis, [(i, i ^ bit) for i in range(size)]))
        array = array + stages[-1]
        bit *= 2
    return array, stages


def gelu(hidden):
    return 0.5 * hidden * (1.0 + jnp.tanh(gelu_root * (hidden + 0.044715 * hidden * hidden * hidden)))


def gelu_slope(hidden):
    square = hidden * hidden
    bend = jnp.tanh(gelu_root * (hidden + 0.044715 * hidden * square))
    return 0.5 * (1.0 + bend) + 0.5 * hidden * (1.0 - bend * bend) * gelu_root * (
        1.0 + 3 * 0.044715 * square
    )


def local(
    tokens,
    cotangent,
    lengths,
    dealing,
    query_weight,
    key_weight,
    value_weight,
    output_weight,
    up_weight,
    down_weight,
    query_bias,
    value_bias,
    output_bias,
    attention_gain,
    attention_shift,
    up_bias,
    down_bias,
    feedforward_gain,
    feedforward_shift,
):
    tensor, group = TensorAxis(), GroupAxis()
    groups, splits = group.size, tensor.size
    slots, own_rows, model_width = cotangent.shape
    over = range(slots)
    slot_rows = own_rows * splits
    arrival_rows = tokens.shape[1]
    head_width = query_weight.shape[1]
    half = head_width // 2
    piece = query_bias.shape[0]
    hidden_width = up_weight.shape[1]
    spans = tensor.spans(slot_rows)

    slot_dealing = dealing.reshape(groups, slots)
    sent = jnp.take(tokens, dealing, axis=0, mode="clip").reshape(groups, slots, arrival_rows, model_width)
    came = lax.all_to_all(sent, "dp", split_axis=0, concat_axis=0, tiled=True)
    zero = came[0, 0, 0, 0] * 0.0
    token_pieces, arrived = [], []
    for s in over:
        rows = came[:, s].reshape(own_rows, model_width)
        if s > 0 and tensor.square:
            rows = rows + token_pieces[0][1][0, 0] * 0.0
        arrived.append(rows)
        token_pieces.append(tensor.gather(rows))

    head_piece = jnp.concatenate([query_bias, value_bias, up_bias]).astype(bf16)
    row_piece = jnp.concatenate(
        [output_bias, attention_gain, attention_shift, down_bias, feedforward_gain, feedforward_shift]
    ).astype(bf16)
    vector = jnp.concatenate([head_piece, row_piece])
    shard_rows, spare = query_weight.shape[0], 128
    padded = jnp.zeros((shard_rows * spare,), bf16).at[: vector.shape[0]].set(vector) + zero
    three = [w.astype(bf16) for w in (query_weight, key_weight, value_weight)]
    qkv_weight = group.gather(
        jnp.concatenate(
            [w[:, :half] for w in three] + [w[:, half:] for w in three] + [padded.reshape(shard_rows, spare)],
            axis=1,
        )
    )
    mid_weight = group.gather(touched(output_weight.astype(bf16).T, came))
    up_full = group.gather(touched(up_weight.astype(bf16), came))
    down_full = group.gather(touched(down_weight.astype(bf16).T, came))
    used = -(-vector.shape[0] // spare)
    table = qkv_weight[:, 3 * head_width :].reshape(groups, shard_rows, spare)[:, :used]
    table = table.reshape(groups, -1)[:, : vector.shape[0]]
    head_vectors = table.astype(f32)
    row_table = table[:, head_piece.shape[0] :].reshape(groups, 6, piece)
    row_table = jnp.moveaxis(row_table, 1, 0).reshape(6, groups * piece)
    row_vectors = tensor.line_up(row_table).astype(f32)
    query_bias_here = head_vectors[:, :piece].reshape(-1)
    value_bias_here = head_vectors[:, piece : 2 * piece].reshape(-1)
    hidden_bias = head_vectors[:, 2 * piece : head_piece.shape[0]].reshape(1, -1)
    row_vectors = jnp.concatenate([row_vectors, jnp.zeros((2, model_width), f32)], axis=0)
    blank = jnp.zeros((half,), f32)
    qkv_bias = jnp.concatenate(
        [query_bias_here[:half], blank, value_bias_here[:half]]
        + [query_bias_here[half:], blank, value_bias_here[half:]]
    )[None]

    positions = (tensor.origins[:, None] * own_rows + jnp.arange(own_rows)[None, :]).reshape(-1)
    slot_lengths = lax.dynamic_slice_in_dim(jnp.take(lengths, dealing, axis=0), group.me * slots, slots)
    biases = [
        jnp.where(positions < slot_lengths[s], 0.0, masked_score).astype(f32)[:, None] for s in over
    ]

    def near(pieces):
        return tuple(pieces[1:2] + pieces[4:])

    rows_bf16 = [(slot_rows, bf16)]
    qkv, mixed, logs, terms, sums = [], [], [], [], []
    before = near(token_pieces[1])
    for s in over:
        qkv += rows_matmul(
            token_pieces[s],
            qkv_weight,
            3 * head_width,
            lambda product, bias: ((product + bias).astype(bf16),),
            [qkv_bias],
            rows_bf16,
            before,
            most=256,
        )
        mix, log = attend(qkv[s], biases[s], 2)
        mixed.append(mix)
        logs.append(log)
        terms.append(terms_matmul(mix, mid_weight, spans, sums[-1][1] if sums else (row_vectors,)))
        sums.append(tensor.scatter(terms[s]))
        before = (terms[s][0][0],)
    first, first_pieces = [], []
    for s in over:
        first.append(first_norm(sums[s][0], arrived[s], row_vectors, before))
        first_pieces.append(tensor.gather(first[s][0]))
        before = near(first_pieces[s])
    hidden, active, terms, sums = [], [], [], []
    before = ()
    for s in over:
        wide, narrow = rows_matmul(
            first_pieces[s],
            up_full,
            hidden_width,
            lambda product, bias: (product + bias, gelu(product + bias).astype(bf16)),
            [hidden_bias],
            [(slot_rows, f32), (slot_rows, bf16)],
            before,
        )
        hidden.append(wide)
        active.append(narrow)
        before = (narrow,)
    second, down_pieces = [], []
    for s in over:
        terms.append(terms_matmul(active[s], down_full, spans, before))
        sums.append(tensor.scatter(terms[s]))
        second.append(second_norm(sums[s][0], first[s][1], cotangent[s], row_vectors, (terms[s][0][0],)))
        down_pieces.append(tensor.gather(second[s][2]))
        before = near(down_pieces[s])

    def give_back(rows):
        return lax.all_to_all(
            rows.reshape(groups, arrival_rows, model_width), "dp", split_axis=0, concat_axis=0, tiled=True
        )

    returned_rows = [give_back(s[0]) for s in second]

    hidden_grad, up_sums, terms, first_sums = [], [], [], []

    def through_gelu(product, wide):
        grad = (product * gelu_slope(wide)).astype(bf16)
        return grad, jnp.sum(grad.astype(f32), axis=0, keepdims=True)

    first_back = []

    def back_to_hidden(s, later, held):
        grad, total = rows_matmul(
            down_pieces[s], down_full, hidden_width, through_gelu, [hidden[s]], [(slot_rows, bf16), (1, f32)], later
        )
        hidden_grad.append(grad)
        up_sums.append(total)
        terms.append(terms_matmul(grad, up_full, spans, held))
        first_sums.append(tensor.scatter(terms[s]))

    def back_to_first(s, later):
        first_back.append(
            first_norm_back(
                first_sums[s][0], second[s][1], first[s][1], first[s][2], row_vectors, later
            )
        )
        return tensor.gather(first_back[s][1])

    back_to_hidden(0, (), (returned_rows[0],))
    grad_pieces = [back_to_first(0, (terms[0][0][0],))]
    down_terms = weight_grad(down_pieces, active, (first_back[0][0],))
    down_terms = touched(down_terms, *near(grad_pieces[0]))
    down_sum = group.scatter(down_terms)
    back_to_hidden(1, (down_terms,), (returned_rows[1],))
    last_first = (terms[1][0][0],)

    def attention_in(s, later):
        return rows_matmul(
            grad_pieces[s],
            mid_weight,
            head_width,
            lambda product: (product.astype(bf16),),
            [],
            rows_bf16,
            later,
        )[0]

    def attention_back(s, mixed_grad, later):
        return attend_back(qkv[s], biases[s], mixed[s], mixed_grad, logs[s], 2, later)

    mixed_grad = [attention_in(0, last_first)]
    backs = [attention_back(0, mixed_grad[0], first_sums[1][1])]
    terms = [terms_matmul(backs[0][0], qkv_weight, spans)]
    sums = [tensor.scatter(terms[0])]
    grad_pieces.append(back_to_first(1, (terms[0][0][0],)))
    up_terms = weight_grad(first_pieces, hidden_grad, (first_back[1][0],))
    up_terms = touched(up_terms, *near(grad_pieces[1]), *sums[0][1])
    up_sum = group.scatter(up_terms)
    row_grads = jnp.concatenate(
        [sum(f[2] for f in first_back)[:3], sum(s[3] for s in second)[:3]], axis=0
    ).reshape(-1, 128)
    mixed_grad.append(attention_in(1, (up_terms,)))
    mid_terms = weight_grad(grad_pieces, mixed, (mixed_grad[1],))
    row_grads, spread = add_up(row_grads, "tensor", (mixed_grad[1],))
    small = jnp.concatenate([row_grads, sum(up_sums).reshape(-1, 128)], axis=0)
    small, stages = add_up(small, "dp")
    mid_sum = group.scatter(mid_terms)
    backs.append(attention_back(1, mixed_grad[1], (mid_terms, spread[0])))
    token_grad = [input_grad(sums[0][0], first_back[0][0], (backs[1][0],))]
    returned_grads = [give_back(token_grad[0])]
    qkv_grad = [b[0] for b in backs]
    bias_terms = sum(b[1] for b in backs).reshape(1, -1)
    qkv_sum, bias_sum, qkv_terms, *qkv_stage = group.weight_scatter(
        token_pieces, qkv_grad, bias_terms, (token_grad[0], down_sum, spread[1])
    )
    terms.append(terms_matmul(qkv_grad[-1], qkv_weight, spans, (qkv_terms, stages[0], *returned_grads)))
    last_grad = input_grad(
        tensor.scatter(terms[-1])[0], first_back[-1][0], (*qkv_stage[1], up_sum, stages[2])
    )
    returned_grads.append(give_back(last_grad))

    places = slot_dealing.T.reshape(-1)
    inverse = jnp.zeros(places.shape, jnp.int32).at[places].set(
        jnp.arange(places.shape[0], dtype=jnp.int32)
    )
    result = jnp.take(jnp.concatenate(returned_rows, axis=0), inverse, axis=0, mode="clip")
    inverse = inverse + nothing(mid_sum).astype(jnp.int32)
    token_gradient = jnp.take(jnp.concatenate(returned_grads, axis=0), inverse, axis=0, mode="clip")

    row_shares = lax.dynamic_slice_in_dim(
        small.reshape(-1)[: 6 * model_width].reshape(6, splits * groups, piece),
        tensor.me * groups + group.me,
        1,
        axis=1,
    )[:, 0]

    def share(values):
        return lax.dynamic_index_in_dim(values.reshape(groups, -1), group.me, 0, False)

    bias_sum = bias_sum.reshape(2, 3, half)
    query_share = share(bias_sum[:, 0])
    value_share = share(bias_sum[:, 2])
    up_share = share(small.reshape(-1)[6 * model_width :])

    qkv_sum = qkv_sum.reshape(-1, 2, 3, half)
    return (
        result,
        token_gradient,
        qkv_sum[:, :, 0].reshape(-1, head_width),
        qkv_sum[:, :, 1].reshape(-1, head_width),
        qkv_sum[:, :, 2].reshape(-1, head_width),
        mid_sum.T,
        up_sum,
        down_sum.T,
        query_share,
        value_share,
        row_shares[0],
        row_shares[1],
        row_shares[2],
        up_share,
        row_shares[3],
        row_shares[4],
        row_shares[5],
    )


def solution(mesh):
    matrix = P("dp", "tensor")
    flipped = P("tensor", "dp")
    vector = P(("tensor", "dp"))
    arrival = P(None, ("tensor", "dp"), None)
    return jax.shard_map(
        local,
        mesh=mesh,
        in_specs=(arrival, P("dp", "tensor", None), P(), P())
        + (matrix, matrix, matrix, flipped, matrix, flipped)
        + (vector,) * 9,
        out_specs=(arrival, arrival) + (matrix, matrix, matrix, flipped, matrix, flipped) + (vector,) * 9,
        check_vma=False,
    )
```

```python
import functools
import math

import jax
import jax.numpy as jnp
from jax import lax
from jax.experimental import pallas as pl
from jax.experimental.pallas import tpu as pltpu
from jax.sharding import PartitionSpec as P

HEAD = 128
norm_epsilon = 1e-05
masked_score = -1e30
log2_e = math.log2(math.e)
head_scale = 1.0 / math.sqrt(HEAD)
gelu_root = math.sqrt(2.0 / math.pi)
bf16 = jnp.bfloat16
f32 = jnp.float32
MIB = 1024 * 1024
cost = 2.0
TALL = ((1,), (0,))
FLAT = ((1,), (1,))
DEEP = ((0,), (0,))


def dot(left, right, contract):
    return lax.dot_general(left, right, (contract, ((), ())), preferred_element_type=f32)


def shape(dims, dtype):
    return jax.ShapeDtypeStruct(tuple(dims), dtype)


def whole(array):
    return pl.BlockSpec(array.shape, lambda *i: (0,) * array.ndim)


def launch(body, grid, ins, in_specs, outs, out_specs, later=(), scratch=(), flops=0, nbytes=0, exps=0):
    later = tuple(later)
    count, skip = len(ins), len(later)

    def run(*refs):
        body(refs[:count], refs[count + skip :])

    return pl.pallas_call(
        run,
        grid=grid,
        in_specs=list(in_specs) + [pl.BlockSpec(memory_space=pl.ANY)] * skip,
        out_specs=list(out_specs),
        out_shape=list(outs),
        scratch_shapes=list(scratch),
        compiler_params=pltpu.CompilerParams(vmem_limit_bytes=60 * MIB),
        cost_estimate=pl.CostEstimate(
            flops=int(cost * flops), bytes_accessed=int(cost * nbytes), transcendentals=int(cost * exps)
        ),
    )(*ins, *later)


def attend(qkv, bias, halves, later=()):
    rows, columns = qkv.shape
    group = columns // halves
    heads = group // (3 * HEAD)
    width = heads * HEAD
    block = min(256, rows)

    def body(ins, outs):
        bias_ref, qkv_ref = ins
        mixed_ref, log_ref = outs
        shift = bias_ref[...]
        for head in range(heads):
            low = head * HEAD
            keys = qkv_ref[:, width + low : width + low + HEAD]
            values = qkv_ref[:, 2 * width + low : 2 * width + low + HEAD]
            for first in range(0, rows, block):
                part = slice(first, first + block)
                queries = qkv_ref[part, low : low + HEAD]
                scores = dot(keys, queries, FLAT) * (head_scale * log2_e) + shift
                peak = jnp.max(scores, axis=0, keepdims=True)
                weight = jnp.exp2(scores - peak)
                total = jnp.sum(weight, axis=0, keepdims=True)
                mixed = dot(values, weight.astype(bf16), DEEP) * (1.0 / total)
                mixed_ref[part, low : low + HEAD] = mixed.T.astype(bf16)
                log_ref[0, head : head + 1, part] = peak + jnp.log2(total)

    return launch(
        body,
        (halves,),
        [bias, qkv],
        [pl.BlockSpec((rows, 1), lambda i: (0, 0)), pl.BlockSpec((rows, group), lambda i: (0, i))],
        [shape((rows, halves * width), bf16), shape((halves, heads, rows), f32)],
        [pl.BlockSpec((rows, width), lambda i: (0, i)), pl.BlockSpec((1, heads, rows), lambda i: (i, 0, 0))],
        later,
        flops=4 * halves * heads * rows * rows * HEAD * 4,
        nbytes=rows * columns * 3,
        exps=halves * heads * rows * rows,
    )


def attend_back(qkv, bias, mixed, grads, logs, halves, later=()):
    rows, columns = qkv.shape
    group = columns // halves
    heads = group // (3 * HEAD)
    width = heads * HEAD
    block = min(256, rows)

    def body(ins, outs):
        bias_ref, qkv_ref, mixed_ref, grad_ref, log_ref = ins
        out_ref, sum_ref = outs
        shift = bias_ref[...]
        for head in range(heads):
            low = head * HEAD
            keys = qkv_ref[:, width + low : width + low + HEAD]
            values = qkv_ref[:, 2 * width + low : 2 * width + low + HEAD]
            key_total = jnp.zeros((rows, HEAD), f32)
            value_total = jnp.zeros((rows, HEAD), f32)
            query_sum = jnp.zeros((1, HEAD), f32)
            for first in range(0, rows, block):
                part = slice(first, first + block)
                queries = qkv_ref[part, low : low + HEAD]
                grad = grad_ref[part, low : low + HEAD]
                mix = mixed_ref[part, low : low + HEAD]
                centre = jnp.sum((grad.astype(f32) * mix.astype(f32)).T, axis=0, keepdims=True)
                scores = dot(keys, queries, FLAT) * (head_scale * log2_e) + shift
                weight = jnp.exp2(scores - log_ref[0, head : head + 1, part])
                weight_grad = dot(values, grad, FLAT)
                score_grad = (weight * (weight_grad - centre)).astype(bf16)
                value_total = value_total + dot(weight.astype(bf16), grad, TALL)
                key_total = key_total + dot(score_grad, queries, TALL)
                query_grad = (dot(keys, score_grad, DEEP) * head_scale).T.astype(bf16)
                out_ref[part, low : low + HEAD] = query_grad
                query_sum = query_sum + jnp.sum(query_grad.astype(f32), axis=0, keepdims=True)
            value_total = value_total.astype(bf16)
            out_ref[:, width + low : width + low + HEAD] = (key_total * head_scale).astype(bf16)
            out_ref[:, 2 * width + low : 2 * width + low + HEAD] = value_total
            sum_ref[0, :, low : low + HEAD] = query_sum
            sum_ref[0, :, width + low : width + low + HEAD] = jnp.zeros_like(query_sum)
            sum_ref[0, :, 2 * width + low : 2 * width + low + HEAD] = jnp.sum(
                value_total.astype(f32), axis=0, keepdims=True
            )

    columns_of = lambda n: pl.BlockSpec((rows, n), lambda i: (0, i))
    return launch(
        body,
        (halves,),
        [bias, qkv, mixed, grads, logs],
        [
            pl.BlockSpec((rows, 1), lambda i: (0, 0)),
            columns_of(group),
            columns_of(width),
            columns_of(width),
            pl.BlockSpec((1, heads, rows), lambda i: (i, 0, 0)),
        ],
        [shape((rows, columns), bf16), shape((halves, 1, group), f32)],
        [columns_of(group), pl.BlockSpec((1, 1, group), lambda i: (i, 0, 0))],
        later,
        flops=10 * halves * heads * rows * rows * HEAD * 4,
        nbytes=rows * columns * 6,
        exps=halves * heads * rows * rows,
    )


def tile_of(width, most):
    tile = min(width, most)
    while width % tile:
        tile //= 2
    return tile


def rows_matmul(pieces, weight, width, finish, extras, kinds, later=(), most=512):
    rows = sum(p.shape[0] for p in pieces)
    inner = weight.shape[0]
    tile = tile_of(width, most)

    def body(ins, refs):
        piece_refs, weight_ref = ins[: len(pieces)], ins[len(pieces)]
        extra_refs = ins[len(pieces) + 1 :]
        out_refs, gathered = refs[: len(kinds)], refs[len(kinds)]

        @pl.when(pl.program_id(0) == 0)
        def _():
            first = 0
            for ref in piece_refs:
                gathered[first : first + ref.shape[0], :] = ref[...]
                first += ref.shape[0]

        product = dot(gathered[...], weight_ref[...], TALL)
        for ref, value in zip(out_refs, finish(product, *[r[...] for r in extra_refs])):
            ref[...] = value

    def along(n):
        return pl.BlockSpec((n, tile), lambda j: (0, j))

    return launch(
        body,
        (width // tile,),
        [*pieces, weight, *extras],
        [whole(p) for p in pieces] + [along(inner)] + [along(e.shape[0]) for e in extras],
        [shape((n, width), dtype) for n, dtype in kinds],
        [along(n) for n, _ in kinds],
        later,
        scratch=[pltpu.VMEM((rows, inner), bf16)],
        flops=2 * rows * inner * width,
        nbytes=2 * (rows * inner + inner * width) + sum(4 * n * width for n, _ in kinds),
    )


def terms_matmul(left, weight, spans, later=(), most=512):
    rows, inner = left.shape
    outer = weight.shape[0]
    tile = tile_of(outer // 2, most)
    steps = outer // 2 // tile

    def body(ins, outs):
        left_ref, weight_ref = ins
        step = pl.program_id(0)
        product = dot(left_ref[...], weight_ref[...], FLAT).astype(bf16)
        groups = outs[: len(spans[0])], outs[len(spans[0]) :]
        for side in range(2):

            @pl.when((step < steps) if side == 0 else (step >= steps))
            def _():
                for ref, (low, high) in zip(groups[side], spans[side]):
                    ref[...] = product[low:high]

    places = [
        lambda j: (0, jnp.minimum(j, steps - 1)),
        lambda j: (0, jnp.maximum(j - steps, 0)),
    ]
    sizes = [(side, high - low) for side in range(2) for low, high in spans[side]]
    outs = launch(
        body,
        (2 * steps,),
        [left, weight],
        [whole(left), pl.BlockSpec((tile, inner), lambda j: (j, 0))],
        [shape((n, outer // 2), bf16) for _, n in sizes],
        [pl.BlockSpec((n, tile), places[side]) for side, n in sizes],
        later,
        flops=2 * rows * inner * outer,
        nbytes=2 * (rows * inner + outer * inner + rows * outer),
    )
    return outs[: len(spans[0])], outs[len(spans[0]) :]


def weight_grad(lefts, rights, later=(), core=None, most=256, row=None):
    flat = [p for pieces in lefts for p in pieces]
    outer = flat[0].shape[1]
    rows, columns = rights[0].shape
    tile = tile_of(outer, most)
    slots = len(rights)
    scalars = [] if core is None else [core.reshape(1)]
    rows_added = [] if core is None else [row]
    spare = 0 if core is None else 16

    def body(ins, refs):
        piece_refs, right_refs = ins[: len(flat)], ins[len(flat) :]
        gathered = refs[-1]
        first = 0
        for ref in piece_refs:
            gathered[first : first + ref.shape[0], :] = ref[...]
            first += ref.shape[0]
        total = None
        for slot in range(slots):
            term = dot(gathered[slot * rows : (slot + 1) * rows, :], right_refs[slot][...], DEEP)
            total = term if total is None else total + term
        refs[0][...] = total.astype(bf16)

    def body_apart(ins, refs):
        parity = lax.rem(pl.program_id(0), 2)
        total_ref = refs[2]
        body(ins[2:], (total_ref, refs[3]))
        added = jnp.broadcast_to(ins[1][...].astype(bf16), (spare, columns))

        def put(ref):
            ref[:tile, :] = total_ref[...]
            ref[tile:, :] = added

        @pl.when(parity == ins[0][0])
        def _():
            put(refs[0])

        @pl.when(parity != ins[0][0])
        def _():
            put(refs[1])

    outs = [shape((outer, columns), bf16)] if core is None else [shape((outer // tile // 2 * (tile + spare), columns), bf16)] * 2
    where = (lambda j: (j, 0)) if core is None else (lambda j: (j // 2, 0))
    result = launch(
        body if core is None else body_apart,
        (outer // tile,),
        [*scalars, *rows_added, *flat, *rights],
        [pl.BlockSpec(memory_space=pltpu.SMEM)] * len(scalars)
        + [whole(r) for r in rows_added]
        + [pl.BlockSpec((p.shape[0], tile), lambda j: (0, j)) for p in flat]
        + [whole(r) for r in rights],
        outs,
        [pl.BlockSpec((tile + spare, columns), where)] * len(outs),
        later,
        scratch=([] if core is None else [pltpu.VMEM((tile, columns), bf16)])
        + [pltpu.VMEM((slots * rows, tile), bf16)],
        flops=2 * slots * rows * outer * columns,
        nbytes=2 * (slots * rows * (outer + columns) + outer * columns),
    )
    return result[0] if core is None else result


def norm_tiles(body, rows, width, left, right, tiled, vectors, outs, sums, later):
    steps = 4
    tile = rows // steps
    n_left, n_right, n_tiled = len(left), len(right), len(tiled)

    def run(ins, refs):
        step = pl.program_id(0)
        left_refs = ins[:n_left]
        right_refs = ins[n_left : n_left + n_right]
        tiled_refs = ins[n_left + n_right : n_left + n_right + n_tiled]
        vector_ref = ins[-1] if vectors is not None else None

        def added(group):
            total = group[0][...].astype(f32)
            for ref in group[1:]:
                total = total + ref[...].astype(f32)
            return total

        both = jnp.concatenate([added(left_refs), added(right_refs)], axis=1)
        values, totals = body(both, [r[...] for r in tiled_refs], vector_ref)
        for ref, value in zip(refs, values):
            ref[...] = value.astype(ref.dtype)
        if sums:
            sum_ref = refs[-1]

            @pl.when(step == 0)
            def _():
                sum_ref[...] = jnp.zeros_like(sum_ref)

            for i, value in enumerate(totals):
                sum_ref[i : i + 1, :] += jnp.sum(value, axis=0, keepdims=True)

    def of(columns):
        return pl.BlockSpec((tile, columns), lambda i: (i, 0))

    def start(array, first):
        return pl.BlockSpec((tile, array.shape[1]), lambda i: (i + first // tile, 0))

    ins = [a for a, _ in (*left, *right)] + [*tiled] + ([vectors] if vectors is not None else [])
    return launch(
        run,
        (steps,),
        ins,
        [start(*a) for a in (*left, *right)]
        + [of(a.shape[1]) for a in tiled]
        + ([whole(vectors)] if vectors is not None else []),
        [shape((rows, c), dtype) for c, dtype in outs]
        + ([shape((8, width), f32)] if sums else []),
        [of(c) for c, _ in outs]
        + ([pl.BlockSpec((8, width), lambda i: (0, 0))] if sums else []),
        later,
        flops=rows * width * 20,
        nbytes=rows * width * 16,
    )


def normed(values):
    centred = values - jnp.mean(values, axis=-1, keepdims=True)
    inverse = lax.rsqrt(jnp.mean(centred * centred, axis=-1, keepdims=True) + norm_epsilon)
    return centred * inverse, inverse


def norm_back(grads, unit, inverse, gain):
    scaled = grads * gain
    return inverse * (
        scaled
        - jnp.mean(scaled, axis=-1, keepdims=True)
        - unit * jnp.mean(scaled * unit, axis=-1, keepdims=True)
    )


def first_norm(terms, rows, vectors, later=()):
    def body(both, tiled, v):
        unit, inverse = normed(tiled[0].astype(f32) + (both + v[0:1, :]))
        return [unit * v[1:2, :] + v[2:3, :], unit, inverse], []

    n, width = rows.shape
    kinds = [(width, bf16), (width, f32), (1, f32)]
    return norm_tiles(body, n, width, *terms, [rows], vectors, kinds, False, later)


def second_norm(terms, unit, cotangent, vectors, later=()):
    def body(both, tiled, v):
        first, grads = tiled[0] * v[1:2, :] + v[2:3, :], tiled[1].astype(f32)
        unit_two, inverse = normed(first + (both + v[3:4, :]))
        back = norm_back(grads, unit_two, inverse, v[4:5, :])
        return [unit_two * v[4:5, :] + v[5:6, :], back, back], [back, grads * unit_two, grads]

    n, width = unit.shape
    kinds = [(width, bf16), (width, f32), (width, bf16)]
    return norm_tiles(body, n, width, *terms, [unit, cotangent], vectors, kinds, True, later)


def first_norm_back(terms, back_two, unit, inverse, vectors, later=()):
    def body(both, tiled, v):
        grads = tiled[0] + both
        back = norm_back(grads, tiled[1], tiled[2], v[1:2, :])
        return [back, back], [back, grads * tiled[1], grads]

    n, width = unit.shape
    kinds = [(width, f32), (width, bf16)]
    return norm_tiles(body, n, width, *terms, [back_two, unit, inverse], vectors, kinds, True, later)


def input_grad(terms, back, later=()):
    def body(both, tiled, v):
        return [tiled[0] + both], []

    n, width = back.shape
    return norm_tiles(body, n, width, *terms, [back], None, [(width, bf16)], False, later)[0]


class TensorAxis:
    def __init__(self):
        self.size = lax.axis_size("tensor")
        self.me = lax.axis_index("tensor")
        self.square = self.size == 4
        if self.square:
            self.origins = self.me ^ jnp.array([0, 1, 3, 2], jnp.int32)
        else:
            self.origins = jnp.arange(self.size, dtype=jnp.int32)

    def swap(self, array, bit):
        return lax.ppermute(array, "tensor", [(i, i ^ bit) for i in range(self.size)])

    def gather(self, block):
        if not self.square:
            return [lax.all_gather(block, "tensor", axis=0, tiled=True)]
        half = block.shape[0] // 2
        along_x, along_y = self.swap(block, 1), self.swap(block, 2)
        far_top, far_bottom = self.swap(along_y[:half], 1), self.swap(along_x[half:], 2)
        return [block, along_x, far_top, far_bottom, along_y]

    def spans(self, rows):
        if not self.square:
            return [(0, rows)], [(0, rows)]
        r = rows // 4
        return [(r, 3 * r), (3 * r, 4 * r), (0, r)], [(2 * r, 4 * r), (r, 2 * r), (0, r)]

    def line_up(self, block):
        if not self.square:
            return lax.all_gather(block, "tensor", axis=1, tiled=True)
        width = block.shape[1]
        full = jnp.zeros((block.shape[0], 4 * width), block.dtype)
        for bits in range(4):
            piece = self.swap(block, bits) if bits else block
            full = lax.dynamic_update_slice(full, piece, (0, (self.me ^ bits) * width))
        return full

    def scatter(self, terms):
        left, right = terms
        if not self.square:
            full = jnp.concatenate([left[0], right[0]], axis=1)
            mine = lax.psum_scatter(full, "tensor", scatter_dimension=0, tiled=True)
            half = mine.shape[1] // 2
            return ([(mine[:, :half], 0)], [(mine[:, half:], 0)]), (), ()
        rows = left[1].shape[0]
        from_x, from_y = self.swap(left[0], 1), self.swap(right[0], 2)
        left_far = self.swap((left[1].astype(f32) + from_x[rows:].astype(f32)).astype(bf16), 2)
        right_far = self.swap((right[1].astype(f32) + from_y[:rows].astype(f32)).astype(bf16), 1)
        left = [(left[2], 0), (from_x, 0), (left_far, 0)]
        right = [(right[2], 0), (from_y, rows), (right_far, 0)]
        return (left, right), (from_x, from_y), (left_far, right_far)


class GroupAxis:
    def __init__(self):
        self.size = lax.axis_size("dp")
        self.me = lax.axis_index("dp")
        self.line = self.size == 8
        self.z = self.me // 2
        n = self.size
        self.next = [(i, (i + 2) % n) for i in range(n)]
        self.last = [(i, (i - 2) % n) for i in range(n)]

    def send(self, array, pairs):
        return lax.ppermute(array, "dp", pairs)

    def gather(self, shard):
        return lax.all_gather(shard, "dp", axis=0, tiled=True)

    def scatter(self, terms):
        return lax.psum_scatter(terms, "dp", scatter_dimension=0, tiled=True).astype(f32)

    def weight_scatter(self, lefts, rights, row, later):
        if not self.line:
            terms = weight_grad(lefts, rights, later)
            return self.scatter(terms), lax.psum(row, "dp")[0], terms, (), (), ()
        block = lefts[0][0].shape[1] // self.size
        mine, theirs = weight_grad(lefts, rights, later, self.me % 2, block, row)
        got = self.send(theirs, [(i, i ^ 1) for i in range(self.size)])
        rows = mine.shape[0] // 4

        def toward(step):
            first = ((self.z + step) % 4) * rows
            parts = [lax.dynamic_slice_in_dim(a, first, rows).astype(f32) for a in (mine, got)]
            return parts[0] + parts[1]

        far = toward(2).astype(bf16)
        up = self.send(far, [(0, 2), (1, 3), (2, 4), (3, 5)])
        down = self.send(far, [(6, 4), (7, 5), (4, 2), (5, 3)])
        ahead = (toward(1) + up.astype(f32)).astype(bf16)
        behind = (toward(3) + down.astype(f32)).astype(bf16)
        ahead, behind = self.send(ahead, self.next), self.send(behind, self.last)
        total = toward(0) + ahead.astype(f32) + behind.astype(f32)
        return total[:block], total[block], mine, (got,), (up, down), (ahead, behind)


def nothing(*arrays):
    return sum(a[(0,) * a.ndim].astype(f32) * 0.0 for a in arrays)


def touched(array, *arrays):
    if not arrays:
        return array
    corner = array[:16, :128]
    return lax.dynamic_update_slice(array, corner + nothing(*arrays).astype(array.dtype), (0, 0))


def add_up(array, axis, earlier=()):
    size = lax.axis_size(axis)
    bit, stages = 1, []
    while bit < size:
        if len(stages) < len(earlier) and earlier[len(stages)] is not None:
            array = array + nothing(earlier[len(stages)])
        stages.append(lax.ppermute(array, axis, [(i, i ^ bit) for i in range(size)]))
        array = array + stages[-1]
        bit *= 2
    return array, stages


def gelu(hidden):
    return 0.5 * hidden * (1.0 + jnp.tanh(gelu_root * (hidden + 0.044715 * hidden * hidden * hidden)))


def gelu_slope(hidden):
    square = hidden * hidden
    bend = jnp.tanh(gelu_root * (hidden + 0.044715 * hidden * square))
    return 0.5 * (1.0 + bend) + 0.5 * hidden * (1.0 - bend * bend) * gelu_root * (
        1.0 + 3 * 0.044715 * square
    )


def local(
    tokens,
    cotangent,
    lengths,
    dealing,
    query_weight,
    key_weight,
    value_weight,
    output_weight,
    up_weight,
    down_weight,
    query_bias,
    value_bias,
    output_bias,
    attention_gain,
    attention_shift,
    up_bias,
    down_bias,
    feedforward_gain,
    feedforward_shift,
):
    tensor, group = TensorAxis(), GroupAxis()
    groups, splits = group.size, tensor.size
    slots, own_rows, model_width = cotangent.shape
    over = range(slots)
    slot_rows = own_rows * splits
    arrival_rows = tokens.shape[1]
    head_width = query_weight.shape[1]
    half = head_width // 2
    piece = query_bias.shape[0]
    hidden_width = up_weight.shape[1]
    spans = tensor.spans(slot_rows)

    slot_dealing = dealing.reshape(groups, slots)
    sent = jnp.take(tokens, dealing, axis=0, mode="clip").reshape(groups, slots, arrival_rows, model_width)
    came = lax.all_to_all(sent, "dp", split_axis=0, concat_axis=0, tiled=True)
    zero = came[0, 0, 0, 0] * 0.0
    token_pieces, arrived = [], []
    for s in over:
        rows = came[:, s].reshape(own_rows, model_width)
        if s > 0 and tensor.square:
            rows = rows + token_pieces[0][1][0, 0] * 0.0
        arrived.append(rows)
        token_pieces.append(tensor.gather(rows))

    head_piece = jnp.concatenate([query_bias, value_bias, up_bias]).astype(bf16)
    row_piece = jnp.concatenate(
        [output_bias, attention_gain, attention_shift, down_bias, feedforward_gain, feedforward_shift]
    ).astype(bf16)
    vector = jnp.concatenate([head_piece, row_piece])
    shard_rows, spare = query_weight.shape[0], 128
    padded = jnp.zeros((shard_rows * spare,), bf16).at[: vector.shape[0]].set(vector) + zero
    three = [w.astype(bf16) for w in (query_weight, key_weight, value_weight)]
    qkv_weight = group.gather(
        jnp.concatenate(
            [w[:, :half] for w in three] + [w[:, half:] for w in three] + [padded.reshape(shard_rows, spare)],
            axis=1,
        )
    )
    mid_weight = group.gather(touched(output_weight.astype(bf16).T, came))
    up_full = group.gather(touched(up_weight.astype(bf16), came))
    down_full = group.gather(touched(down_weight.astype(bf16).T, came))
    used = -(-vector.shape[0] // spare)
    table = qkv_weight[:, 3 * head_width :].reshape(groups, shard_rows, spare)[:, :used]
    table = table.reshape(groups, -1)[:, : vector.shape[0]]
    head_vectors = table.astype(f32)
    row_table = table[:, head_piece.shape[0] :].reshape(groups, 6, piece)
    row_table = jnp.moveaxis(row_table, 1, 0).reshape(6, groups * piece)
    row_vectors = tensor.line_up(row_table).astype(f32)
    query_bias_here = head_vectors[:, :piece].reshape(-1)
    value_bias_here = head_vectors[:, piece : 2 * piece].reshape(-1)
    hidden_bias = head_vectors[:, 2 * piece : head_piece.shape[0]].reshape(1, -1)
    row_vectors = jnp.concatenate([row_vectors, jnp.zeros((2, model_width), f32)], axis=0)
    blank = jnp.zeros((half,), f32)
    qkv_bias = jnp.concatenate(
        [query_bias_here[:half], blank, value_bias_here[:half]]
        + [query_bias_here[half:], blank, value_bias_here[half:]]
    )[None]

    positions = (tensor.origins[:, None] * own_rows + jnp.arange(own_rows)[None, :]).reshape(-1)
    slot_lengths = lax.dynamic_slice_in_dim(jnp.take(lengths, dealing, axis=0), group.me * slots, slots)
    biases = [
        jnp.where(positions < slot_lengths[s], 0.0, masked_score).astype(f32)[:, None] for s in over
    ]

    def near(pieces):
        return tuple(pieces[1:2] + pieces[4:])

    rows_bf16 = [(slot_rows, bf16)]
    qkv, mixed, logs, terms, sums = [], [], [], [], []
    before = near(token_pieces[1])
    for s in over:
        qkv += rows_matmul(
            token_pieces[s],
            qkv_weight,
            3 * head_width,
            lambda product, bias: ((product + bias).astype(bf16),),
            [qkv_bias],
            rows_bf16,
            before,
            most=256,
        )
        mix, log = attend(qkv[s], biases[s], 2)
        mixed.append(mix)
        logs.append(log)
        terms.append(terms_matmul(mix, mid_weight, spans, sums[-1][2] if sums else (row_vectors,)))
        sums.append(tensor.scatter(terms[s]))
        before = (terms[s][0][0],)
    first, first_pieces = [], []
    for s in over:
        first.append(first_norm(sums[s][0], arrived[s], row_vectors, before))
        first_pieces.append(tensor.gather(first[s][0]))
        before = tuple(first_pieces[s][1:])
    hidden, active, terms, sums = [], [], [], []
    before = ()
    for s in over:
        wide, narrow = rows_matmul(
            first_pieces[s],
            up_full,
            hidden_width,
            lambda product, bias: (product + bias, gelu(product + bias).astype(bf16)),
            [hidden_bias],
            [(slot_rows, f32), (slot_rows, bf16)],
            before,
        )
        hidden.append(wide)
        active.append(narrow)
        before = (narrow,)
    for s in over:
        terms.append(terms_matmul(active[s], down_full, spans, before))
        sums.append(tensor.scatter(terms[s]))
        before = (terms[s][0][0],)
    second, down_pieces = [], []
    for s in over:
        second.append(second_norm(sums[s][0], first[s][1], cotangent[s], row_vectors, before))
        down_pieces.append(tensor.gather(second[s][2]))
        before = near(down_pieces[s])

    def give_back(rows):
        return lax.all_to_all(
            rows.reshape(groups, arrival_rows, model_width), "dp", split_axis=0, concat_axis=0, tiled=True
        )

    returned_rows = [give_back(s[0]) for s in second]

    hidden_grad, up_sums, terms, first_sums = [], [], [], []
    before = ()

    def through_gelu(product, wide):
        grad = (product * gelu_slope(wide)).astype(bf16)
        return grad, jnp.sum(grad.astype(f32), axis=0, keepdims=True)

    for s in over:
        grad, total = rows_matmul(
            down_pieces[s],
            down_full,
            hidden_width,
            through_gelu,
            [hidden[s]],
            [(slot_rows, bf16), (1, f32)],
            before,
        )
        hidden_grad.append(grad)
        up_sums.append(total)
        if s == 0:
            terms.append(terms_matmul(grad, up_full, spans, (*near(down_pieces[1]), returned_rows[0])))
            first_sums.append(tensor.scatter(terms[s]))
            before = (terms[s][0][0],)
    first_back = []

    def back_to_first(s, later):
        first_back.append(
            first_norm_back(
                first_sums[s][0], second[s][1], first[s][1], first[s][2], row_vectors, later
            )
        )
        return tensor.gather(first_back[s][1])

    down_terms = weight_grad(down_pieces, active, (hidden_grad[1], *first_sums[0][1], *returned_rows))
    down_terms = touched(down_terms, *first_sums[0][2])
    down_sum = group.scatter(down_terms)
    grad_pieces = [back_to_first(0, (down_terms,))]
    terms.append(terms_matmul(hidden_grad[1], up_full, spans, (first_back[0][0],)))
    first_sums.append(tensor.scatter(terms[1]))
    up_terms = weight_grad(first_pieces, hidden_grad, (terms[1][0][0],))
    up_terms = touched(up_terms, *first_sums[1][1], *near(grad_pieces[0]))
    up_sum = group.scatter(up_terms)
    grad_pieces.append(back_to_first(1, (up_terms,)))

    def attention_in(s, later):
        return rows_matmul(
            grad_pieces[s],
            mid_weight,
            head_width,
            lambda product: (product.astype(bf16),),
            [],
            rows_bf16,
            later,
        )[0]

    def attention_back(s, mixed_grad, later):
        return attend_back(qkv[s], biases[s], mixed[s], mixed_grad, logs[s], 2, later)

    mixed_grad = [attention_in(0, (up_terms,))]
    row_grads = jnp.concatenate(
        [sum(f[2] for f in first_back)[:3], sum(s[3] for s in second)[:3]], axis=0
    ).reshape(-1, 128)
    row_grads, stages = add_up(row_grads, "tensor", (mixed_grad[0],))
    stages = [(stage,) for stage in stages] + [(), ()]
    backs = [attention_back(0, mixed_grad[0], ())]
    terms = [terms_matmul(backs[0][0], qkv_weight, spans, (*stages[0], *near(grad_pieces[1])))]
    sums = [tensor.scatter(terms[0])]
    mixed_grad.append(attention_in(1, (terms[0][0][0], *stages[1])))
    mid_terms = weight_grad(grad_pieces, mixed, (mixed_grad[1],))
    small = jnp.concatenate([row_grads, sum(up_sums).reshape(-1, 128)], axis=0)
    small, stages = add_up(small, "dp", (mixed_grad[1], mid_terms, None))
    mid_sum = group.scatter(touched(mid_terms, *sums[0][1]))
    backs.append(attention_back(1, mixed_grad[1], (mid_terms, *sums[0][1], stages[0])))
    token_grad = [input_grad(sums[0][0], first_back[0][0], (backs[1][0],))]
    returned_grads = [give_back(token_grad[0])]
    qkv_grad = [b[0] for b in backs]
    bias_terms = sum(b[1] for b in backs).reshape(1, -1)
    qkv_sum, bias_sum, qkv_terms, *qkv_stage = group.weight_scatter(
        token_pieces, qkv_grad, bias_terms, (token_grad[0], down_sum, stages[1])
    )
    terms.append(terms_matmul(qkv_grad[-1], qkv_weight, spans, (qkv_terms, *returned_grads)))
    last_grad = input_grad(
        tensor.scatter(terms[-1])[0], first_back[-1][0], (*qkv_stage[1], up_sum, stages[2])
    )
    returned_grads.append(give_back(last_grad))

    places = slot_dealing.T.reshape(-1)
    inverse = jnp.zeros(places.shape, jnp.int32).at[places].set(
        jnp.arange(places.shape[0], dtype=jnp.int32)
    )
    result = jnp.take(jnp.concatenate(returned_rows, axis=0), inverse, axis=0, mode="clip")
    inverse = inverse + nothing(mid_sum).astype(jnp.int32)
    token_gradient = jnp.take(jnp.concatenate(returned_grads, axis=0), inverse, axis=0, mode="clip")

    row_shares = lax.dynamic_slice_in_dim(
        small.reshape(-1)[: 6 * model_width].reshape(6, splits * groups, piece),
        tensor.me * groups + group.me,
        1,
        axis=1,
    )[:, 0]

    def share(values):
        return lax.dynamic_index_in_dim(values.reshape(groups, -1), group.me, 0, False)

    bias_sum = bias_sum.reshape(2, 3, half)
    query_share = share(bias_sum[:, 0])
    value_share = share(bias_sum[:, 2])
    up_share = share(small.reshape(-1)[6 * model_width :])

    qkv_sum = qkv_sum.reshape(-1, 2, 3, half)
    return (
        result,
        token_gradient,
        qkv_sum[:, :, 0].reshape(-1, head_width),
        qkv_sum[:, :, 1].reshape(-1, head_width),
        qkv_sum[:, :, 2].reshape(-1, head_width),
        mid_sum.T,
        up_sum,
        down_sum.T,
        query_share,
        value_share,
        row_shares[0],
        row_shares[1],
        row_shares[2],
        up_share,
        row_shares[3],
        row_shares[4],
        row_shares[5],
    )


def solution(mesh):
    matrix = P("dp", "tensor")
    flipped = P("tensor", "dp")
    vector = P(("tensor", "dp"))
    arrival = P(None, ("tensor", "dp"), None)
    return jax.shard_map(
        local,
        mesh=mesh,
        in_specs=(arrival, P("dp", "tensor", None), P(), P())
        + (matrix, matrix, matrix, flipped, matrix, flipped)
        + (vector,) * 9,
        out_specs=(arrival, arrival) + (matrix, matrix, matrix, flipped, matrix, flipped) + (vector,) * 9,
        check_vma=False,
    )
```

```python
import functools
import math

import jax
import jax.numpy as jnp
from jax import lax
from jax.experimental import pallas as pl
from jax.experimental.pallas import tpu as pltpu
from jax.sharding import PartitionSpec as P

HEAD = 128
norm_epsilon = 1e-05
masked_score = -1e30
log2_e = math.log2(math.e)
head_scale = 1.0 / math.sqrt(HEAD)
gelu_root = math.sqrt(2.0 / math.pi)
bf16 = jnp.bfloat16
f32 = jnp.float32
MIB = 1024 * 1024
cost = 2.0
TALL = ((1,), (0,))
FLAT = ((1,), (1,))
DEEP = ((0,), (0,))


def dot(left, right, contract):
    return lax.dot_general(left, right, (contract, ((), ())), preferred_element_type=f32)


def shape(dims, dtype):
    return jax.ShapeDtypeStruct(tuple(dims), dtype)


def whole(array):
    return pl.BlockSpec(array.shape, lambda *i: (0,) * array.ndim)


def launch(body, grid, ins, in_specs, outs, out_specs, later=(), scratch=(), flops=0, nbytes=0, exps=0):
    later = tuple(later)
    count, skip = len(ins), len(later)

    def run(*refs):
        body(refs[:count], refs[count + skip :])

    return pl.pallas_call(
        run,
        grid=grid,
        in_specs=list(in_specs) + [pl.BlockSpec(memory_space=pl.ANY)] * skip,
        out_specs=list(out_specs),
        out_shape=list(outs),
        scratch_shapes=list(scratch),
        compiler_params=pltpu.CompilerParams(vmem_limit_bytes=60 * MIB),
        cost_estimate=pl.CostEstimate(
            flops=int(cost * flops), bytes_accessed=int(cost * nbytes), transcendentals=int(cost * exps)
        ),
    )(*ins, *later)


def attend(qkv, bias, halves, later=()):
    rows, columns = qkv.shape
    group = columns // halves
    heads = group // (3 * HEAD)
    width = heads * HEAD
    block = min(256, rows)

    def body(ins, outs):
        bias_ref, qkv_ref = ins
        mixed_ref, log_ref = outs
        shift = bias_ref[...]
        for head in range(heads):
            low = head * HEAD
            keys = qkv_ref[:, width + low : width + low + HEAD]
            values = qkv_ref[:, 2 * width + low : 2 * width + low + HEAD]
            for first in range(0, rows, block):
                part = slice(first, first + block)
                queries = qkv_ref[part, low : low + HEAD]
                scores = dot(keys, queries, FLAT) * (head_scale * log2_e) + shift
                peak = jnp.max(scores, axis=0, keepdims=True)
                weight = jnp.exp2(scores - peak)
                total = jnp.sum(weight, axis=0, keepdims=True)
                mixed = dot(values, weight.astype(bf16), DEEP) * (1.0 / total)
                mixed_ref[part, low : low + HEAD] = mixed.T.astype(bf16)
                log_ref[0, head : head + 1, part] = peak + jnp.log2(total)

    return launch(
        body,
        (halves,),
        [bias, qkv],
        [pl.BlockSpec((rows, 1), lambda i: (0, 0)), pl.BlockSpec((rows, group), lambda i: (0, i))],
        [shape((rows, halves * width), bf16), shape((halves, heads, rows), f32)],
        [pl.BlockSpec((rows, width), lambda i: (0, i)), pl.BlockSpec((1, heads, rows), lambda i: (i, 0, 0))],
        later,
        flops=4 * halves * heads * rows * rows * HEAD * 4,
        nbytes=rows * columns * 3,
        exps=halves * heads * rows * rows,
    )


def attend_back(qkv, bias, mixed, grads, logs, halves, later=()):
    rows, columns = qkv.shape
    group = columns // halves
    heads = group // (3 * HEAD)
    width = heads * HEAD
    block = min(256, rows)

    def body(ins, outs):
        bias_ref, qkv_ref, mixed_ref, grad_ref, log_ref = ins
        out_ref, sum_ref = outs
        shift = bias_ref[...]
        for head in range(heads):
            low = head * HEAD
            keys = qkv_ref[:, width + low : width + low + HEAD]
            values = qkv_ref[:, 2 * width + low : 2 * width + low + HEAD]
            key_total = jnp.zeros((rows, HEAD), f32)
            value_total = jnp.zeros((rows, HEAD), f32)
            query_sum = jnp.zeros((1, HEAD), f32)
            for first in range(0, rows, block):
                part = slice(first, first + block)
                queries = qkv_ref[part, low : low + HEAD]
                grad = grad_ref[part, low : low + HEAD]
                mix = mixed_ref[part, low : low + HEAD]
                centre = jnp.sum((grad.astype(f32) * mix.astype(f32)).T, axis=0, keepdims=True)
                scores = dot(keys, queries, FLAT) * (head_scale * log2_e) + shift
                weight = jnp.exp2(scores - log_ref[0, head : head + 1, part])
                weight_grad = dot(values, grad, FLAT)
                score_grad = (weight * (weight_grad - centre)).astype(bf16)
                value_total = value_total + dot(weight.astype(bf16), grad, TALL)
                key_total = key_total + dot(score_grad, queries, TALL)
                query_grad = (dot(keys, score_grad, DEEP) * head_scale).T.astype(bf16)
                out_ref[part, low : low + HEAD] = query_grad
                query_sum = query_sum + jnp.sum(query_grad.astype(f32), axis=0, keepdims=True)
            value_total = value_total.astype(bf16)
            out_ref[:, width + low : width + low + HEAD] = (key_total * head_scale).astype(bf16)
            out_ref[:, 2 * width + low : 2 * width + low + HEAD] = value_total
            sum_ref[0, :, low : low + HEAD] = query_sum
            sum_ref[0, :, width + low : width + low + HEAD] = jnp.zeros_like(query_sum)
            sum_ref[0, :, 2 * width + low : 2 * width + low + HEAD] = jnp.sum(
                value_total.astype(f32), axis=0, keepdims=True
            )

    columns_of = lambda n: pl.BlockSpec((rows, n), lambda i: (0, i))
    return launch(
        body,
        (halves,),
        [bias, qkv, mixed, grads, logs],
        [
            pl.BlockSpec((rows, 1), lambda i: (0, 0)),
            columns_of(group),
            columns_of(width),
            columns_of(width),
            pl.BlockSpec((1, heads, rows), lambda i: (i, 0, 0)),
        ],
        [shape((rows, columns), bf16), shape((halves, 1, group), f32)],
        [columns_of(group), pl.BlockSpec((1, 1, group), lambda i: (i, 0, 0))],
        later,
        flops=10 * halves * heads * rows * rows * HEAD * 4,
        nbytes=rows * columns * 6,
        exps=halves * heads * rows * rows,
    )


def tile_of(width, most):
    tile = min(width, most)
    while width % tile:
        tile //= 2
    return tile


def rows_matmul(pieces, weight, width, finish, extras, kinds, later=(), most=512):
    rows = sum(p.shape[0] for p in pieces)
    inner = weight.shape[0]
    tile = tile_of(width, most)

    def body(ins, refs):
        piece_refs, weight_ref = ins[: len(pieces)], ins[len(pieces)]
        extra_refs = ins[len(pieces) + 1 :]
        out_refs, gathered = refs[: len(kinds)], refs[len(kinds)]

        @pl.when(pl.program_id(0) == 0)
        def _():
            first = 0
            for ref in piece_refs:
                gathered[first : first + ref.shape[0], :] = ref[...]
                first += ref.shape[0]

        product = dot(gathered[...], weight_ref[...], TALL)
        for ref, value in zip(out_refs, finish(product, *[r[...] for r in extra_refs])):
            ref[...] = value

    def along(n):
        return pl.BlockSpec((n, tile), lambda j: (0, j))

    return launch(
        body,
        (width // tile,),
        [*pieces, weight, *extras],
        [whole(p) for p in pieces] + [along(inner)] + [along(e.shape[0]) for e in extras],
        [shape((n, width), dtype) for n, dtype in kinds],
        [along(n) for n, _ in kinds],
        later,
        scratch=[pltpu.VMEM((rows, inner), bf16)],
        flops=2 * rows * inner * width,
        nbytes=2 * (rows * inner + inner * width) + sum(4 * n * width for n, _ in kinds),
    )


def terms_matmul(left, weight, spans, later=(), most=512):
    rows, inner = left.shape
    outer = weight.shape[0]
    tile = tile_of(outer // 2, most)
    steps = outer // 2 // tile

    def body(ins, outs):
        left_ref, weight_ref = ins
        step = pl.program_id(0)
        product = dot(left_ref[...], weight_ref[...], FLAT).astype(bf16)
        groups = outs[: len(spans[0])], outs[len(spans[0]) :]
        for side in range(2):

            @pl.when((step < steps) if side == 0 else (step >= steps))
            def _():
                for ref, (low, high) in zip(groups[side], spans[side]):
                    ref[...] = product[low:high]

    places = [
        lambda j: (0, jnp.minimum(j, steps - 1)),
        lambda j: (0, jnp.maximum(j - steps, 0)),
    ]
    sizes = [(side, high - low) for side in range(2) for low, high in spans[side]]
    outs = launch(
        body,
        (2 * steps,),
        [left, weight],
        [whole(left), pl.BlockSpec((tile, inner), lambda j: (j, 0))],
        [shape((n, outer // 2), bf16) for _, n in sizes],
        [pl.BlockSpec((n, tile), places[side]) for side, n in sizes],
        later,
        flops=2 * rows * inner * outer,
        nbytes=2 * (rows * inner + outer * inner + rows * outer),
    )
    return outs[: len(spans[0])], outs[len(spans[0]) :]


def weight_grad(lefts, rights, later=(), core=None, most=256, row=None):
    flat = [p for pieces in lefts for p in pieces]
    outer = flat[0].shape[1]
    rows, columns = rights[0].shape
    tile = tile_of(outer, most)
    slots = len(rights)
    scalars = [] if core is None else [core.reshape(1)]
    rows_added = [] if core is None else [row]
    spare = 0 if core is None else 16

    def body(ins, refs):
        piece_refs, right_refs = ins[: len(flat)], ins[len(flat) :]
        gathered = refs[-1]
        first = 0
        for ref in piece_refs:
            gathered[first : first + ref.shape[0], :] = ref[...]
            first += ref.shape[0]
        total = None
        for slot in range(slots):
            term = dot(gathered[slot * rows : (slot + 1) * rows, :], right_refs[slot][...], DEEP)
            total = term if total is None else total + term
        refs[0][...] = total.astype(bf16)

    def body_apart(ins, refs):
        parity = lax.rem(pl.program_id(0), 2)
        total_ref = refs[2]
        body(ins[2:], (total_ref, refs[3]))
        added = jnp.broadcast_to(ins[1][...].astype(bf16), (spare, columns))

        def put(ref):
            ref[:tile, :] = total_ref[...]
            ref[tile:, :] = added

        @pl.when(parity == ins[0][0])
        def _():
            put(refs[0])

        @pl.when(parity != ins[0][0])
        def _():
            put(refs[1])

    outs = [shape((outer, columns), bf16)] if core is None else [shape((outer // tile // 2 * (tile + spare), columns), bf16)] * 2
    where = (lambda j: (j, 0)) if core is None else (lambda j: (j // 2, 0))
    result = launch(
        body if core is None else body_apart,
        (outer // tile,),
        [*scalars, *rows_added, *flat, *rights],
        [pl.BlockSpec(memory_space=pltpu.SMEM)] * len(scalars)
        + [whole(r) for r in rows_added]
        + [pl.BlockSpec((p.shape[0], tile), lambda j: (0, j)) for p in flat]
        + [whole(r) for r in rights],
        outs,
        [pl.BlockSpec((tile + spare, columns), where)] * len(outs),
        later,
        scratch=([] if core is None else [pltpu.VMEM((tile, columns), bf16)])
        + [pltpu.VMEM((slots * rows, tile), bf16)],
        flops=2 * slots * rows * outer * columns,
        nbytes=2 * (slots * rows * (outer + columns) + outer * columns),
    )
    return result[0] if core is None else result


def norm_tiles(body, rows, width, left, right, tiled, vectors, outs, sums, later):
    steps = 4
    tile = rows // steps
    n_left, n_right, n_tiled = len(left), len(right), len(tiled)

    def run(ins, refs):
        step = pl.program_id(0)
        left_refs = ins[:n_left]
        right_refs = ins[n_left : n_left + n_right]
        tiled_refs = ins[n_left + n_right : n_left + n_right + n_tiled]
        vector_ref = ins[-1] if vectors is not None else None

        def added(group):
            total = group[0][...].astype(f32)
            for ref in group[1:]:
                total = total + ref[...].astype(f32)
            return total

        both = jnp.concatenate([added(left_refs), added(right_refs)], axis=1)
        values, totals = body(both, [r[...] for r in tiled_refs], vector_ref)
        for ref, value in zip(refs, values):
            ref[...] = value.astype(ref.dtype)
        if sums:
            sum_ref = refs[-1]

            @pl.when(step == 0)
            def _():
                sum_ref[...] = jnp.zeros_like(sum_ref)

            for i, value in enumerate(totals):
                sum_ref[i : i + 1, :] += jnp.sum(value, axis=0, keepdims=True)

    def of(columns):
        return pl.BlockSpec((tile, columns), lambda i: (i, 0))

    def start(array, first):
        return pl.BlockSpec((tile, array.shape[1]), lambda i: (i + first // tile, 0))

    ins = [a for a, _ in (*left, *right)] + [*tiled] + ([vectors] if vectors is not None else [])
    return launch(
        run,
        (steps,),
        ins,
        [start(*a) for a in (*left, *right)]
        + [of(a.shape[1]) for a in tiled]
        + ([whole(vectors)] if vectors is not None else []),
        [shape((rows, c), dtype) for c, dtype in outs]
        + ([shape((8, width), f32)] if sums else []),
        [of(c) for c, _ in outs]
        + ([pl.BlockSpec((8, width), lambda i: (0, 0))] if sums else []),
        later,
        flops=rows * width * 20,
        nbytes=rows * width * 16,
    )


def normed(values):
    centred = values - jnp.mean(values, axis=-1, keepdims=True)
    inverse = lax.rsqrt(jnp.mean(centred * centred, axis=-1, keepdims=True) + norm_epsilon)
    return centred * inverse, inverse


def norm_back(grads, unit, inverse, gain):
    scaled = grads * gain
    return inverse * (
        scaled
        - jnp.mean(scaled, axis=-1, keepdims=True)
        - unit * jnp.mean(scaled * unit, axis=-1, keepdims=True)
    )


def first_norm(terms, rows, vectors, later=()):
    def body(both, tiled, v):
        unit, inverse = normed(tiled[0].astype(f32) + (both + v[0:1, :]))
        return [unit * v[1:2, :] + v[2:3, :], unit, inverse], []

    n, width = rows.shape
    kinds = [(width, bf16), (width, f32), (1, f32)]
    return norm_tiles(body, n, width, *terms, [rows], vectors, kinds, False, later)


def second_norm(terms, unit, cotangent, vectors, later=()):
    def body(both, tiled, v):
        first, grads = tiled[0] * v[1:2, :] + v[2:3, :], tiled[1].astype(f32)
        unit_two, inverse = normed(first + (both + v[3:4, :]))
        back = norm_back(grads, unit_two, inverse, v[4:5, :])
        return [unit_two * v[4:5, :] + v[5:6, :], back, back], [back, grads * unit_two, grads]

    n, width = unit.shape
    kinds = [(width, bf16), (width, f32), (width, bf16)]
    return norm_tiles(body, n, width, *terms, [unit, cotangent], vectors, kinds, True, later)


def first_norm_back(terms, back_two, unit, inverse, vectors, later=()):
    def body(both, tiled, v):
        grads = tiled[0] + both
        back = norm_back(grads, tiled[1], tiled[2], v[1:2, :])
        return [back, back], [back, grads * tiled[1], grads]

    n, width = unit.shape
    kinds = [(width, f32), (width, bf16)]
    return norm_tiles(body, n, width, *terms, [back_two, unit, inverse], vectors, kinds, True, later)


def input_grad(terms, back, later=()):
    def body(both, tiled, v):
        return [tiled[0] + both], []

    n, width = back.shape
    return norm_tiles(body, n, width, *terms, [back], None, [(width, bf16)], False, later)[0]


class TensorAxis:
    def __init__(self):
        self.size = lax.axis_size("tensor")
        self.me = lax.axis_index("tensor")
        self.square = self.size == 4
        if self.square:
            self.origins = self.me ^ jnp.array([0, 1, 3, 2], jnp.int32)
        else:
            self.origins = jnp.arange(self.size, dtype=jnp.int32)

    def swap(self, array, bit):
        return lax.ppermute(array, "tensor", [(i, i ^ bit) for i in range(self.size)])

    def gather(self, block, earlier=()):
        if not self.square:
            return [lax.all_gather(block, "tensor", axis=0, tiled=True)]
        half = block.shape[0] // 2
        along_x, along_y = self.swap(block, 1), self.swap(block, 2)
        onward_x, onward_y = along_y[:half], along_x[half:]
        if earlier:
            zero = nothing(*earlier).astype(block.dtype)
            onward_x, onward_y = onward_x + zero, onward_y + zero
        far_top, far_bottom = self.swap(onward_x, 1), self.swap(onward_y, 2)
        return [block, along_x, far_top, far_bottom, along_y]

    def spans(self, rows):
        if not self.square:
            return [(0, rows)], [(0, rows)]
        r = rows // 4
        return [(r, 3 * r), (3 * r, 4 * r), (0, r)], [(2 * r, 4 * r), (r, 2 * r), (0, r)]

    def line_up(self, block):
        if not self.square:
            return lax.all_gather(block, "tensor", axis=1, tiled=True)
        width = block.shape[1]
        full = jnp.zeros((block.shape[0], 4 * width), block.dtype)
        for bits in range(4):
            piece = self.swap(block, bits) if bits else block
            full = lax.dynamic_update_slice(full, piece, (0, (self.me ^ bits) * width))
        return full

    def scatter(self, terms):
        left, right = terms
        if not self.square:
            full = jnp.concatenate([left[0], right[0]], axis=1)
            mine = lax.psum_scatter(full, "tensor", scatter_dimension=0, tiled=True)
            half = mine.shape[1] // 2
            return ([(mine[:, :half], 0)], [(mine[:, half:], 0)]), (), ()
        rows = left[1].shape[0]
        from_x, from_y = self.swap(left[0], 1), self.swap(right[0], 2)
        left_far = self.swap((left[1].astype(f32) + from_x[rows:].astype(f32)).astype(bf16), 2)
        right_far = self.swap((right[1].astype(f32) + from_y[:rows].astype(f32)).astype(bf16), 1)
        left = [(left[2], 0), (from_x, 0), (left_far, 0)]
        right = [(right[2], 0), (from_y, rows), (right_far, 0)]
        return (left, right), (from_x, from_y), (left_far, right_far)


class GroupAxis:
    def __init__(self):
        self.size = lax.axis_size("dp")
        self.me = lax.axis_index("dp")
        self.line = self.size == 8
        self.z = self.me // 2
        n = self.size
        self.next = [(i, (i + 2) % n) for i in range(n)]
        self.last = [(i, (i - 2) % n) for i in range(n)]

    def send(self, array, pairs):
        return lax.ppermute(array, "dp", pairs)

    def gather(self, shard):
        return lax.all_gather(shard, "dp", axis=0, tiled=True)

    def scatter(self, terms):
        return lax.psum_scatter(terms, "dp", scatter_dimension=0, tiled=True).astype(f32)

    def weight_scatter(self, lefts, rights, row, later):
        if not self.line:
            terms = weight_grad(lefts, rights, later)
            return self.scatter(terms), lax.psum(row, "dp")[0], terms, (), (), ()
        block = lefts[0][0].shape[1] // self.size
        mine, theirs = weight_grad(lefts, rights, later, self.me % 2, block, row)
        got = self.send(theirs, [(i, i ^ 1) for i in range(self.size)])
        rows = mine.shape[0] // 4

        def toward(step):
            first = ((self.z + step) % 4) * rows
            parts = [lax.dynamic_slice_in_dim(a, first, rows).astype(f32) for a in (mine, got)]
            return parts[0] + parts[1]

        far = toward(2).astype(bf16)
        up = self.send(far, [(0, 2), (1, 3), (2, 4), (3, 5)])
        down = self.send(far, [(6, 4), (7, 5), (4, 2), (5, 3)])
        ahead = (toward(1) + up.astype(f32)).astype(bf16)
        behind = (toward(3) + down.astype(f32)).astype(bf16)
        ahead, behind = self.send(ahead, self.next), self.send(behind, self.last)
        total = toward(0) + ahead.astype(f32) + behind.astype(f32)
        return total[:block], total[block], mine, (got,), (up, down), (ahead, behind)


def nothing(*arrays):
    return sum(a[(0,) * a.ndim].astype(f32) * 0.0 for a in arrays)


def touched(array, *arrays):
    if not arrays:
        return array
    corner = array[:16, :128]
    return lax.dynamic_update_slice(array, corner + nothing(*arrays).astype(array.dtype), (0, 0))


def add_up(array, axis, earlier=()):
    size = lax.axis_size(axis)
    bit, stages = 1, []
    while bit < size:
        if len(stages) < len(earlier) and earlier[len(stages)] is not None:
            array = array + nothing(earlier[len(stages)])
        stages.append(lax.ppermute(array, axis, [(i, i ^ bit) for i in range(size)]))
        array = array + stages[-1]
        bit *= 2
    return array, stages


def gelu(hidden):
    return 0.5 * hidden * (1.0 + jnp.tanh(gelu_root * (hidden + 0.044715 * hidden * hidden * hidden)))


def gelu_slope(hidden):
    square = hidden * hidden
    bend = jnp.tanh(gelu_root * (hidden + 0.044715 * hidden * square))
    return 0.5 * (1.0 + bend) + 0.5 * hidden * (1.0 - bend * bend) * gelu_root * (
        1.0 + 3 * 0.044715 * square
    )


def local(
    tokens,
    cotangent,
    lengths,
    dealing,
    query_weight,
    key_weight,
    value_weight,
    output_weight,
    up_weight,
    down_weight,
    query_bias,
    value_bias,
    output_bias,
    attention_gain,
    attention_shift,
    up_bias,
    down_bias,
    feedforward_gain,
    feedforward_shift,
):
    tensor, group = TensorAxis(), GroupAxis()
    groups, splits = group.size, tensor.size
    slots, own_rows, model_width = cotangent.shape
    over = range(slots)
    slot_rows = own_rows * splits
    arrival_rows = tokens.shape[1]
    head_width = query_weight.shape[1]
    half = head_width // 2
    piece = query_bias.shape[0]
    hidden_width = up_weight.shape[1]
    spans = tensor.spans(slot_rows)

    slot_dealing = dealing.reshape(groups, slots)
    sent = jnp.take(tokens, dealing, axis=0, mode="clip").reshape(groups, slots, arrival_rows, model_width)
    came = lax.all_to_all(sent, "dp", split_axis=0, concat_axis=0, tiled=True)
    zero = came[0, 0, 0, 0] * 0.0
    token_pieces, arrived = [], []
    for s in over:
        rows = came[:, s].reshape(own_rows, model_width)
        if s > 0 and tensor.square:
            rows = rows + token_pieces[0][1][0, 0] * 0.0
        arrived.append(rows)
        token_pieces.append(tensor.gather(rows))

    head_piece = jnp.concatenate([query_bias, value_bias, up_bias]).astype(bf16)
    row_piece = jnp.concatenate(
        [output_bias, attention_gain, attention_shift, down_bias, feedforward_gain, feedforward_shift]
    ).astype(bf16)
    vector = jnp.concatenate([head_piece, row_piece])
    shard_rows, spare = query_weight.shape[0], 128
    padded = jnp.zeros((shard_rows * spare,), bf16).at[: vector.shape[0]].set(vector) + zero
    three = [w.astype(bf16) for w in (query_weight, key_weight, value_weight)]
    qkv_weight = group.gather(
        jnp.concatenate(
            [w[:, :half] for w in three] + [w[:, half:] for w in three] + [padded.reshape(shard_rows, spare)],
            axis=1,
        )
    )
    mid_weight = group.gather(touched(output_weight.astype(bf16).T, came))
    up_full = group.gather(touched(up_weight.astype(bf16), came))
    down_full = group.gather(touched(down_weight.astype(bf16).T, came))
    used = -(-vector.shape[0] // spare)
    table = qkv_weight[:, 3 * head_width :].reshape(groups, shard_rows, spare)[:, :used]
    table = table.reshape(groups, -1)[:, : vector.shape[0]]
    head_vectors = table.astype(f32)
    row_table = table[:, head_piece.shape[0] :].reshape(groups, 6, piece)
    row_table = jnp.moveaxis(row_table, 1, 0).reshape(6, groups * piece)
    row_vectors = tensor.line_up(row_table).astype(f32)
    query_bias_here = head_vectors[:, :piece].reshape(-1)
    value_bias_here = head_vectors[:, piece : 2 * piece].reshape(-1)
    hidden_bias = head_vectors[:, 2 * piece : head_piece.shape[0]].reshape(1, -1)
    row_vectors = jnp.concatenate([row_vectors, jnp.zeros((2, model_width), f32)], axis=0)
    blank = jnp.zeros((half,), f32)
    qkv_bias = jnp.concatenate(
        [query_bias_here[:half], blank, value_bias_here[:half]]
        + [query_bias_here[half:], blank, value_bias_here[half:]]
    )[None]

    positions = (tensor.origins[:, None] * own_rows + jnp.arange(own_rows)[None, :]).reshape(-1)
    slot_lengths = lax.dynamic_slice_in_dim(jnp.take(lengths, dealing, axis=0), group.me * slots, slots)
    biases = [
        jnp.where(positions < slot_lengths[s], 0.0, masked_score).astype(f32)[:, None] for s in over
    ]

    def near(pieces):
        return tuple(pieces[1:2] + pieces[4:])

    rows_bf16 = [(slot_rows, bf16)]
    qkv, mixed, logs, terms, sums = [], [], [], [], []
    before = near(token_pieces[1])
    for s in over:
        qkv += rows_matmul(
            token_pieces[s],
            qkv_weight,
            3 * head_width,
            lambda product, bias: ((product + bias).astype(bf16),),
            [qkv_bias],
            rows_bf16,
            before,
            most=256,
        )
        mix, log = attend(qkv[s], biases[s], 2)
        mixed.append(mix)
        logs.append(log)
        terms.append(terms_matmul(mix, mid_weight, spans, sums[-1][2] if sums else (row_vectors,)))
        sums.append(tensor.scatter(terms[s]))
        before = (terms[s][0][0],)
    first = [first_norm(sums[0][0], arrived[0], row_vectors, before)]
    first_pieces = [tensor.gather(first[0][0])]
    first.append(first_norm(sums[1][0], arrived[1], row_vectors, tuple(first_pieces[0][1:])))
    hidden, active, terms, sums = [], [], [], []

    def to_hidden(s, later):
        wide, narrow = rows_matmul(
            first_pieces[s],
            up_full,
            hidden_width,
            lambda product, bias: (product + bias, gelu(product + bias).astype(bf16)),
            [hidden_bias],
            [(slot_rows, f32), (slot_rows, bf16)],
            later,
        )
        hidden.append(wide)
        active.append(narrow)

    def from_hidden(s, later):
        terms.append(terms_matmul(active[s], down_full, spans, later))
        sums.append(tensor.scatter(terms[s]))

    to_hidden(0, (first[1][0],))
    first_pieces.append(tensor.gather(first[1][0], (active[0],)))
    from_hidden(0, tuple(first_pieces[1][1:]))
    to_hidden(1, (terms[0][0][0],))
    second, down_pieces = [], []

    def to_second(s, later):
        second.append(second_norm(sums[s][0], first[s][1], cotangent[s], row_vectors, later))
        down_pieces.append(tensor.gather(second[s][2]))

    from_hidden(1, sums[0][1])
    to_second(0, (terms[1][0][0],))
    to_second(1, near(down_pieces[0]))

    def give_back(rows):
        return lax.all_to_all(
            rows.reshape(groups, arrival_rows, model_width), "dp", split_axis=0, concat_axis=0, tiled=True
        )

    returned_rows = [give_back(s[0]) for s in second]

    hidden_grad, up_sums, terms, first_sums = [], [], [], []
    before = ()

    def through_gelu(product, wide):
        grad = (product * gelu_slope(wide)).astype(bf16)
        return grad, jnp.sum(grad.astype(f32), axis=0, keepdims=True)

    for s in over:
        grad, total = rows_matmul(
            down_pieces[s],
            down_full,
            hidden_width,
            through_gelu,
            [hidden[s]],
            [(slot_rows, bf16), (1, f32)],
            before,
        )
        hidden_grad.append(grad)
        up_sums.append(total)
        if s == 0:
            terms.append(terms_matmul(grad, up_full, spans, (*near(down_pieces[1]), returned_rows[0])))
            first_sums.append(tensor.scatter(terms[s]))
            before = (terms[s][0][0],)
    first_back = []

    def back_to_first(s, later):
        first_back.append(
            first_norm_back(
                first_sums[s][0], second[s][1], first[s][1], first[s][2], row_vectors, later
            )
        )
        return tensor.gather(first_back[s][1])

    down_terms = weight_grad(down_pieces, active, (hidden_grad[1], *first_sums[0][1], *returned_rows))
    down_terms = touched(down_terms, *first_sums[0][2])
    down_sum = group.scatter(down_terms)
    grad_pieces = [back_to_first(0, (down_terms,))]
    terms.append(terms_matmul(hidden_grad[1], up_full, spans, (first_back[0][0],)))
    first_sums.append(tensor.scatter(terms[1]))
    up_terms = weight_grad(first_pieces, hidden_grad, (terms[1][0][0],))
    up_terms = touched(up_terms, *first_sums[1][1], *near(grad_pieces[0]))
    up_sum = group.scatter(up_terms)
    grad_pieces.append(back_to_first(1, (up_terms,)))

    def attention_in(s, later):
        return rows_matmul(
            grad_pieces[s],
            mid_weight,
            head_width,
            lambda product: (product.astype(bf16),),
            [],
            rows_bf16,
            later,
        )[0]

    def attention_back(s, mixed_grad, later):
        return attend_back(qkv[s], biases[s], mixed[s], mixed_grad, logs[s], 2, later)

    mixed_grad = [attention_in(0, (up_terms,))]
    row_grads = jnp.concatenate(
        [sum(f[2] for f in first_back)[:3], sum(s[3] for s in second)[:3]], axis=0
    ).reshape(-1, 128)
    row_grads, stages = add_up(row_grads, "tensor", (mixed_grad[0],))
    stages = [(stage,) for stage in stages] + [(), ()]
    backs = [attention_back(0, mixed_grad[0], ())]
    terms = [terms_matmul(backs[0][0], qkv_weight, spans, (*stages[0], *near(grad_pieces[1])))]
    sums = [tensor.scatter(terms[0])]
    mixed_grad.append(attention_in(1, (terms[0][0][0], *stages[1])))
    mid_terms = weight_grad(grad_pieces, mixed, (mixed_grad[1],))
    small = jnp.concatenate([row_grads, sum(up_sums).reshape(-1, 128)], axis=0)
    small, stages = add_up(small, "dp", (mixed_grad[1], mid_terms, None))
    mid_sum = group.scatter(touched(mid_terms, *sums[0][1]))
    backs.append(attention_back(1, mixed_grad[1], (mid_terms, *sums[0][1], stages[0])))
    token_grad = [input_grad(sums[0][0], first_back[0][0], (backs[1][0],))]
    returned_grads = [give_back(token_grad[0])]
    qkv_grad = [b[0] for b in backs]
    bias_terms = sum(b[1] for b in backs).reshape(1, -1)
    qkv_sum, bias_sum, qkv_terms, *qkv_stage = group.weight_scatter(
        token_pieces, qkv_grad, bias_terms, (token_grad[0], down_sum, stages[1])
    )
    terms.append(terms_matmul(qkv_grad[-1], qkv_weight, spans, (qkv_terms, *returned_grads)))
    last_grad = input_grad(
        tensor.scatter(terms[-1])[0], first_back[-1][0], (*qkv_stage[1], up_sum, stages[2])
    )
    returned_grads.append(give_back(last_grad))

    places = slot_dealing.T.reshape(-1)
    inverse = jnp.zeros(places.shape, jnp.int32).at[places].set(
        jnp.arange(places.shape[0], dtype=jnp.int32)
    )
    result = jnp.take(jnp.concatenate(returned_rows, axis=0), inverse, axis=0, mode="clip")
    inverse = inverse + nothing(mid_sum).astype(jnp.int32)
    token_gradient = jnp.take(jnp.concatenate(returned_grads, axis=0), inverse, axis=0, mode="clip")

    row_shares = lax.dynamic_slice_in_dim(
        small.reshape(-1)[: 6 * model_width].reshape(6, splits * groups, piece),
        tensor.me * groups + group.me,
        1,
        axis=1,
    )[:, 0]

    def share(values):
        return lax.dynamic_index_in_dim(values.reshape(groups, -1), group.me, 0, False)

    bias_sum = bias_sum.reshape(2, 3, half)
    query_share = share(bias_sum[:, 0])
    value_share = share(bias_sum[:, 2])
    up_share = share(small.reshape(-1)[6 * model_width :])

    qkv_sum = qkv_sum.reshape(-1, 2, 3, half)
    return (
        result,
        token_gradient,
        qkv_sum[:, :, 0].reshape(-1, head_width),
        qkv_sum[:, :, 1].reshape(-1, head_width),
        qkv_sum[:, :, 2].reshape(-1, head_width),
        mid_sum.T,
        up_sum,
        down_sum.T,
        query_share,
        value_share,
        row_shares[0],
        row_shares[1],
        row_shares[2],
        up_share,
        row_shares[3],
        row_shares[4],
        row_shares[5],
    )


def solution(mesh):
    matrix = P("dp", "tensor")
    flipped = P("tensor", "dp")
    vector = P(("tensor", "dp"))
    arrival = P(None, ("tensor", "dp"), None)
    return jax.shard_map(
        local,
        mesh=mesh,
        in_specs=(arrival, P("dp", "tensor", None), P(), P())
        + (matrix, matrix, matrix, flipped, matrix, flipped)
        + (vector,) * 9,
        out_specs=(arrival, arrival) + (matrix, matrix, matrix, flipped, matrix, flipped) + (vector,) * 9,
        check_vma=False,
    )
```

```python
import functools
import math

import jax
import jax.numpy as jnp
from jax import lax
from jax.experimental import pallas as pl
from jax.experimental.pallas import tpu as pltpu
from jax.sharding import PartitionSpec as P

HEAD = 128
norm_epsilon = 1e-05
masked_score = -1e30
log2_e = math.log2(math.e)
head_scale = 1.0 / math.sqrt(HEAD)
gelu_root = math.sqrt(2.0 / math.pi)
bf16 = jnp.bfloat16
f32 = jnp.float32
MIB = 1024 * 1024
cost = 2.0
TALL = ((1,), (0,))
FLAT = ((1,), (1,))
DEEP = ((0,), (0,))


def dot(left, right, contract):
    return lax.dot_general(left, right, (contract, ((), ())), preferred_element_type=f32)


def shape(dims, dtype):
    return jax.ShapeDtypeStruct(tuple(dims), dtype)


def whole(array):
    return pl.BlockSpec(array.shape, lambda *i: (0,) * array.ndim)


def launch(body, grid, ins, in_specs, outs, out_specs, later=(), scratch=(), flops=0, nbytes=0, exps=0):
    later = tuple(later)
    count, skip = len(ins), len(later)

    def run(*refs):
        body(refs[:count], refs[count + skip :])

    return pl.pallas_call(
        run,
        grid=grid,
        in_specs=list(in_specs) + [pl.BlockSpec(memory_space=pl.ANY)] * skip,
        out_specs=list(out_specs),
        out_shape=list(outs),
        scratch_shapes=list(scratch),
        compiler_params=pltpu.CompilerParams(vmem_limit_bytes=60 * MIB),
        cost_estimate=pl.CostEstimate(
            flops=int(cost * flops), bytes_accessed=int(cost * nbytes), transcendentals=int(cost * exps)
        ),
    )(*ins, *later)


def attend(qkv, bias, halves, later=()):
    rows, columns = qkv.shape
    group = columns // halves
    heads = group // (3 * HEAD)
    width = heads * HEAD
    block = min(256, rows)

    def body(ins, outs):
        bias_ref, qkv_ref = ins
        mixed_ref, log_ref = outs
        shift = bias_ref[...]
        for head in range(heads):
            low = head * HEAD
            keys = qkv_ref[:, width + low : width + low + HEAD]
            values = qkv_ref[:, 2 * width + low : 2 * width + low + HEAD]
            for first in range(0, rows, block):
                part = slice(first, first + block)
                queries = qkv_ref[part, low : low + HEAD]
                scores = dot(keys, queries, FLAT) * (head_scale * log2_e) + shift
                peak = jnp.max(scores, axis=0, keepdims=True)
                weight = jnp.exp2(scores - peak)
                total = jnp.sum(weight, axis=0, keepdims=True)
                mixed = dot(values, weight.astype(bf16), DEEP) * (1.0 / total)
                mixed_ref[part, low : low + HEAD] = mixed.T.astype(bf16)
                log_ref[0, head : head + 1, part] = peak + jnp.log2(total)

    return launch(
        body,
        (halves,),
        [bias, qkv],
        [pl.BlockSpec((rows, 1), lambda i: (0, 0)), pl.BlockSpec((rows, group), lambda i: (0, i))],
        [shape((rows, halves * width), bf16), shape((halves, heads, rows), f32)],
        [pl.BlockSpec((rows, width), lambda i: (0, i)), pl.BlockSpec((1, heads, rows), lambda i: (i, 0, 0))],
        later,
        flops=4 * halves * heads * rows * rows * HEAD * 4,
        nbytes=rows * columns * 3,
        exps=halves * heads * rows * rows,
    )


def attend_back(qkv, bias, mixed, grads, logs, halves, later=()):
    rows, columns = qkv.shape
    group = columns // halves
    heads = group // (3 * HEAD)
    width = heads * HEAD
    block = min(256, rows)

    def body(ins, outs):
        bias_ref, qkv_ref, mixed_ref, grad_ref, log_ref = ins
        out_ref, sum_ref = outs
        shift = bias_ref[...]
        for head in range(heads):
            low = head * HEAD
            keys = qkv_ref[:, width + low : width + low + HEAD]
            values = qkv_ref[:, 2 * width + low : 2 * width + low + HEAD]
            key_total = jnp.zeros((rows, HEAD), f32)
            value_total = jnp.zeros((rows, HEAD), f32)
            query_sum = jnp.zeros((1, HEAD), f32)
            for first in range(0, rows, block):
                part = slice(first, first + block)
                queries = qkv_ref[part, low : low + HEAD]
                grad = grad_ref[part, low : low + HEAD]
                mix = mixed_ref[part, low : low + HEAD]
                centre = jnp.sum((grad.astype(f32) * mix.astype(f32)).T, axis=0, keepdims=True)
                scores = dot(keys, queries, FLAT) * (head_scale * log2_e) + shift
                weight = jnp.exp2(scores - log_ref[0, head : head + 1, part])
                weight_grad = dot(values, grad, FLAT)
                score_grad = (weight * (weight_grad - centre)).astype(bf16)
                value_total = value_total + dot(weight.astype(bf16), grad, TALL)
                key_total = key_total + dot(score_grad, queries, TALL)
                query_grad = (dot(keys, score_grad, DEEP) * head_scale).T.astype(bf16)
                out_ref[part, low : low + HEAD] = query_grad
                query_sum = query_sum + jnp.sum(query_grad.astype(f32), axis=0, keepdims=True)
            value_total = value_total.astype(bf16)
            out_ref[:, width + low : width + low + HEAD] = (key_total * head_scale).astype(bf16)
            out_ref[:, 2 * width + low : 2 * width + low + HEAD] = value_total
            sum_ref[0, :, low : low + HEAD] = query_sum
            sum_ref[0, :, width + low : width + low + HEAD] = jnp.zeros_like(query_sum)
            sum_ref[0, :, 2 * width + low : 2 * width + low + HEAD] = jnp.sum(
                value_total.astype(f32), axis=0, keepdims=True
            )

    columns_of = lambda n: pl.BlockSpec((rows, n), lambda i: (0, i))
    return launch(
        body,
        (halves,),
        [bias, qkv, mixed, grads, logs],
        [
            pl.BlockSpec((rows, 1), lambda i: (0, 0)),
            columns_of(group),
            columns_of(width),
            columns_of(width),
            pl.BlockSpec((1, heads, rows), lambda i: (i, 0, 0)),
        ],
        [shape((rows, columns), bf16), shape((halves, 1, group), f32)],
        [columns_of(group), pl.BlockSpec((1, 1, group), lambda i: (i, 0, 0))],
        later,
        flops=10 * halves * heads * rows * rows * HEAD * 4,
        nbytes=rows * columns * 6,
        exps=halves * heads * rows * rows,
    )


def tile_of(width, most):
    tile = min(width, most)
    while width % tile:
        tile //= 2
    return tile


def rows_matmul(pieces, weight, width, finish, extras, kinds, later=(), most=512):
    rows = sum(p.shape[0] for p in pieces)
    inner = weight.shape[0]
    tile = tile_of(width, most)

    def body(ins, refs):
        piece_refs, weight_ref = ins[: len(pieces)], ins[len(pieces)]
        extra_refs = ins[len(pieces) + 1 :]
        out_refs, gathered = refs[: len(kinds)], refs[len(kinds)]

        @pl.when(pl.program_id(0) == 0)
        def _():
            first = 0
            for ref in piece_refs:
                gathered[first : first + ref.shape[0], :] = ref[...]
                first += ref.shape[0]

        product = dot(gathered[...], weight_ref[...], TALL)
        for ref, value in zip(out_refs, finish(product, *[r[...] for r in extra_refs])):
            ref[...] = value

    def along(n):
        return pl.BlockSpec((n, tile), lambda j: (0, j))

    return launch(
        body,
        (width // tile,),
        [*pieces, weight, *extras],
        [whole(p) for p in pieces] + [along(inner)] + [along(e.shape[0]) for e in extras],
        [shape((n, width), dtype) for n, dtype in kinds],
        [along(n) for n, _ in kinds],
        later,
        scratch=[pltpu.VMEM((rows, inner), bf16)],
        flops=2 * rows * inner * width,
        nbytes=2 * (rows * inner + inner * width) + sum(4 * n * width for n, _ in kinds),
    )


def terms_matmul(left, weight, spans, later=(), most=512):
    rows, inner = left.shape
    outer = weight.shape[0]
    tile = tile_of(outer // 2, most)
    steps = outer // 2 // tile

    def body(ins, outs):
        left_ref, weight_ref = ins
        step = pl.program_id(0)
        product = dot(left_ref[...], weight_ref[...], FLAT).astype(bf16)
        groups = outs[: len(spans[0])], outs[len(spans[0]) :]
        for side in range(2):

            @pl.when((step < steps) if side == 0 else (step >= steps))
            def _():
                for ref, (low, high) in zip(groups[side], spans[side]):
                    ref[...] = product[low:high]

    places = [
        lambda j: (0, jnp.minimum(j, steps - 1)),
        lambda j: (0, jnp.maximum(j - steps, 0)),
    ]
    sizes = [(side, high - low) for side in range(2) for low, high in spans[side]]
    outs = launch(
        body,
        (2 * steps,),
        [left, weight],
        [whole(left), pl.BlockSpec((tile, inner), lambda j: (j, 0))],
        [shape((n, outer // 2), bf16) for _, n in sizes],
        [pl.BlockSpec((n, tile), places[side]) for side, n in sizes],
        later,
        flops=2 * rows * inner * outer,
        nbytes=2 * (rows * inner + outer * inner + rows * outer),
    )
    return outs[: len(spans[0])], outs[len(spans[0]) :]


def weight_grad(lefts, rights, later=(), core=None, most=256, row=None):
    flat = [p for pieces in lefts for p in pieces]
    outer = flat[0].shape[1]
    rows, columns = rights[0].shape
    tile = tile_of(outer, most)
    slots = len(rights)
    scalars = [] if core is None else [core.reshape(1)]
    rows_added = [] if core is None else [row]
    spare = 0 if core is None else 16

    def body(ins, refs):
        piece_refs, right_refs = ins[: len(flat)], ins[len(flat) :]
        gathered = refs[-1]
        first = 0
        for ref in piece_refs:
            gathered[first : first + ref.shape[0], :] = ref[...]
            first += ref.shape[0]
        total = None
        for slot in range(slots):
            term = dot(gathered[slot * rows : (slot + 1) * rows, :], right_refs[slot][...], DEEP)
            total = term if total is None else total + term
        refs[0][...] = total.astype(bf16)

    def body_apart(ins, refs):
        parity = lax.rem(pl.program_id(0), 2)
        total_ref = refs[2]
        body(ins[2:], (total_ref, refs[3]))
        added = jnp.broadcast_to(ins[1][...].astype(bf16), (spare, columns))

        def put(ref):
            ref[:tile, :] = total_ref[...]
            ref[tile:, :] = added

        @pl.when(parity == ins[0][0])
        def _():
            put(refs[0])

        @pl.when(parity != ins[0][0])
        def _():
            put(refs[1])

    outs = [shape((outer, columns), bf16)] if core is None else [shape((outer // tile // 2 * (tile + spare), columns), bf16)] * 2
    where = (lambda j: (j, 0)) if core is None else (lambda j: (j // 2, 0))
    result = launch(
        body if core is None else body_apart,
        (outer // tile,),
        [*scalars, *rows_added, *flat, *rights],
        [pl.BlockSpec(memory_space=pltpu.SMEM)] * len(scalars)
        + [whole(r) for r in rows_added]
        + [pl.BlockSpec((p.shape[0], tile), lambda j: (0, j)) for p in flat]
        + [whole(r) for r in rights],
        outs,
        [pl.BlockSpec((tile + spare, columns), where)] * len(outs),
        later,
        scratch=([] if core is None else [pltpu.VMEM((tile, columns), bf16)])
        + [pltpu.VMEM((slots * rows, tile), bf16)],
        flops=2 * slots * rows * outer * columns,
        nbytes=2 * (slots * rows * (outer + columns) + outer * columns),
    )
    return result[0] if core is None else result


def norm_tiles(body, rows, width, left, right, tiled, vectors, outs, sums, later):
    steps = 4
    tile = rows // steps
    n_left, n_right, n_tiled = len(left), len(right), len(tiled)

    def run(ins, refs):
        step = pl.program_id(0)
        left_refs = ins[:n_left]
        right_refs = ins[n_left : n_left + n_right]
        tiled_refs = ins[n_left + n_right : n_left + n_right + n_tiled]
        vector_ref = ins[-1] if vectors is not None else None

        def added(group):
            total = group[0][...].astype(f32)
            for ref in group[1:]:
                total = total + ref[...].astype(f32)
            return total

        both = jnp.concatenate([added(left_refs), added(right_refs)], axis=1)
        values, totals = body(both, [r[...] for r in tiled_refs], vector_ref)
        for ref, value in zip(refs, values):
            ref[...] = value.astype(ref.dtype)
        if sums:
            sum_ref = refs[-1]

            @pl.when(step == 0)
            def _():
                sum_ref[...] = jnp.zeros_like(sum_ref)

            for i, value in enumerate(totals):
                sum_ref[i : i + 1, :] += jnp.sum(value, axis=0, keepdims=True)

    def of(columns):
        return pl.BlockSpec((tile, columns), lambda i: (i, 0))

    def start(array, first):
        return pl.BlockSpec((tile, array.shape[1]), lambda i: (i + first // tile, 0))

    ins = [a for a, _ in (*left, *right)] + [*tiled] + ([vectors] if vectors is not None else [])
    return launch(
        run,
        (steps,),
        ins,
        [start(*a) for a in (*left, *right)]
        + [of(a.shape[1]) for a in tiled]
        + ([whole(vectors)] if vectors is not None else []),
        [shape((rows, c), dtype) for c, dtype in outs]
        + ([shape((8, width), f32)] if sums else []),
        [of(c) for c, _ in outs]
        + ([pl.BlockSpec((8, width), lambda i: (0, 0))] if sums else []),
        later,
        flops=rows * width * 20,
        nbytes=rows * width * 16,
    )


def normed(values):
    centred = values - jnp.mean(values, axis=-1, keepdims=True)
    inverse = lax.rsqrt(jnp.mean(centred * centred, axis=-1, keepdims=True) + norm_epsilon)
    return centred * inverse, inverse


def norm_back(grads, unit, inverse, gain):
    scaled = grads * gain
    return inverse * (
        scaled
        - jnp.mean(scaled, axis=-1, keepdims=True)
        - unit * jnp.mean(scaled * unit, axis=-1, keepdims=True)
    )


def first_norm(terms, rows, vectors, later=()):
    def body(both, tiled, v):
        unit, inverse = normed(tiled[0].astype(f32) + (both + v[0:1, :]))
        return [unit * v[1:2, :] + v[2:3, :], unit, inverse], []

    n, width = rows.shape
    kinds = [(width, bf16), (width, f32), (1, f32)]
    return norm_tiles(body, n, width, *terms, [rows], vectors, kinds, False, later)


def second_norm(terms, unit, cotangent, vectors, later=()):
    def body(both, tiled, v):
        first, grads = tiled[0] * v[1:2, :] + v[2:3, :], tiled[1].astype(f32)
        unit_two, inverse = normed(first + (both + v[3:4, :]))
        back = norm_back(grads, unit_two, inverse, v[4:5, :])
        return [unit_two * v[4:5, :] + v[5:6, :], back, back], [back, grads * unit_two, grads]

    n, width = unit.shape
    kinds = [(width, bf16), (width, f32), (width, bf16)]
    return norm_tiles(body, n, width, *terms, [unit, cotangent], vectors, kinds, True, later)


def first_norm_back(terms, back_two, unit, inverse, vectors, later=()):
    def body(both, tiled, v):
        grads = tiled[0] + both
        back = norm_back(grads, tiled[1], tiled[2], v[1:2, :])
        return [back, back], [back, grads * tiled[1], grads]

    n, width = unit.shape
    kinds = [(width, f32), (width, bf16)]
    return norm_tiles(body, n, width, *terms, [back_two, unit, inverse], vectors, kinds, True, later)


def input_grad(terms, back, later=()):
    def body(both, tiled, v):
        return [tiled[0] + both], []

    n, width = back.shape
    return norm_tiles(body, n, width, *terms, [back], None, [(width, bf16)], False, later)[0]


class TensorAxis:
    def __init__(self):
        self.size = lax.axis_size("tensor")
        self.me = lax.axis_index("tensor")
        self.square = self.size == 4
        if self.square:
            self.origins = self.me ^ jnp.array([0, 1, 3, 2], jnp.int32)
        else:
            self.origins = jnp.arange(self.size, dtype=jnp.int32)

    def swap(self, array, bit):
        return lax.ppermute(array, "tensor", [(i, i ^ bit) for i in range(self.size)])

    def gather(self, block, earlier=()):
        if not self.square:
            return [lax.all_gather(block, "tensor", axis=0, tiled=True)]
        half = block.shape[0] // 2
        along_x, along_y = self.swap(block, 1), self.swap(block, 2)
        onward_x, onward_y = along_y[:half], along_x[half:]
        if earlier:
            zero = nothing(*earlier).astype(block.dtype)
            onward_x, onward_y = onward_x + zero, onward_y + zero
        far_top, far_bottom = self.swap(onward_x, 1), self.swap(onward_y, 2)
        return [block, along_x, far_top, far_bottom, along_y]

    def spans(self, rows):
        if not self.square:
            return [(0, rows)], [(0, rows)]
        r = rows // 4
        return [(r, 3 * r), (3 * r, 4 * r), (0, r)], [(2 * r, 4 * r), (r, 2 * r), (0, r)]

    def line_up(self, block):
        if not self.square:
            return lax.all_gather(block, "tensor", axis=1, tiled=True)
        width = block.shape[1]
        full = jnp.zeros((block.shape[0], 4 * width), block.dtype)
        for bits in range(4):
            piece = self.swap(block, bits) if bits else block
            full = lax.dynamic_update_slice(full, piece, (0, (self.me ^ bits) * width))
        return full

    def scatter(self, terms):
        left, right = terms
        if not self.square:
            full = jnp.concatenate([left[0], right[0]], axis=1)
            mine = lax.psum_scatter(full, "tensor", scatter_dimension=0, tiled=True)
            half = mine.shape[1] // 2
            return ([(mine[:, :half], 0)], [(mine[:, half:], 0)]), (), ()
        rows = left[1].shape[0]
        from_x, from_y = self.swap(left[0], 1), self.swap(right[0], 2)
        left_far = self.swap((left[1].astype(f32) + from_x[rows:].astype(f32)).astype(bf16), 2)
        right_far = self.swap((right[1].astype(f32) + from_y[:rows].astype(f32)).astype(bf16), 1)
        left = [(left[2], 0), (from_x, 0), (left_far, 0)]
        right = [(right[2], 0), (from_y, rows), (right_far, 0)]
        return (left, right), (from_x, from_y), (left_far, right_far)


class GroupAxis:
    def __init__(self):
        self.size = lax.axis_size("dp")
        self.me = lax.axis_index("dp")
        self.line = self.size == 8
        self.z = self.me // 2
        n = self.size
        self.next = [(i, (i + 2) % n) for i in range(n)]
        self.last = [(i, (i - 2) % n) for i in range(n)]

    def send(self, array, pairs):
        return lax.ppermute(array, "dp", pairs)

    def gather(self, shard):
        return lax.all_gather(shard, "dp", axis=0, tiled=True)

    def scatter(self, terms):
        return lax.psum_scatter(terms, "dp", scatter_dimension=0, tiled=True).astype(f32)

    def weight_scatter(self, lefts, rights, row, later):
        if not self.line:
            terms = weight_grad(lefts, rights, later)
            return self.scatter(terms), lax.psum(row, "dp")[0], terms, (), (), ()
        block = lefts[0][0].shape[1] // self.size
        mine, theirs = weight_grad(lefts, rights, later, self.me % 2, block, row)
        got = self.send(theirs, [(i, i ^ 1) for i in range(self.size)])
        rows = mine.shape[0] // 4

        def toward(step):
            first = ((self.z + step) % 4) * rows
            parts = [lax.dynamic_slice_in_dim(a, first, rows).astype(f32) for a in (mine, got)]
            return parts[0] + parts[1]

        far = toward(2).astype(bf16)
        up = self.send(far, [(0, 2), (1, 3), (2, 4), (3, 5)])
        down = self.send(far, [(6, 4), (7, 5), (4, 2), (5, 3)])
        ahead = (toward(1) + up.astype(f32)).astype(bf16)
        behind = (toward(3) + down.astype(f32)).astype(bf16)
        ahead, behind = self.send(ahead, self.next), self.send(behind, self.last)
        total = toward(0) + ahead.astype(f32) + behind.astype(f32)
        return total[:block], total[block], mine, (got,), (up, down), (ahead, behind)


def nothing(*arrays):
    return sum(a[(0,) * a.ndim].astype(f32) * 0.0 for a in arrays)


def touched(array, *arrays):
    if not arrays:
        return array
    corner = array[:16, :128]
    return lax.dynamic_update_slice(array, corner + nothing(*arrays).astype(array.dtype), (0, 0))


def add_up(array, axis, earlier=()):
    size = lax.axis_size(axis)
    bit, stages = 1, []
    while bit < size:
        if len(stages) < len(earlier) and earlier[len(stages)] is not None:
            array = array + nothing(earlier[len(stages)])
        stages.append(lax.ppermute(array, axis, [(i, i ^ bit) for i in range(size)]))
        array = array + stages[-1]
        bit *= 2
    return array, stages


def gelu(hidden):
    return 0.5 * hidden * (1.0 + jnp.tanh(gelu_root * (hidden + 0.044715 * hidden * hidden * hidden)))


def gelu_slope(hidden):
    square = hidden * hidden
    bend = jnp.tanh(gelu_root * (hidden + 0.044715 * hidden * square))
    return 0.5 * (1.0 + bend) + 0.5 * hidden * (1.0 - bend * bend) * gelu_root * (
        1.0 + 3 * 0.044715 * square
    )


def local(
    tokens,
    cotangent,
    lengths,
    dealing,
    query_weight,
    key_weight,
    value_weight,
    output_weight,
    up_weight,
    down_weight,
    query_bias,
    value_bias,
    output_bias,
    attention_gain,
    attention_shift,
    up_bias,
    down_bias,
    feedforward_gain,
    feedforward_shift,
):
    tensor, group = TensorAxis(), GroupAxis()
    groups, splits = group.size, tensor.size
    slots, own_rows, model_width = cotangent.shape
    over = range(slots)
    slot_rows = own_rows * splits
    arrival_rows = tokens.shape[1]
    head_width = query_weight.shape[1]
    half = head_width // 2
    piece = query_bias.shape[0]
    hidden_width = up_weight.shape[1]
    spans = tensor.spans(slot_rows)

    slot_dealing = dealing.reshape(groups, slots)
    sent = jnp.take(tokens, dealing, axis=0, mode="clip").reshape(groups, slots, arrival_rows, model_width)
    came = lax.all_to_all(sent, "dp", split_axis=0, concat_axis=0, tiled=True)
    zero = came[0, 0, 0, 0] * 0.0
    token_pieces, arrived = [], []
    for s in over:
        rows = came[:, s].reshape(own_rows, model_width)
        if s > 0 and tensor.square:
            rows = rows + token_pieces[0][1][0, 0] * 0.0
        arrived.append(rows)
        token_pieces.append(tensor.gather(rows))

    head_piece = jnp.concatenate([query_bias, value_bias, up_bias]).astype(bf16)
    row_piece = jnp.concatenate(
        [output_bias, attention_gain, attention_shift, down_bias, feedforward_gain, feedforward_shift]
    ).astype(bf16)
    vector = jnp.concatenate([head_piece, row_piece])
    shard_rows, spare = query_weight.shape[0], 128
    padded = jnp.zeros((shard_rows * spare,), bf16).at[: vector.shape[0]].set(vector) + zero
    three = [w.astype(bf16) for w in (query_weight, key_weight, value_weight)]
    qkv_weight = group.gather(
        jnp.concatenate(
            [w[:, :half] for w in three] + [w[:, half:] for w in three] + [padded.reshape(shard_rows, spare)],
            axis=1,
        )
    )
    mid_weight = group.gather(touched(output_weight.astype(bf16).T, came))
    up_full = group.gather(touched(up_weight.astype(bf16), came))
    down_full = group.gather(touched(down_weight.astype(bf16).T, came))
    used = -(-vector.shape[0] // spare)
    table = qkv_weight[:, 3 * head_width :].reshape(groups, shard_rows, spare)[:, :used]
    table = table.reshape(groups, -1)[:, : vector.shape[0]]
    head_vectors = table.astype(f32)
    row_table = table[:, head_piece.shape[0] :].reshape(groups, 6, piece)
    row_table = jnp.moveaxis(row_table, 1, 0).reshape(6, groups * piece)
    row_vectors = tensor.line_up(row_table).astype(f32)
    query_bias_here = head_vectors[:, :piece].reshape(-1)
    value_bias_here = head_vectors[:, piece : 2 * piece].reshape(-1)
    hidden_bias = head_vectors[:, 2 * piece : head_piece.shape[0]].reshape(1, -1)
    row_vectors = jnp.concatenate([row_vectors, jnp.zeros((2, model_width), f32)], axis=0)
    blank = jnp.zeros((half,), f32)
    qkv_bias = jnp.concatenate(
        [query_bias_here[:half], blank, value_bias_here[:half]]
        + [query_bias_here[half:], blank, value_bias_here[half:]]
    )[None]

    positions = (tensor.origins[:, None] * own_rows + jnp.arange(own_rows)[None, :]).reshape(-1)
    slot_lengths = lax.dynamic_slice_in_dim(jnp.take(lengths, dealing, axis=0), group.me * slots, slots)
    biases = [
        jnp.where(positions < slot_lengths[s], 0.0, masked_score).astype(f32)[:, None] for s in over
    ]

    def near(pieces):
        return tuple(pieces[1:2] + pieces[4:])

    rows_bf16 = [(slot_rows, bf16)]
    qkv, mixed, logs, terms, sums = [], [], [], [], []
    before = near(token_pieces[1])
    for s in over:
        qkv += rows_matmul(
            token_pieces[s],
            qkv_weight,
            3 * head_width,
            lambda product, bias: ((product + bias).astype(bf16),),
            [qkv_bias],
            rows_bf16,
            before,
            most=256,
        )
        mix, log = attend(qkv[s], biases[s], 2)
        mixed.append(mix)
        logs.append(log)
        terms.append(terms_matmul(mix, mid_weight, spans, sums[-1][2] if sums else (row_vectors,)))
        sums.append(tensor.scatter(terms[s]))
        before = (terms[s][0][0],)
    first = [first_norm(sums[0][0], arrived[0], row_vectors, before)]
    first_pieces = [tensor.gather(first[0][0])]
    first.append(first_norm(sums[1][0], arrived[1], row_vectors, tuple(first_pieces[0][1:])))
    hidden, active, terms, sums = [], [], [], []

    def to_hidden(s, later):
        wide, narrow = rows_matmul(
            first_pieces[s],
            up_full,
            hidden_width,
            lambda product, bias: (product + bias, gelu(product + bias).astype(bf16)),
            [hidden_bias],
            [(slot_rows, f32), (slot_rows, bf16)],
            later,
        )
        hidden.append(wide)
        active.append(narrow)

    def from_hidden(s, later):
        terms.append(terms_matmul(active[s], down_full, spans, later))
        sums.append(tensor.scatter(terms[s]))

    to_hidden(0, (first[1][0],))
    first_pieces.append(tensor.gather(first[1][0], (active[0],)))
    from_hidden(0, tuple(first_pieces[1][1:]))
    to_hidden(1, (terms[0][0][0],))
    second, down_pieces = [], []

    def to_second(s, later):
        second.append(second_norm(sums[s][0], first[s][1], cotangent[s], row_vectors, later))
        down_pieces.append(tensor.gather(second[s][2]))

    from_hidden(1, sums[0][1])
    to_second(0, (terms[1][0][0],))
    to_second(1, near(down_pieces[0]))

    def give_back(rows):
        return lax.all_to_all(
            rows.reshape(groups, arrival_rows, model_width), "dp", split_axis=0, concat_axis=0, tiled=True
        )

    returned_rows = [give_back(s[0]) for s in second]

    hidden_grad, up_sums, terms, first_sums = [], [], [], []
    before = ()

    def through_gelu(product, wide):
        grad = (product * gelu_slope(wide)).astype(bf16)
        return grad, jnp.sum(grad.astype(f32), axis=0, keepdims=True)

    for s in over:
        grad, total = rows_matmul(
            down_pieces[s],
            down_full,
            hidden_width,
            through_gelu,
            [hidden[s]],
            [(slot_rows, bf16), (1, f32)],
            before,
        )
        hidden_grad.append(grad)
        up_sums.append(total)
        if s == 0:
            terms.append(terms_matmul(grad, up_full, spans, near(down_pieces[1])))
            first_sums.append(tensor.scatter(terms[s]))
            before = (terms[s][0][0],)
    first_back = []

    def back_to_first(s, later):
        first_back.append(
            first_norm_back(
                first_sums[s][0], second[s][1], first[s][1], first[s][2], row_vectors, later
            )
        )
        return tensor.gather(first_back[s][1])

    down_terms = weight_grad(down_pieces, active, (hidden_grad[1], *first_sums[0][1], *returned_rows))
    down_terms = touched(down_terms, *first_sums[0][2])
    down_sum = group.scatter(down_terms)
    grad_pieces = [back_to_first(0, (down_terms,))]
    terms.append(terms_matmul(hidden_grad[1], up_full, spans, (first_back[0][0],)))
    first_sums.append(tensor.scatter(terms[1]))
    up_terms = weight_grad(first_pieces, hidden_grad, (terms[1][0][0],))
    up_terms = touched(up_terms, *first_sums[1][1], *near(grad_pieces[0]))
    up_sum = group.scatter(up_terms)
    grad_pieces.append(back_to_first(1, (up_terms,)))

    def attention_in(s, later):
        return rows_matmul(
            grad_pieces[s],
            mid_weight,
            head_width,
            lambda product: (product.astype(bf16),),
            [],
            rows_bf16,
            later,
        )[0]

    def attention_back(s, mixed_grad, later):
        return attend_back(qkv[s], biases[s], mixed[s], mixed_grad, logs[s], 2, later)

    mixed_grad = [attention_in(0, (up_terms,))]
    row_grads = jnp.concatenate(
        [sum(f[2] for f in first_back)[:3], sum(s[3] for s in second)[:3]], axis=0
    ).reshape(-1, 128)
    row_grads, stages = add_up(row_grads, "tensor", (mixed_grad[0],))
    stages = [(stage,) for stage in stages] + [(), ()]
    backs = [attention_back(0, mixed_grad[0], ())]
    terms = [terms_matmul(backs[0][0], qkv_weight, spans, (*stages[0], *near(grad_pieces[1])))]
    sums = [tensor.scatter(terms[0])]
    mixed_grad.append(attention_in(1, (terms[0][0][0], *stages[1])))
    mid_terms = weight_grad(grad_pieces, mixed, (mixed_grad[1],))
    small = jnp.concatenate([row_grads, sum(up_sums).reshape(-1, 128)], axis=0)
    small, stages = add_up(small, "dp", (mixed_grad[1], mid_terms, None))
    mid_sum = group.scatter(touched(mid_terms, *sums[0][1]))
    backs.append(attention_back(1, mixed_grad[1], (mid_terms, *sums[0][1], stages[0])))
    token_grad = [input_grad(sums[0][0], first_back[0][0], (backs[1][0],))]
    returned_grads = [give_back(token_grad[0])]
    qkv_grad = [b[0] for b in backs]
    bias_terms = sum(b[1] for b in backs).reshape(1, -1)
    qkv_sum, bias_sum, qkv_terms, *qkv_stage = group.weight_scatter(
        token_pieces, qkv_grad, bias_terms, (token_grad[0], down_sum, stages[1])
    )
    terms.append(terms_matmul(qkv_grad[-1], qkv_weight, spans, (qkv_terms, *returned_grads)))
    last_grad = input_grad(
        tensor.scatter(terms[-1])[0], first_back[-1][0], (*qkv_stage[1], up_sum, stages[2])
    )
    returned_grads.append(give_back(last_grad))

    places = slot_dealing.T.reshape(-1)
    inverse = jnp.zeros(places.shape, jnp.int32).at[places].set(
        jnp.arange(places.shape[0], dtype=jnp.int32)
    )
    result = jnp.take(jnp.concatenate(returned_rows, axis=0), inverse, axis=0, mode="clip")
    inverse = inverse + nothing(mid_sum).astype(jnp.int32)
    token_gradient = jnp.take(jnp.concatenate(returned_grads, axis=0), inverse, axis=0, mode="clip")

    row_shares = lax.dynamic_slice_in_dim(
        small.reshape(-1)[: 6 * model_width].reshape(6, splits * groups, piece),
        tensor.me * groups + group.me,
        1,
        axis=1,
    )[:, 0]

    def share(values):
        return lax.dynamic_index_in_dim(values.reshape(groups, -1), group.me, 0, False)

    bias_sum = bias_sum.reshape(2, 3, half)
    query_share = share(bias_sum[:, 0])
    value_share = share(bias_sum[:, 2])
    up_share = share(small.reshape(-1)[6 * model_width :])

    qkv_sum = qkv_sum.reshape(-1, 2, 3, half)
    return (
        result,
        token_gradient,
        qkv_sum[:, :, 0].reshape(-1, head_width),
        qkv_sum[:, :, 1].reshape(-1, head_width),
        qkv_sum[:, :, 2].reshape(-1, head_width),
        mid_sum.T,
        up_sum,
        down_sum.T,
        query_share,
        value_share,
        row_shares[0],
        row_shares[1],
        row_shares[2],
        up_share,
        row_shares[3],
        row_shares[4],
        row_shares[5],
    )


def solution(mesh):
    matrix = P("dp", "tensor")
    flipped = P("tensor", "dp")
    vector = P(("tensor", "dp"))
    arrival = P(None, ("tensor", "dp"), None)
    return jax.shard_map(
        local,
        mesh=mesh,
        in_specs=(arrival, P("dp", "tensor", None), P(), P())
        + (matrix, matrix, matrix, flipped, matrix, flipped)
        + (vector,) * 9,
        out_specs=(arrival, arrival) + (matrix, matrix, matrix, flipped, matrix, flipped) + (vector,) * 9,
        check_vma=False,
    )
```
